128 devices in a mesh: expert: 16 (over x, z), context: 4 (over y), dp: 2 (over core).
Axes of the slice: x: 4, y: 4, z: 4, core: 2. Of those that a mesh axis runs over, the one named last changes fastest.
Arguments:
- layer_input: bfloat16 [2, 4, 2048, 1024], P('dp', 'context', 'expert'), may hold values from -6 to 6
- grad_output: bfloat16 [2, 4, 2048, 1024], P('dp', 'context', 'expert'), may hold values from -6 to 6
- norm1_gain: float32 [1024], replicated, may hold values from 0.5 to 1.5
- norm2_gain: float32 [1024], replicated, may hold values from 0.5 to 1.5
- w_query: bfloat16 [1024, 1024], replicated, may hold values from -0.75 to 0.75
- w_key: bfloat16 [1024, 512], replicated, may hold values from -0.75 to 0.75
- w_value: bfloat16 [1024, 512], replicated, may hold values from -0.75 to 0.75
- w_out: bfloat16 [1024, 1024], replicated, may hold values from -1.5 to 1.5
- w_router: bfloat16 [1024, 32], replicated, may hold values from -0.09375 to 0.09375
- w_gate_up: bfloat16 [32, 1024, 1024], P('expert', ('context', 'dp')), may hold values from -0.375 to 0.375
- w_down: bfloat16 [32, 512, 1024], P('expert', ('context', 'dp')), may hold values from -4 to 4
- routes: int32 [2, 4, 2048, 8], P('dp', 'context', 'expert'), may hold values from 0 to 31, all different within a row; in each aligned block of 128 rows (0 to 127, 128 to 255, ..., all dimensions but the last counted through in order) at most 48 rows name the same one
Outputs:
- block_out: float32 [2, 4, 2048, 1024], P('dp', 'context', 'expert')
- grad_input: float32 [2, 4, 2048, 1024], P('dp', 'context', 'expert')
- grad_norm1: float32 [1024], replicated
- grad_norm2: float32 [1024], replicated
- grad_w_query: float32 [1024, 1024], replicated
- grad_w_key: float32 [1024, 512], replicated
- grad_w_value: float32 [1024, 512], replicated
- grad_w_out: float32 [1024, 1024], replicated
- grad_w_router: float32 [1024, 32], replicated
- grad_w_gate_up: float32 [32, 1024, 1024], P('expert', ('context', 'dp'))
- grad_w_down: float32 [32, 512, 1024], P('expert', ('context', 'dp'))
The draws below stay inside these ranges and needn't reach their ends.
Inputs may be any that keep to these rules, and one draw needn't show every extreme that they name: `routes`: each row names 8 different experts. Taken in the order (sequence, block, position), in each aligned block of 128 rows (the tokens of one device) no expert is named by more than 48 rows, a bound that some block reaches.
All inputs are finite; a program needn't handle non-finite values.
Results may differ from the reference program's by a relative error of at most 0.024.
Values may be sent and summed in bfloat16 or wider, within the bound.
No kernel may reach another device: no remote copies, remote signals or barrier semaphores. Data moves between devices by JAX's collectives and lax.ppermute only.
A program may use at most 192 MiB of HBM per device.

```python
import math
from functools import partial
import jax
import jax.numpy as jnp
import numpy as np
from jax import lax

D = 1024
HEADS = 16
KV_HEADS = 8
HEAD_DIM = 64
F = 512
EXPERTS = 32
TOPK = 8
TOK_DEV = 128
BLOCK = 2048
SEQS = 2
CAP = 48
N_CONTEXT = 4


def shard_levels(rng, shape, pieces, least, high):
    def one(axis_at, shards_of):
        draws = jax.random.uniform(jax.random.fold_in(jax.random.fold_in(rng, 6), axis_at), (shards_of,), jnp.float32, least / len(pieces), high / len(pieces))
        return jnp.repeat(jnp.exp(draws), shape[axis_at] // shards_of).reshape((-1,) + (1,) * (len(shape) - axis_at - 1))

    level = one(*pieces[0])
    for cut in pieces[1:]:
        level = level * one(*cut)
    return level


def assign_block(rng, own, number, rows, amount, top, limit, slope):
    ranking = jax.random.permutation(rng, amount)
    packed, usual = shares(amount, rows * top, limit, slope, True), shares(amount, rows * top, limit, slope, False)
    places = jnp.arange(amount)

    def named(lengths, offset_by):
        used = int((lengths > 0).sum())
        fixed = max(1, used // 4)
        shifted = fixed + (places - fixed + offset_by * (used - fixed)) % max(1, amount - fixed)
        return jnp.zeros((amount,), jnp.int32).at[ranking[jnp.where(places < fixed, places, shifted)]].set(jnp.asarray(lengths, jnp.int32))

    lengths = jnp.where(number % 4 == 0, named(packed, number // 4), named(usual, number - number // 4 - 1))
    mixed = jax.random.permutation(jax.random.fold_in(own, 3), amount)
    source_of, sink = mixed[0:amount // 2 * 2:2], mixed[1:amount // 2 * 2:2]
    margin = jnp.minimum(lengths[source_of] - 1, limit - lengths[sink]) // 2
    margin = jnp.where((source_of == ranking[0]) | (sink == ranking[0]) | (lengths[sink] == 0), 0, jnp.maximum(margin, 0))
    shifted = jax.random.randint(jax.random.fold_in(own, 4), (amount // 2,), 0, 1 << 20) % (margin + 1)
    lengths = lengths.at[source_of].add(-shifted).at[sink].add(shifted)
    labels = jnp.searchsorted(jnp.cumsum(lengths), jnp.arange(rows * top), side="right").astype(jnp.int32)
    table = labels.reshape(top, rows).T
    table = table[jax.random.permutation(jax.random.fold_in(own, 1), rows)]
    offset_by = jax.random.randint(jax.random.fold_in(own, 2), (rows, 1), 0, top)
    return jnp.take_along_axis(table, (jnp.arange(top)[None, :] + offset_by) % top, axis=1)


def shares(amount, total, bound, lean, full):
    weights = [(1 << 20) // math.isqrt(grade ** lean) + 1 for grade in range(1, amount + 1)]
    largest = bound if full else min(bound, max(-(-total // amount), total * weights[0] // sum(weights)))
    least = 1 if total - largest >= amount - 1 else 0
    counts, spare = [largest] + [least] * (amount - 1), total - largest - least * (amount - 1)
    while spare > 0:
        candidates = [i for i in range(1, amount) if counts[i] < largest] or [i for i in range(1, amount) if counts[i] < bound]
        whole, budget = sum([weights[i] for i in candidates]), spare
        for i in candidates:
            more = min(bound - counts[i], max(1, budget * weights[i] // whole), spare)
            counts[i] = counts[i] + more
            spare = spare - more
    return np.array(counts)


def scatter_about(key, extent, width, reach, cuts=(), held_as=jnp.bfloat16):
    drawn = jax.random.normal(key, extent, jnp.float32) * width
    if len(cuts) > 0:
        drawn = shard_levels(key, extent, cuts, -0.22, 0.18) * drawn
    return jnp.clip(drawn, min=-reach, max=reach).astype(held_as)


def setup_inputs(seed: int = 0) -> dict:
    keys = jax.random.split(jax.random.key(seed), 13)
    layer_input = scatter_about(keys[0], (SEQS, N_CONTEXT, BLOCK, D), 1.0, 6.0, ((0, 2), (1, 4), (2, 16)))
    grad_output = scatter_about(keys[1], (SEQS, N_CONTEXT, BLOCK, D), 1.0, 6.0, ((0, 2), (1, 4), (2, 16)))
    norm1_gain = jnp.clip(1.0 + 0.1 * jax.random.normal(keys[2], (D,), jnp.float32), 0.5, 1.5)
    norm2_gain = jnp.clip(1.0 + 0.1 * jax.random.normal(keys[3], (D,), jnp.float32), 0.5, 1.5)
    w_query = scatter_about(keys[4], (D, HEADS * HEAD_DIM), (D // 16) ** -0.5, 0.75)
    w_key = scatter_about(keys[5], (D, KV_HEADS * HEAD_DIM), (D // 16) ** -0.5, 0.75)
    w_value = scatter_about(keys[6], (D, KV_HEADS * HEAD_DIM), (D // 16) ** -0.5, 0.75)
    w_out = scatter_about(keys[7], (HEADS * HEAD_DIM, D), (D // 64) ** -0.5, 1.5)
    w_router = scatter_about(keys[8], (D, EXPERTS), (4 * D) ** -0.5, 0.09375)
    w_gate_up = scatter_about(keys[9], (EXPERTS, D, 2 * F), (D // 4) ** -0.5, 0.375, ((0, 16), (1, 8)))
    w_down = scatter_about(keys[10], (EXPERTS, F, D), (max(F // 256, 1)) ** -0.5, 4.0, ((0, 16), (1, 8)))
    routes_keys = jax.random.split(jax.random.fold_in(keys[11], 1), SEQS * N_CONTEXT * BLOCK // TOK_DEV)
    routes_turns = jax.random.permutation(jax.random.fold_in(keys[11], 3), SEQS * N_CONTEXT * BLOCK // TOK_DEV)
    routes = jax.vmap(lambda own, number: assign_block(jax.random.fold_in(keys[11], 2), own, number, TOK_DEV, EXPERTS, TOPK, CAP, 2))(routes_keys, routes_turns).reshape((SEQS, N_CONTEXT, BLOCK, TOPK))
    return dict(layer_input=layer_input, grad_output=grad_output, norm1_gain=norm1_gain, norm2_gain=norm2_gain, w_query=w_query, w_key=w_key, w_value=w_value, w_out=w_out, w_router=w_router, w_gate_up=w_gate_up, w_down=w_down, routes=routes)


norm_eps = 1e-06
score_scale = 0.015625
branch_scale = 0.22
rope_base = 10000.0
huge_negative = -1e+30
highest_precision = lax.Precision.HIGHEST

@jax.custom_vjp
def low(v):
    return lax.optimization_barrier(v.astype(jnp.bfloat16)).astype(jnp.float32)

@jax.custom_vjp
def low_back(v):
    return v

def low_keep(v):
    return (low(v), None)

def low_pass(kept, grad):
    return (grad,)

def back_keep(v):
    return (v, None)

def back_low(kept, grad):
    return (low(grad),)
low.defvjp(low_keep, low_pass)
low_back.defvjp(back_keep, back_low)

def normalize(values):
    return values * lax.rsqrt(lax.optimization_barrier(jnp.mean(values * values, axis=-1, keepdims=True)) + norm_eps)

def rope_tables(positions, head_size):
    frequency = rope_base ** (-jnp.arange(0, head_size, 2, dtype=jnp.float32) / head_size)
    angles = positions.astype(jnp.float32)[:, None] * frequency[None, :]
    angles = jnp.concatenate([angles, angles], -1)
    return (jnp.cos(angles), jnp.sin(angles))

def rope_turn(values, cosine_table, sine_table):
    half_size = values.shape[-1] // 2
    turned = jnp.concatenate([-values[..., half_size:], values[..., :half_size]], -1)
    return values * cosine_table[:, None, :] + turned * sine_table[:, None, :]

def attend_block(queries, key_rows, value_rows, first_row):
    scores = jnp.einsum('qhgd,khd->hgqk', queries, key_rows, precision=highest_precision) * score_scale
    scores = low_back(scores)
    query_pos = first_row + jnp.arange(queries.shape[0], dtype=jnp.int32)
    key_pos = jnp.arange(key_rows.shape[0], dtype=jnp.int32)
    visible = key_pos[None, :] <= query_pos[:, None]
    scores = jnp.where(visible, scores, huge_negative)
    weights = low(jax.nn.softmax(scores, axis=-1))
    return jnp.einsum('hgqk,khd->qhgd', weights, value_rows, precision=highest_precision)

def sequence_forward(sequence, norm1_gain, w_query, w_key, w_value, w_out):
    length = sequence.shape[0]
    group_size = HEADS // KV_HEADS
    act1 = low(normalize(sequence) * norm1_gain)
    cosine_table, sine_table = rope_tables(jnp.arange(length, dtype=jnp.int32), HEAD_DIM)
    query_raw = jnp.dot(act1, w_query, precision=highest_precision).reshape(length, HEADS, HEAD_DIM)
    query_rot = low(rope_turn(low_back(query_raw), cosine_table, sine_table))
    query_rot = query_rot.reshape(length, KV_HEADS, group_size, HEAD_DIM)
    key_raw = jnp.dot(act1, w_key, precision=highest_precision).reshape(length, KV_HEADS, HEAD_DIM)
    key_rot = low(rope_turn(low_back(key_raw), cosine_table, sine_table))
    value_low = low(low_back(jnp.dot(act1, w_value, precision=highest_precision)))
    value_low = value_low.reshape(length, KV_HEADS, HEAD_DIM)
    block_rows = max(512, length // 16)
    outputs = []
    for first_row in range(0, length, block_rows):
        last_row = first_row + block_rows
        step_fn = jax.checkpoint(partial(attend_block, first_row=first_row))
        outputs.append(step_fn(query_rot[first_row:last_row], key_rot[:last_row], value_low[:last_row]))
    attended = jnp.concatenate(outputs, 0).reshape(length, HEADS * HEAD_DIM)
    attended = low(low_back(attended))
    return sequence + branch_scale * low_back(jnp.dot(attended, w_out, precision=highest_precision))

def mixture(act2, router_probs, routes, w_gate_up, w_down):
    row_count = act2.shape[0]
    groups = row_count // TOK_DEV
    token_routes = routes.reshape(groups, TOK_DEV, TOPK)
    expert_hits = lax.optimization_barrier(jnp.sum((token_routes[..., None] == jnp.arange(EXPERTS, dtype=jnp.int32)).astype(jnp.int32), 2))
    slot_rows = jnp.cumsum(expert_hits, 1) - expert_hits
    slot_of = jnp.take_along_axis(slot_rows, token_routes, 2)
    group_ids = jnp.arange(groups, dtype=jnp.int32)[:, None, None]
    slot_index = (token_routes * groups + group_ids) * CAP + slot_of
    token_ids = jnp.broadcast_to(jnp.arange(row_count, dtype=jnp.int32).reshape(groups, TOK_DEV, 1), slot_index.shape)
    slot_table = jnp.full((EXPERTS * groups * CAP,), row_count, jnp.int32)
    slot_table = slot_table.at[slot_index.reshape(-1)].set(token_ids.reshape(-1)).reshape(EXPERTS, groups * CAP)
    padded = jnp.concatenate([act2, jnp.zeros((1, act2.shape[1]), jnp.float32)], 0)

    def one_expert(inputs):
        row_index, gate_up, down_weight = inputs
        taken_rows = low_back(padded[row_index])
        gate_up_pre = low_back(jnp.dot(taken_rows, gate_up, precision=highest_precision))
        hidden = low(jax.nn.silu(gate_up_pre[:, :F]) * gate_up_pre[:, F:])
        return low(low_back(jnp.dot(hidden, down_weight, precision=highest_precision)))
    results = lax.map(jax.checkpoint(one_expert), (slot_table, w_gate_up, w_down)).reshape(-1, D)
    picked = results[slot_index.reshape(row_count, TOPK)]
    gate_values = jnp.take_along_axis(router_probs, routes.reshape(row_count, TOPK), 1)
    return lax.optimization_barrier(jnp.sum(gate_values[..., None] * picked, 1))

def layer_forward(layer_input, norm1_gain, norm2_gain, w_query, w_key, w_value, w_out, w_router, w_gate_up, w_down, routes):
    seq_count = layer_input.shape[0]
    length = layer_input.shape[1] * layer_input.shape[2]
    states = []
    for index_seq in range(seq_count):
        states.append(sequence_forward(layer_input[index_seq].reshape(length, D), norm1_gain, w_query, w_key, w_value, w_out))
    hidden = jnp.concatenate(states, 0)
    act2 = low(normalize(hidden) * norm2_gain)
    router_probs = jax.nn.softmax(jnp.dot(act2, w_router, precision=highest_precision), axis=-1)
    mixture_sum = mixture(act2, router_probs, routes, w_gate_up, w_down)
    return (hidden + branch_scale * mixture_sum).reshape(layer_input.shape)

def reference(layer_input, grad_output, norm1_gain, norm2_gain, w_query, w_key, w_value, w_out, w_router, w_gate_up, w_down, routes):
    floats = [array_value.astype(jnp.float32) for array_value in (layer_input, norm1_gain, norm2_gain, w_query, w_key, w_value, w_out, w_router, w_gate_up, w_down)]
    result, pullback = jax.vjp(partial(layer_forward, routes=routes), *floats)
    gradients = pullback(grad_output.astype(jnp.float32))
    return (result, gradients[0], gradients[1], gradients[2], gradients[3], gradients[4], gradients[5], gradients[6], gradients[7], gradients[8], gradients[9])
```

```python
import functools

import jax
import jax.numpy as jnp
import numpy as np
from jax import lax
from jax.experimental import pallas as pl
from jax.experimental.pallas import tpu as pltpu
from jax.sharding import PartitionSpec as P

D = 1024
HEAD_DIM = 64
F = 512
EXPERTS = 32
CAP = 48
TOK = 128
BLOCK = 2048
LANES = 128
SLOTS = EXPERTS * CAP
PAIRS = 8
CHUNK = 512

norm_eps = 1e-06
score_scale = 0.015625
branch_scale = 0.22
rope_base = 10000.0
huge_negative = -1e30
bf16 = jnp.bfloat16
f32 = jnp.float32
VMEM_LIMIT = 56 * 1024 * 1024


def call(kernel, out_shape, flops, moved, **kw):
    return pl.pallas_call(
        kernel,
        out_shape=out_shape,
        compiler_params=pltpu.CompilerParams(vmem_limit_bytes=VMEM_LIMIT),
        cost_estimate=pl.CostEstimate(flops=int(flops), bytes_accessed=int(moved), transcendentals=0),
        **kw,
    )


def struct(shape, dtype):
    return jax.ShapeDtypeStruct(shape, dtype)


def dot(a, b):
    return jnp.dot(a, b, preferred_element_type=f32)


def dot_rows(a, b):
    return lax.dot_general(a, b, (((1,), (1,)), ((), ())), preferred_element_type=f32)


def dot_down(a, b):
    return lax.dot_general(a, b, (((0,), (0,)), ((), ())), preferred_element_type=f32)


def split2(x):
    hi = x.astype(bf16)
    return hi, (x - hi.astype(f32)).astype(bf16)


def lane_index(shape):
    return lax.broadcasted_iota(jnp.int32, shape, len(shape) - 1)


def project_kernel(x_ref, gain_ref, wq_ref, wk_ref, wv_ref, cos_ref, sin_ref, act_ref, q_ref, kv_ref):
    x = x_ref[...].astype(f32)
    inverse = lax.rsqrt(jnp.mean(x * x, axis=-1, keepdims=True) + norm_eps)
    act = (x * inverse * gain_ref[...]).astype(bf16)
    act_ref[...] = act
    cos = cos_ref[...]
    sin = sin_ref[...]
    lane = lane_index((TOK, LANES))
    first = lane % HEAD_DIM < HEAD_DIM // 2
    left = lane < HEAD_DIM

    def turn(v):
        moved = jnp.where(first, pltpu.roll(v, LANES - 32, 1), pltpu.roll(v, 32, 1))
        return v * cos + moved * sin

    q = dot(act, wq_ref[...])
    for j in range(PAIRS):
        rows = turn(q[:, j * LANES : (j + 1) * LANES]).astype(bf16)
        q_ref[2 * j] = rows[: TOK // 2]
        q_ref[2 * j + 1] = rows[TOK // 2 :]
    k = dot(act, wk_ref[...])
    v = dot(act, wv_ref[...])
    for b in range(PAIRS // 2):
        kb = turn(k[:, b * LANES : (b + 1) * LANES])
        vb = v[:, b * LANES : (b + 1) * LANES]
        even = jnp.where(left, kb, pltpu.roll(vb, HEAD_DIM, 1)).astype(bf16)
        odd = jnp.where(left, pltpu.roll(kb, HEAD_DIM, 1), vb).astype(bf16)
        kv_ref[4 * b] = even
        kv_ref[4 * b + 1] = even
        kv_ref[4 * b + 2] = odd
        kv_ref[4 * b + 3] = odd


def project(x, gain, wq, wk, wv, cos, sin):
    return call(
        project_kernel,
        (struct((TOK, D), bf16), struct((16, TOK // 2, LANES), bf16), struct((16, TOK, LANES), bf16)),
        2 * TOK * D * 2048,
        6e6,
        name="project",
    )(x, gain.reshape(1, D), wq, wk, wv, cos, sin)


def query_of_head(q, head, left):
    q = q.astype(f32) * score_scale
    if head:
        q = pltpu.roll(q, HEAD_DIM, 1)
    return jnp.where(left, q, 0.0).astype(bf16)


def forward_kernel(place_ref, q_ref, kv_ref, o_ref, low_ref, lse_ref, qm_ref, top_ref, acc_ref):
    tile = 1024
    context = place_ref[0]
    half = place_ref[1]
    left = lane_index((CHUNK, LANES)) < HEAD_DIM
    left_keys = lane_index((tile, LANES)) < HEAD_DIM
    for chunk in range(2):
        whole = 2 * (context if chunk == 0 else 3 - context) + chunk
        for head in range(2):
            qm_ref[head] = query_of_head(q_ref[chunk], head, left)
            top_ref[head] = jnp.full((CHUNK, LANES), huge_negative, f32)
            acc_ref[head] = jnp.zeros((CHUNK, LANES), f32)

        def step(index, masked):
            keys = kv_ref[pl.ds(pl.multiple_of(index * tile, tile), tile), :]
            values = jnp.where(left_keys, jnp.ones_like(keys), keys)
            for head in range(2):
                for part in range(2):
                    rows = slice(part * 256, part * 256 + 256)
                    s = dot_rows(qm_ref[head, rows], keys)
                    if masked:
                        r = lax.broadcasted_iota(jnp.int32, s.shape, 0) + part * 256
                        place = r + (r // 64) * 64 + half * 64
                        s = jnp.where(lane_index(s.shape) <= place, s, huge_negative)
                    old = top_ref[head, rows]
                    new = jnp.maximum(old, jnp.max(s, axis=1, keepdims=True))
                    p = jnp.exp(s - new[:, :1]).astype(bf16)
                    acc_ref[head, rows] = acc_ref[head, rows] * jnp.exp(old - new) + dot(p, values)
                    top_ref[head, rows] = new

        def visit(index, carry):
            step(index, False)
            return carry

        lax.fori_loop(0, whole, visit, 0)
        step(whole, True)
        outs = []
        for head in range(2):
            acc = acc_ref[head]
            outs.append(pltpu.roll(acc, HEAD_DIM, 1) / acc)
            total = top_ref[head] + jnp.log(jnp.where(left, acc, 1.0))
            lse_ref[2 * chunk + head] = jnp.transpose(total)[0:8]
        o = jnp.where(left, outs[0], pltpu.roll(outs[1], HEAD_DIM, 1))
        o_ref[chunk] = o
        low_ref[chunk] = o.astype(bf16)


def attend_forward(place, q, kv):
    smem = pl.BlockSpec(memory_space=pltpu.SMEM)
    vmem = pl.BlockSpec(memory_space=pltpu.VMEM)
    return call(
        forward_kernel,
        (
            struct((2, CHUNK, LANES), f32),
            struct((2, CHUNK, LANES), bf16),
            struct((4, 8, CHUNK), f32),
        ),
        2e10,
        4e6,
        in_specs=[smem, vmem, vmem],
        out_specs=(vmem, vmem, vmem),
        scratch_shapes=[
            pltpu.VMEM((2, CHUNK, LANES), bf16),
            pltpu.VMEM((2, CHUNK, LANES), f32),
            pltpu.VMEM((2, CHUNK, LANES), f32),
        ],
        name="attend",
    )(place, q, kv)


def backward_kernel(
    place_ref, q_ref, do_ref, o_ref, lse_ref, kv_ref, dq_ref, dkv_ref, qm_ref, dom_ref, row_ref, dqt_ref, acc_ref
):
    tile = 512
    context = place_ref[0]
    half = place_ref[1]
    left = lane_index((CHUNK, LANES)) < HEAD_DIM
    acc_ref[...] = jnp.zeros_like(acc_ref)
    for chunk in range(2):
        whole = 2 * (2 * (context if chunk == 0 else 3 - context) + chunk)
        do = do_ref[chunk].astype(f32)
        product = jnp.transpose(do * o_ref[chunk])
        for head in range(2):
            qm_ref[head] = query_of_head(q_ref[chunk], head, left)
            moved = do if head else pltpu.roll(do, HEAD_DIM, 1)
            dom_ref[head] = jnp.where(left, 0.0, moved).astype(bf16)
            dqt_ref[head] = jnp.zeros((LANES, CHUNK), f32)
            rows = product[head * HEAD_DIM : (head + 1) * HEAD_DIM]
            row_ref[head] = jnp.broadcast_to(jnp.sum(rows, axis=0, keepdims=True), (8, CHUNK))

        def step(index, offset):
            span = pl.ds(pl.multiple_of(index * tile, tile), tile)
            keys = kv_ref[span, :]
            for head in range(2):
                qm = qm_ref[head]
                dom = dom_ref[head]
                s = dot_rows(keys, qm)
                dp = dot_rows(keys, dom)
                p = jnp.exp(s - lse_ref[2 * chunk + head, 0:1])
                if offset is not None:
                    r = lane_index(s.shape)
                    place = r + (r // 64) * 64 + half * 64
                    key = lax.broadcasted_iota(jnp.int32, s.shape, 0) + offset
                    p = jnp.where(key <= place, p, 0.0)
                ds = (p * (dp - row_ref[head, 0:1])).astype(bf16)
                acc_ref[span, :] += dot(ds, qm) + dot(p.astype(bf16), dom)
                dqt_ref[head] += dot_down(keys, ds)

        def visit(index, carry):
            step(index, None)
            return carry

        lax.fori_loop(0, whole, visit, 0)
        step(whole, 0)
        step(whole + 1, tile)
        parts = [jnp.transpose(dqt_ref[head]) * score_scale for head in range(2)]
        dq_ref[chunk] = jnp.where(left, parts[0], pltpu.roll(parts[1], HEAD_DIM, 1)).astype(bf16)
    dkv_ref[...] = acc_ref[...].astype(bf16)


def attend_backward(place, q, do, o, lse, kv):
    smem = pl.BlockSpec(memory_space=pltpu.SMEM)
    vmem = pl.BlockSpec(memory_space=pltpu.VMEM)
    rows = kv.shape[0]
    return call(
        backward_kernel,
        (struct((2, CHUNK, LANES), bf16), struct((rows, LANES), bf16)),
        5e10,
        8e6,
        in_specs=[smem] + [vmem] * 5,
        out_specs=(vmem, vmem),
        scratch_shapes=[
            pltpu.VMEM((2, CHUNK, LANES), bf16),
            pltpu.VMEM((2, CHUNK, LANES), bf16),
            pltpu.VMEM((2, 8, CHUNK), f32),
            pltpu.VMEM((2, LANES, CHUNK), f32),
            pltpu.VMEM((rows, LANES), f32),
        ],
        name="attend_back",
    )(place, q, do, o, lse, kv)


def middle_kernel(
    att_ref, x_ref, wo_ref, gain_ref, wr_ref, pick_ref, attended_ref, hidden_ref, act_ref, probs_ref, send_ref
):
    for j in range(PAIRS):
        for h in range(2):
            attended_ref[h * 64 : h * 64 + 64, j * LANES : (j + 1) * LANES] = att_ref[2 * j + h]
    hidden = x_ref[...].astype(f32) + branch_scale * dot(attended_ref[...], wo_ref[...])
    hidden_ref[...] = hidden
    inverse = lax.rsqrt(jnp.mean(hidden * hidden, axis=-1, keepdims=True) + norm_eps)
    act = (hidden * inverse * gain_ref[...]).astype(bf16)
    act_ref[...] = act
    send_ref[...] = dot(pick_ref[...], act).astype(bf16)
    logits = dot(act, wr_ref[...])
    raised = jnp.exp(logits - jnp.max(logits, axis=-1, keepdims=True))
    probs_ref[...] = raised / jnp.sum(raised, axis=-1, keepdims=True)


def middle(att, x, wo, gain, wr, pick):
    return call(
        middle_kernel,
        (
            struct((TOK, D), bf16),
            struct((TOK, D), f32),
            struct((TOK, D), bf16),
            struct((TOK, EXPERTS), f32),
            struct((SLOTS, D), bf16),
        ),
        2 * TOK * D * (D + SLOTS),
        8e6,
        name="middle",
    )(att, x, wo, gain.reshape(1, D), wr, pick)


def expert_kernel(x_ref, top_ref, gu_ref, down_ref, back_ref, hidden_ref, mixed_ref, gg_ref):
    ones = jnp.ones((8, F), bf16)
    for part in range(2):
        take = slice(8 * part, 8 * part + 8)
        rows = slice(384 * part, 384 * part + 384)
        pre = dot(x_ref[take].reshape(384, D), gu_ref[...])
        raw = branch_scale * dot_rows(top_ref[take].reshape(384, D), down_ref[...])
        gate = pre[:, :F]
        up = pre[:, F:]
        sig = 1.0 / (1.0 + jnp.exp(-gate))
        act = gate * sig
        hidden = (act * up).astype(bf16)
        hidden_ref[rows] = hidden
        hi, lo = split2(hidden.astype(f32) * raw)
        gg_ref[:, rows] = dot_rows(ones, hi) + dot_rows(ones, lo)
        mixed_gate = (raw * up * sig * (1.0 + gate * (1.0 - sig))).astype(bf16)
        mixed_up = (raw * act).astype(bf16)
        mixed_ref[rows, :F] = mixed_gate
        mixed_ref[rows, F:] = mixed_up
        back = dot_rows(mixed_gate, gu_ref[:, :F]) + dot_rows(mixed_up, gu_ref[:, F:])
        back_ref[take] = back.astype(bf16).reshape(8, CAP, D)


def experts(x, top, gate_up, down):
    per = pl.BlockSpec((16, None, CAP, D), lambda n: (0, n, 0, 0))
    return call(
        expert_kernel,
        (
            struct((16, 2, CAP, D), bf16),
            struct((2, 768, F), bf16),
            struct((2, 768, D), bf16),
            struct((2, 8, 768), f32),
        ),
        2 * SLOTS * D * 2560,
        2e7,
        grid=(2,),
        in_specs=[
            per,
            per,
            pl.BlockSpec((None, D, D), lambda n: (n, 0, 0)),
            pl.BlockSpec((None, F, D), lambda n: (n, 0, 0)),
        ],
        out_specs=(
            per,
            pl.BlockSpec((None, 768, F), lambda n: (n, 0, 0)),
            pl.BlockSpec((None, 768, D), lambda n: (n, 0, 0)),
            pl.BlockSpec((None, 8, 768), lambda n: (n, 0, 0)),
        ),
        name="experts",
    )(x, top, gate_up, down)


def expert_grads_kernel(x_ref, top_ref, gate_ref, hidden_ref, mixed_ref, down_ref, out_ref, dgu_ref, ddown_ref):
    hidden = hidden_ref[...]
    gate = gate_ref[...]
    out_ref[...] = dot(hidden, down_ref[...]).astype(bf16).reshape(16, CAP, D)
    top = (branch_scale * gate * top_ref[...].reshape(768, D).astype(f32)).astype(bf16)
    ddown_ref[...] = dot_down(hidden, top).astype(bf16)
    mixed = (gate * mixed_ref[...].astype(f32)).astype(bf16)
    dgu_ref[...] = dot_down(x_ref[...].reshape(768, D), mixed).astype(bf16)


def expert_grads(x, top, gate, hidden, mixed, down):
    per = pl.BlockSpec((16, None, CAP, D), lambda n: (0, n, 0, 0))
    return call(
        expert_grads_kernel,
        (struct((16, 2, CAP, D), bf16), struct((2, D, D), bf16), struct((2, F, D), bf16)),
        2 * SLOTS * D * 2048,
        2.4e7,
        grid=(2,),
        in_specs=[
            per,
            per,
            pl.BlockSpec((None, 768, 1), lambda n: (n, 0, 0)),
            pl.BlockSpec((None, 768, F), lambda n: (n, 0, 0)),
            pl.BlockSpec((None, 768, D), lambda n: (n, 0, 0)),
            pl.BlockSpec((None, F, D), lambda n: (n, 0, 0)),
        ],
        out_specs=(
            per,
            pl.BlockSpec((None, D, D), lambda n: (n, 0, 0)),
            pl.BlockSpec((None, F, D), lambda n: (n, 0, 0)),
        ),
        name="expert_grads",
    )(x, top, gate, hidden, mixed, down)


def turn_back_kernel(
    back_ref, mix_ref, spot_ref, gg_ref, owner_ref, probs_ref, wr_ref, act_ref, hidden_ref, gain_ref, top_ref, wo_ref,
    state_ref, attn_ref, send_ref, router_ref, norm_ref,
):
    both = dot(mix_ref[...], back_ref[...])
    grad = both[:TOK] + both[TOK:]
    hi, lo = split2(spot_ref[...].astype(f32) * gg_ref[...])
    grad_probs = dot(hi, owner_ref[...]) + dot(lo, owner_ref[...])
    probs = probs_ref[...]
    logits = probs * (grad_probs - jnp.sum(probs * grad_probs, axis=-1, keepdims=True))
    hi, lo = split2(logits)
    grad = grad + dot_rows(hi, wr_ref[...]) + dot_rows(lo, wr_ref[...])
    act = act_ref[...]
    router_ref[...] = dot_down(act, hi) + dot_down(act, lo)
    hidden = hidden_ref[...]
    inverse = lax.rsqrt(jnp.mean(hidden * hidden, axis=-1, keepdims=True) + norm_eps)
    normed = hidden * inverse
    norm_ref[...] = jnp.broadcast_to(jnp.sum(grad * normed, axis=0, keepdims=True), (8, D))
    scaled = grad * gain_ref[...]
    state = top_ref[...].astype(f32) + inverse * (scaled - normed * jnp.mean(scaled * normed, axis=-1, keepdims=True))
    state_ref[...] = state
    attn = (branch_scale * state).astype(bf16)
    attn_ref[...] = attn
    attended = dot_rows(attn, wo_ref[...]).astype(bf16)
    for j in range(PAIRS):
        for h in range(2):
            send_ref[2 * j + h] = attended[h * 64 : h * 64 + 64, j * LANES : (j + 1) * LANES]


def turn_back(back, mix, spot, gg, owner, probs, wr, act, hidden, gain, top, wo):
    return call(
        turn_back_kernel,
        (
            struct((TOK, D), f32),
            struct((TOK, D), bf16),
            struct((16, TOK // 2, LANES), bf16),
            struct((D, EXPERTS), f32),
            struct((8, D), f32),
        ),
        2 * 256 * D * (D + SLOTS),
        8e6,
        name="turn_back",
    )(back, mix, spot, gg, owner, probs, wr, act, hidden, gain.reshape(1, D), top, wo)


def finish_kernel(
    dq_ref, dkv_ref, cos_ref, sin_ref, x_ref, gain_ref, wq_ref, wk_ref, wv_ref, state_ref, act_ref,
    out_ref, norm_ref, dw_ref, flat_ref,
):
    cos = cos_ref[...]
    sin = sin_ref[...]
    lane = lane_index((TOK, LANES))
    first = lane % HEAD_DIM < HEAD_DIM // 2
    left = lane < HEAD_DIM

    def back(v):
        scaled = v * sin
        return v * cos + jnp.where(first, pltpu.roll(scaled, LANES - 32, 1), pltpu.roll(scaled, 32, 1))

    for j in range(PAIRS):
        rows = jnp.concatenate([dq_ref[2 * j], dq_ref[2 * j + 1]], axis=0).astype(f32)
        flat_ref[:, j * LANES : (j + 1) * LANES] = back(rows).astype(bf16)
    for b in range(PAIRS // 2):
        even = dkv_ref[4 * b].astype(f32) + dkv_ref[4 * b + 1].astype(f32)
        odd = dkv_ref[4 * b + 2].astype(f32) + dkv_ref[4 * b + 3].astype(f32)
        k = jnp.where(left, even, pltpu.roll(odd, HEAD_DIM, 1))
        v = jnp.where(left, pltpu.roll(even, HEAD_DIM, 1), odd)
        flat_ref[:, D + b * LANES : D + (b + 1) * LANES] = back(k).astype(bf16)
        flat_ref[:, D + 512 + b * LANES : D + 512 + (b + 1) * LANES] = v.astype(bf16)
    dw_ref[...] = dot_down(act_ref[...], flat_ref[...]).astype(bf16)
    grad = dot_rows(flat_ref[:, :D], wq_ref[...])
    grad = grad + dot_rows(flat_ref[:, D : D + 512], wk_ref[...])
    grad = grad + dot_rows(flat_ref[:, D + 512 :], wv_ref[...])
    x = x_ref[...].astype(f32)
    inverse = lax.rsqrt(jnp.mean(x * x, axis=-1, keepdims=True) + norm_eps)
    normed = x * inverse
    norm_ref[...] = jnp.broadcast_to(jnp.sum(grad * normed, axis=0, keepdims=True), (8, D))
    scaled = grad * gain_ref[...]
    out_ref[...] = state_ref[...] + inverse * (scaled - normed * jnp.mean(scaled * normed, axis=-1, keepdims=True))


def finish(dq, dkv, cos, sin, x, gain, wq, wk, wv, state, act):
    return call(
        finish_kernel,
        (struct((TOK, D), f32), struct((8, D), f32), struct((D, 2048), bf16)),
        2 * 2 * 256 * D * 2048,
        1.2e7,
        scratch_shapes=[pltpu.VMEM((TOK, 2048), bf16)],
        name="finish",
    )(dq, dkv, cos, sin, x, gain.reshape(1, D), wq, wk, wv, state, act)


def to_owners(x):
    return lax.all_to_all(x, "expert", split_axis=0, concat_axis=0, tiled=True)


def mirror(x):
    return lax.ppermute(x, "context", [(0, 3), (1, 2), (2, 1), (3, 0)])


def swap_cores(x):
    return lax.ppermute(x, "dp", [(0, 1), (1, 0)])


def sum_everywhere(x):
    rows, columns = x.shape
    core = lax.axis_index("dp")
    parts = x.reshape(2, rows // 2, columns)
    mine = lax.dynamic_index_in_dim(parts, core, 0, False)
    other = lax.dynamic_index_in_dim(parts, 1 - core, 0, False)
    half = (mine.astype(f32) + swap_cores(other).astype(f32)).astype(bf16)
    pieces = lax.all_to_all(
        half.reshape(64, rows // 128, columns), ("expert", "context"), split_axis=0, concat_axis=0, tiled=True
    )
    total = jnp.sum(pieces.astype(f32), 0).astype(bf16)
    half = lax.all_gather(total, ("expert", "context"), axis=0, tiled=True)
    other = swap_cores(half)
    low = jnp.where(core == 0, half, other)
    high = jnp.where(core == 0, other, half)
    return jnp.concatenate([low, high], 0)


def local(
    layer_input, grad_output, norm1_gain, norm2_gain, w_query, w_key, w_value, w_out, w_router, w_gate_up, w_down, routes
):
    context = lax.axis_index("context")
    expert = lax.axis_index("expert")
    x = layer_input[0, 0]
    top = grad_output[0, 0]

    positions = context * BLOCK + expert * TOK + jnp.arange(TOK, dtype=jnp.int32)
    frequency = rope_base ** (-jnp.arange(0, HEAD_DIM, 2, dtype=f32) / HEAD_DIM)
    angles = positions.astype(f32)[:, None] * frequency[None, :]
    cos, sin = jnp.cos(angles), jnp.sin(angles)
    cos = jnp.concatenate([cos] * 4, -1)
    sin = jnp.concatenate([-sin, sin] * 2, -1)

    hits = jnp.sum((routes[0, 0][:, :, None] == jnp.arange(EXPERTS, dtype=jnp.int32)).astype(f32), 1)
    lower = np.tril(np.ones((TOK, TOK), np.float32), -1)
    place = dot(jnp.asarray(lower, bf16), hits.astype(bf16))
    owner = np.repeat(np.eye(EXPERTS, dtype=np.float32), CAP, 0)
    owner16 = jnp.asarray(owner, bf16)
    slot_number = jnp.arange(SLOTS, dtype=jnp.int32) % CAP
    marked = jnp.where(hits > 0.5, place, 255.0).astype(bf16)
    spot = (dot_rows(marked, owner16) == slot_number[None, :].astype(f32)).astype(bf16)
    pick = (dot_rows(owner16, marked) == slot_number[:, None].astype(f32)).astype(bf16)

    act1, q_send, kv_send = project(x, norm1_gain, w_query, w_key, w_value, cos, sin)
    kv_block = to_owners(kv_send).reshape(BLOCK, LANES)
    kv = lax.all_gather(kv_block, "context", axis=0, tiled=True)
    q_own = to_owners(q_send).reshape(2, CHUNK, LANES)
    q = jnp.stack([q_own[0], mirror(q_own[1])], 0)

    gate_up = lax.all_gather(w_gate_up, ("context", "dp"), axis=1, tiled=True)
    down = lax.all_gather(w_down, ("context", "dp"), axis=1, tiled=True)
    top_rows = to_owners(dot(pick, top).astype(bf16).reshape(16, 2, CAP, D))

    seat = jnp.stack([context, expert % 2]).astype(jnp.int32)
    o, o_low, lse = attend_forward(seat, q, kv)
    o_own = jnp.stack([o_low[0], mirror(o_low[1])], 0)
    att = to_owners(o_own.reshape(16, TOK // 2, LANES))

    attended, hidden, act2, probs, send = middle(att, x, w_out, norm2_gain, w_router, pick)
    rows = to_owners(send.reshape(16, 2, CAP, D))

    hi, lo = split2(probs)
    mix = jnp.concatenate([dot(hi, owner16.T).astype(bf16) * spot, dot(lo, owner16.T).astype(bf16) * spot], 0)
    gate_slots = jnp.sum(mix[:TOK].astype(f32) + mix[TOK:].astype(f32), 0).reshape(16, 2, CAP)
    gates = to_owners(gate_slots).transpose(1, 0, 2).reshape(2, 768, 1)

    grad_rows, expert_hidden, mixed, gg = experts(rows, top_rows, gate_up, down)
    back = to_owners(grad_rows).reshape(SLOTS, D)
    gg_back = to_owners(gg[:, 0].reshape(2, 16, CAP).transpose(1, 0, 2)).reshape(1, SLOTS)
    out_rows, dgu, ddown = expert_grads(rows, top_rows, gates, expert_hidden, mixed, down)

    state, attn, do_send, router_grad, norm2_grad = turn_back(
        back, mix, spot, gg_back, owner16, probs, w_router, act2, hidden, norm2_gain, top, w_out
    )
    do_own = to_owners(do_send).reshape(2, CHUNK, LANES)
    do = jnp.stack([do_own[0], mirror(do_own[1])], 0)

    grad_gate_up = lax.psum_scatter(dgu, ("context", "dp"), scatter_dimension=1, tiled=True).astype(f32)
    grad_down = lax.psum_scatter(ddown, ("context", "dp"), scatter_dimension=1, tiled=True).astype(f32)

    out_grad = dot_down(attended, attn).astype(bf16)
    extra = jnp.concatenate(
        [router_grad.reshape(32, D), norm2_grad[:1], jnp.zeros((95, D), f32)], 0
    ).astype(bf16)
    early = sum_everywhere(jnp.concatenate([out_grad, extra], 0))

    dq, dkv = attend_backward(seat, q, do, o, lse, kv)
    dq_own = jnp.stack([dq[0], mirror(dq[1])], 0).reshape(16, TOK // 2, LANES)
    dq_back = to_owners(dq_own)
    dkv_own = lax.psum_scatter(dkv, "context", scatter_dimension=0, tiled=True)
    dkv_back = to_owners(dkv_own.reshape(16, TOK, LANES))

    grad_input, norm1_grad, dw = finish(
        dq_back, dkv_back, cos, sin, x, norm1_gain, w_query, w_key, w_value, state, act1
    )

    returned = to_owners(out_rows).reshape(SLOTS, D)
    mixture = dot(mix, returned)
    block_out = hidden + branch_scale * (mixture[:TOK] + mixture[TOK:])

    last = jnp.concatenate([norm1_grad[:1], jnp.zeros((127, D), f32)], 0).astype(bf16)
    last = jnp.concatenate([last, jnp.zeros((128, D), bf16)], 1)
    late = sum_everywhere(jnp.concatenate([dw, last], 0))
    dw_sum = late[:D].astype(f32)
    return (
        block_out.reshape(1, 1, TOK, D),
        grad_input.reshape(1, 1, TOK, D),
        late[D, :D].astype(f32),
        early[D + 32].astype(f32),
        dw_sum[:, :D],
        dw_sum[:, D : D + 512],
        dw_sum[:, D + 512 :],
        early[:D].astype(f32),
        early[D : D + 32].astype(f32).reshape(D, EXPERTS),
        grad_gate_up,
        grad_down,
    )


def solution(mesh):
    tokens = P("dp", "context", "expert", None)
    weights = P("expert", ("context", "dp"), None)
    return jax.shard_map(
        local,
        mesh=mesh,
        in_specs=(tokens, tokens, P(), P(), P(), P(), P(), P(), P(), weights, weights, tokens),
        out_specs=(tokens, tokens, P(), P(), P(), P(), P(), P(), P(), weights, weights),
        check_vma=False,
    )
```

```python
import jax
import jax.numpy as jnp
import numpy as np
from jax import lax
from jax.experimental import pallas as pl
from jax.experimental.pallas import tpu as pltpu
from jax.sharding import PartitionSpec as P

D = 1024
HEAD_DIM = 64
F = 512
EXPERTS = 32
CAP = 48
TOK = 128
BLOCK = 2048
LANES = 128
SLOTS = EXPERTS * CAP
PAIRS = 8
CHUNK = 512

norm_eps = 1e-06
score_scale = 0.015625
branch_scale = 0.22
rope_base = 10000.0
huge_negative = -1e30
bf16 = jnp.bfloat16
f32 = jnp.float32
VMEM_LIMIT = 56 * 1024 * 1024


def call(kernel, out_shape, flops, moved, **kw):
    return pl.pallas_call(
        kernel,
        out_shape=out_shape,
        compiler_params=pltpu.CompilerParams(vmem_limit_bytes=VMEM_LIMIT),
        cost_estimate=pl.CostEstimate(flops=int(flops), bytes_accessed=int(moved), transcendentals=0),
        **kw,
    )


def struct(shape, dtype):
    return jax.ShapeDtypeStruct(shape, dtype)


def dot(a, b):
    return jnp.dot(a, b, preferred_element_type=f32)


def dot_rows(a, b):
    return lax.dot_general(a, b, (((1,), (1,)), ((), ())), preferred_element_type=f32)


def dot_down(a, b):
    return lax.dot_general(a, b, (((0,), (0,)), ((), ())), preferred_element_type=f32)


def split2(x):
    hi = x.astype(bf16)
    return hi, (x - hi.astype(f32)).astype(bf16)


def lane_index(shape):
    return lax.broadcasted_iota(jnp.int32, shape, len(shape) - 1)


def project_kernel(x_ref, gain_ref, wq_ref, wk_ref, wv_ref, cos_ref, sin_ref, act_ref, q_ref, kv_ref):
    x = x_ref[...].astype(f32)
    inverse = lax.rsqrt(jnp.mean(x * x, axis=-1, keepdims=True) + norm_eps)
    act = (x * inverse * gain_ref[...]).astype(bf16)
    act_ref[...] = act
    cos = cos_ref[...]
    sin = sin_ref[...]
    lane = lane_index((TOK, LANES))
    first = lane % HEAD_DIM < HEAD_DIM // 2
    left = lane < HEAD_DIM

    def turn(v):
        moved = jnp.where(first, pltpu.roll(v, LANES - 32, 1), pltpu.roll(v, 32, 1))
        return v * cos + moved * sin

    q = dot(act, wq_ref[...])
    for j in range(PAIRS):
        rows = turn(q[:, j * LANES : (j + 1) * LANES]).astype(bf16)
        q_ref[2 * j] = rows[: TOK // 2]
        q_ref[2 * j + 1] = rows[TOK // 2 :]
    k = dot(act, wk_ref[...])
    v = dot(act, wv_ref[...])
    for b in range(PAIRS // 2):
        kb = turn(k[:, b * LANES : (b + 1) * LANES])
        vb = v[:, b * LANES : (b + 1) * LANES]
        even = jnp.where(left, kb, pltpu.roll(vb, HEAD_DIM, 1)).astype(bf16)
        odd = jnp.where(left, pltpu.roll(kb, HEAD_DIM, 1), vb).astype(bf16)
        kv_ref[4 * b] = even
        kv_ref[4 * b + 1] = even
        kv_ref[4 * b + 2] = odd
        kv_ref[4 * b + 3] = odd


def project(x, gain, wq, wk, wv, cos, sin):
    return call(
        project_kernel,
        (struct((TOK, D), bf16), struct((16, TOK // 2, LANES), bf16), struct((16, TOK, LANES), bf16)),
        2 * TOK * D * 2048,
        6e6,
        name="project",
    )(x, gain.reshape(1, D), wq, wk, wv, cos, sin)


def query_of_head(q, head, left):
    q = q.astype(f32) * score_scale
    if head:
        q = pltpu.roll(q, HEAD_DIM, 1)
    return jnp.where(left, q, 0.0).astype(bf16)


def forward_kernel(place_ref, q_ref, kv_ref, o_ref, low_ref, lse_ref, qm_ref, top_ref, acc_ref):
    tile = 1024
    context = place_ref[0]
    half = place_ref[1]
    left = lane_index((CHUNK, LANES)) < HEAD_DIM
    left_keys = lane_index((tile, LANES)) < HEAD_DIM
    for chunk in range(2):
        whole = 2 * (context if chunk == 0 else 3 - context) + chunk
        for head in range(2):
            qm_ref[head] = query_of_head(q_ref[chunk], head, left)
            top_ref[head] = jnp.full((CHUNK, LANES), huge_negative, f32)
            acc_ref[head] = jnp.zeros((CHUNK, LANES), f32)

        def step(index, masked):
            keys = kv_ref[pl.ds(pl.multiple_of(index * tile, tile), tile), :]
            values = jnp.where(left_keys, jnp.ones_like(keys), keys)
            for head in range(2):
                for part in range(2):
                    rows = slice(part * 256, part * 256 + 256)
                    s = dot_rows(qm_ref[head, rows], keys)
                    if masked:
                        r = lax.broadcasted_iota(jnp.int32, s.shape, 0) + part * 256
                        place = r + (r // 64) * 64 + half * 64
                        s = jnp.where(lane_index(s.shape) <= place, s, huge_negative)
                    old = top_ref[head, rows]
                    new = jnp.maximum(old, jnp.max(s, axis=1, keepdims=True))
                    p = jnp.exp(s - new[:, :1]).astype(bf16)
                    acc_ref[head, rows] = acc_ref[head, rows] * jnp.exp(old - new) + dot(p, values)
                    top_ref[head, rows] = new

        def visit(index, carry):
            step(index, False)
            return carry

        lax.fori_loop(0, whole, visit, 0)
        step(whole, True)
        outs = []
        for head in range(2):
            acc = acc_ref[head]
            outs.append(pltpu.roll(acc, HEAD_DIM, 1) / acc)
            total = top_ref[head] + jnp.log(jnp.where(left, acc, 1.0))
            lse_ref[2 * chunk + head] = jnp.transpose(total)[0:8]
        o = jnp.where(left, outs[0], pltpu.roll(outs[1], HEAD_DIM, 1))
        o_ref[chunk] = o
        low_ref[chunk] = o.astype(bf16)


def attend_forward(place, q, kv):
    smem = pl.BlockSpec(memory_space=pltpu.SMEM)
    vmem = pl.BlockSpec(memory_space=pltpu.VMEM)
    return call(
        forward_kernel,
        (
            struct((2, CHUNK, LANES), f32),
            struct((2, CHUNK, LANES), bf16),
            struct((4, 8, CHUNK), f32),
        ),
        2e10,
        4e6,
        in_specs=[smem, vmem, vmem],
        out_specs=(vmem, vmem, vmem),
        scratch_shapes=[
            pltpu.VMEM((2, CHUNK, LANES), bf16),
            pltpu.VMEM((2, CHUNK, LANES), f32),
            pltpu.VMEM((2, CHUNK, LANES), f32),
        ],
        name="attend",
    )(place, q, kv)


def backward_kernel(
    place_ref, q_ref, do_ref, o_ref, lse_ref, kv_ref, dq_ref, dkv_ref, qm_ref, dom_ref, row_ref, dqt_ref, acc_ref
):
    tile = 512
    context = place_ref[0]
    half = place_ref[1]
    left = lane_index((CHUNK, LANES)) < HEAD_DIM
    acc_ref[...] = jnp.zeros_like(acc_ref)
    for chunk in range(2):
        whole = 2 * (2 * (context if chunk == 0 else 3 - context) + chunk)
        do = do_ref[chunk].astype(f32)
        product = jnp.transpose(do * o_ref[chunk])
        for head in range(2):
            qm_ref[head] = query_of_head(q_ref[chunk], head, left)
            moved = do if head else pltpu.roll(do, HEAD_DIM, 1)
            dom_ref[head] = jnp.where(left, 0.0, moved).astype(bf16)
            dqt_ref[head] = jnp.zeros((LANES, CHUNK), f32)
            rows = product[head * HEAD_DIM : (head + 1) * HEAD_DIM]
            row_ref[head] = jnp.broadcast_to(jnp.sum(rows, axis=0, keepdims=True), (8, CHUNK))

        def step(index, offset):
            span = pl.ds(pl.multiple_of(index * tile, tile), tile)
            keys = kv_ref[span, :]
            for head in range(2):
                qm = qm_ref[head]
                dom = dom_ref[head]
                s = dot_rows(keys, qm)
                dp = dot_rows(keys, dom)
                p = jnp.exp(s - lse_ref[2 * chunk + head, 0:1])
                if offset is not None:
                    r = lane_index(s.shape)
                    place = r + (r // 64) * 64 + half * 64
                    key = lax.broadcasted_iota(jnp.int32, s.shape, 0) + offset
                    p = jnp.where(key <= place, p, 0.0)
                ds = (p * (dp - row_ref[head, 0:1])).astype(bf16)
                acc_ref[span, :] += dot(ds, qm) + dot(p.astype(bf16), dom)
                dqt_ref[head] += dot_down(keys, ds)

        def visit(index, carry):
            step(index, None)
            return carry

        lax.fori_loop(0, whole, visit, 0)
        step(whole, 0)
        step(whole + 1, tile)
        parts = [jnp.transpose(dqt_ref[head]) * score_scale for head in range(2)]
        dq_ref[chunk] = jnp.where(left, parts[0], pltpu.roll(parts[1], HEAD_DIM, 1)).astype(bf16)
    dkv_ref[...] = acc_ref[...].astype(bf16)


def attend_backward(place, q, do, o, lse, kv):
    smem = pl.BlockSpec(memory_space=pltpu.SMEM)
    vmem = pl.BlockSpec(memory_space=pltpu.VMEM)
    rows = kv.shape[0]
    return call(
        backward_kernel,
        (struct((2, CHUNK, LANES), bf16), struct((rows, LANES), bf16)),
        5e10,
        8e6,
        in_specs=[smem] + [vmem] * 5,
        out_specs=(vmem, vmem),
        scratch_shapes=[
            pltpu.VMEM((2, CHUNK, LANES), bf16),
            pltpu.VMEM((2, CHUNK, LANES), bf16),
            pltpu.VMEM((2, 8, CHUNK), f32),
            pltpu.VMEM((2, LANES, CHUNK), f32),
            pltpu.VMEM((rows, LANES), f32),
        ],
        name="attend_back",
    )(place, q, do, o, lse, kv)


def middle_kernel(att_ref, x_ref, wo_ref, gain_ref, pick_ref, attended_ref, hidden_ref, send_ref):
    for j in range(PAIRS):
        for h in range(2):
            attended_ref[h * 64 : h * 64 + 64, j * LANES : (j + 1) * LANES] = att_ref[2 * j + h]
    hidden = x_ref[...].astype(f32) + branch_scale * dot(attended_ref[...], wo_ref[...])
    hidden_ref[...] = hidden
    inverse = lax.rsqrt(jnp.mean(hidden * hidden, axis=-1, keepdims=True) + norm_eps)
    act = (hidden * inverse * gain_ref[...]).astype(bf16)
    send_ref[...] = dot(pick_ref[...], act).astype(bf16)


def middle(att, x, wo, gain, pick):
    return call(
        middle_kernel,
        (struct((TOK, D), bf16), struct((TOK, D), f32), struct((SLOTS, D), bf16)),
        2 * TOK * D * (D + SLOTS),
        8e6,
        name="middle",
    )(att, x, wo, gain.reshape(1, D), pick)


def expert_kernel(
    first_ref, x_ref, top_ref, gu_ref, down_ref, wr_ref, back_ref, hidden_ref, mixed_ref, gate_ref, logit_ref
):
    number = first_ref[0] + pl.program_id(0)
    wr = wr_ref[...]
    for part in range(2):
        take = slice(8 * part, 8 * part + 8)
        rows = slice(384 * part, 384 * part + 384)
        x = x_ref[take].reshape(384, D)
        logits = dot(x, wr)
        raised = jnp.exp(logits - jnp.max(logits, axis=-1, keepdims=True))
        probs = raised / jnp.sum(raised, axis=-1, keepdims=True)
        chosen = (lane_index(probs.shape) == number).astype(f32)
        gate_value = jnp.sum(probs * chosen, axis=-1, keepdims=True)
        gate_ref[rows] = gate_value
        pre = dot(x, gu_ref[...])
        raw = branch_scale * dot_rows(top_ref[take].reshape(384, D), down_ref[...])
        gate = pre[:, :F]
        up = pre[:, F:]
        sig = 1.0 / (1.0 + jnp.exp(-gate))
        act = gate * sig
        hidden = (act * up).astype(bf16)
        hidden_ref[rows] = hidden
        grad_gate = jnp.sum(hidden.astype(f32) * raw, axis=-1, keepdims=True)
        grad_logits = (gate_value * grad_gate) * (chosen - probs)
        logit_ref[rows] = grad_logits
        raw = raw * gate_value
        mixed_gate = (raw * up * sig * (1.0 + gate * (1.0 - sig))).astype(bf16)
        mixed_up = (raw * act).astype(bf16)
        mixed_ref[rows, :F] = mixed_gate
        mixed_ref[rows, F:] = mixed_up
        hi, lo = split2(grad_logits)
        back = dot_rows(mixed_gate, gu_ref[:, :F]) + dot_rows(mixed_up, gu_ref[:, F:])
        back = back + dot_rows(hi, wr) + dot_rows(lo, wr)
        back_ref[take] = back.astype(bf16).reshape(8, CAP, D)


def owned(*shape):
    return pl.BlockSpec((None, *shape), lambda n: (n, *([0] * len(shape))))


def experts(first, x, top, gate_up, down, wr):
    per = pl.BlockSpec((16, None, CAP, D), lambda n: (0, n, 0, 0))
    return call(
        expert_kernel,
        (
            struct((16, 2, CAP, D), bf16),
            struct((2, 768, F), bf16),
            struct((2, 768, D), bf16),
            struct((2, 768, 1), f32),
            struct((2, 768, EXPERTS), f32),
        ),
        2 * SLOTS * D * 2560,
        2e7,
        grid=(2,),
        in_specs=[
            pl.BlockSpec(memory_space=pltpu.SMEM),
            per,
            per,
            owned(D, D),
            owned(F, D),
            pl.BlockSpec((D, EXPERTS), lambda n: (0, 0)),
        ],
        out_specs=(per, owned(768, F), owned(768, D), owned(768, 1), owned(768, EXPERTS)),
        name="experts",
    )(first, x, top, gate_up, down, wr)


def expert_grads_kernel(
    x_ref, top_ref, gate_ref, logit_ref, hidden_ref, mixed_ref, down_ref, out_ref, dgu_ref, ddown_ref, router_ref
):
    hidden = hidden_ref[...]
    gate = gate_ref[...]
    x = x_ref[...].reshape(768, D)
    out_ref[...] = (gate * dot(hidden, down_ref[...])).astype(bf16).reshape(16, CAP, D)
    top = (branch_scale * gate * top_ref[...].reshape(768, D).astype(f32)).astype(bf16)
    ddown_ref[...] = dot_down(hidden, top).astype(bf16)
    dgu_ref[...] = dot_down(x, mixed_ref[...]).astype(bf16)
    hi, lo = split2(logit_ref[...])
    router_ref[...] = dot_down(x, hi) + dot_down(x, lo)


def expert_grads(x, top, gate, logits, hidden, mixed, down):
    per = pl.BlockSpec((16, None, CAP, D), lambda n: (0, n, 0, 0))
    return call(
        expert_grads_kernel,
        (
            struct((16, 2, CAP, D), bf16),
            struct((2, D, D), bf16),
            struct((2, F, D), bf16),
            struct((2, D, EXPERTS), f32),
        ),
        2 * SLOTS * D * 2048,
        2.4e7,
        grid=(2,),
        in_specs=[per, per, owned(768, 1), owned(768, EXPERTS), owned(768, F), owned(768, D), owned(F, D)],
        out_specs=(per, owned(D, D), owned(F, D), owned(D, EXPERTS)),
        name="expert_grads",
    )(x, top, gate, logits, hidden, mixed, down)


def as_column(rows):
    hi, lo = split2(rows)
    ones = jnp.ones((TOK, LANES), bf16)
    return dot_down(hi, ones) + dot_down(lo, ones)


def turn_back_kernel(
    back_ref, spot_ref, hidden_ref, gain_ref, top_ref, wo_ref, state_ref, attn_ref, send_ref, norm_ref
):
    grad = dot(spot_ref[...], back_ref[...])
    hidden = hidden_ref[...]
    inverse = lax.rsqrt(jnp.mean(hidden * hidden, axis=-1, keepdims=True) + norm_eps)
    normed = hidden * inverse
    scaled = grad * gain_ref[...]
    state = top_ref[...].astype(f32) + inverse * (scaled - normed * jnp.mean(scaled * normed, axis=-1, keepdims=True))
    state_ref[...] = state
    attn = (branch_scale * state).astype(bf16)
    attn_ref[...] = attn
    attended = dot_rows(attn, wo_ref[...]).astype(bf16)
    for j in range(PAIRS):
        for h in range(2):
            send_ref[2 * j + h] = attended[h * 64 : h * 64 + 64, j * LANES : (j + 1) * LANES]
    norm_ref[...] = as_column(grad * normed)


def turn_back(back, spot, hidden, gain, top, wo):
    return call(
        turn_back_kernel,
        (
            struct((TOK, D), f32),
            struct((TOK, D), bf16),
            struct((16, TOK // 2, LANES), bf16),
            struct((D, LANES), f32),
        ),
        2 * 256 * D * (D + SLOTS),
        8e6,
        name="turn_back",
    )(back, spot, hidden, gain.reshape(1, D), top, wo)


def core_half(core):
    return pl.ds(pl.multiple_of(core * 512, 512), 512)


def early_kernel(core_ref, attended_ref, attn_ref, extra_ref, mine_ref, other_ref):
    core = core_ref[0]
    for which, out in ((core, mine_ref), (1 - core, other_ref)):
        half = core_half(which)
        out[:, :D] = dot_down(attended_ref[:, half], attn_ref[...]).astype(bf16)
        out[:, D:] = extra_ref[half, :]


def early_terms(core, attended, attn, extra):
    smem = pl.BlockSpec(memory_space=pltpu.SMEM)
    vmem = pl.BlockSpec(memory_space=pltpu.VMEM)
    half = struct((512, D + LANES), bf16)
    return call(
        early_kernel, (half, half), 2 * TOK * D * D, 3e6, in_specs=[smem] + [vmem] * 3, out_specs=(vmem, vmem),
        name="early",
    )(core, attended, attn, extra)


def finish_kernel(
    core_ref, dq_ref, dkv_ref, cos_ref, sin_ref, x_ref, gain_ref, wq_ref, wk_ref, wv_ref, state_ref, act_ref,
    out_ref, mine_ref, other_ref, flat_ref, product_ref,
):
    cos = cos_ref[...]
    sin = sin_ref[...]
    lane = lane_index((TOK, LANES))
    first = lane % HEAD_DIM < HEAD_DIM // 2
    left = lane < HEAD_DIM

    def back(v):
        scaled = v * sin
        return v * cos + jnp.where(first, pltpu.roll(scaled, LANES - 32, 1), pltpu.roll(scaled, 32, 1))

    for j in range(PAIRS):
        rows = jnp.concatenate([dq_ref[2 * j], dq_ref[2 * j + 1]], axis=0).astype(f32)
        flat_ref[:, j * LANES : (j + 1) * LANES] = back(rows).astype(bf16)
    for b in range(PAIRS // 2):
        even = dkv_ref[4 * b].astype(f32) + dkv_ref[4 * b + 1].astype(f32)
        odd = dkv_ref[4 * b + 2].astype(f32) + dkv_ref[4 * b + 3].astype(f32)
        k = jnp.where(left, even, pltpu.roll(odd, HEAD_DIM, 1))
        v = jnp.where(left, pltpu.roll(even, HEAD_DIM, 1), odd)
        flat_ref[:, D + b * LANES : D + (b + 1) * LANES] = back(k).astype(bf16)
        flat_ref[:, D + 512 + b * LANES : D + 512 + (b + 1) * LANES] = v.astype(bf16)
    grad = dot_rows(flat_ref[:, :D], wq_ref[...])
    grad = grad + dot_rows(flat_ref[:, D : D + 512], wk_ref[...])
    grad = grad + dot_rows(flat_ref[:, D + 512 :], wv_ref[...])
    x = x_ref[...].astype(f32)
    inverse = lax.rsqrt(jnp.mean(x * x, axis=-1, keepdims=True) + norm_eps)
    normed = x * inverse
    product_ref[...] = grad * normed
    scaled = grad * gain_ref[...]
    out_ref[...] = state_ref[...] + inverse * (scaled - normed * jnp.mean(scaled * normed, axis=-1, keepdims=True))
    core = core_ref[0]
    for which, out in ((1 - core, other_ref), (core, mine_ref)):
        half = core_half(which)
        out[:, :2048] = dot_down(act_ref[:, half], flat_ref[...]).astype(bf16)
        out[:, 2048:] = as_column(product_ref[:, half]).astype(bf16)


def finish(core, dq, dkv, cos, sin, x, gain, wq, wk, wv, state, act):
    smem = pl.BlockSpec(memory_space=pltpu.SMEM)
    vmem = pl.BlockSpec(memory_space=pltpu.VMEM)
    half = struct((512, 2048 + LANES), bf16)
    return call(
        finish_kernel,
        (struct((TOK, D), f32), half, half),
        2 * 2 * 256 * D * 2048,
        1.2e7,
        in_specs=[smem] + [vmem] * 11,
        out_specs=(vmem, vmem, vmem),
        scratch_shapes=[pltpu.VMEM((TOK, 2048), bf16), pltpu.VMEM((TOK, D), f32)],
        name="finish",
    )(core, dq, dkv, cos, sin, x, gain.reshape(1, D), wq, wk, wv, state, act)


def assemble_kernel(
    core_ref, late_ref, late_other_ref, early_ref, early_other_ref, q_ref, k_ref, v_ref, o_ref, late_extra, early_extra
):
    core = core_ref[0]
    for which, late, early in ((core, late_ref, early_ref), (1 - core, late_other_ref, early_other_ref)):
        half = core_half(which)
        q_ref[half, :] = late[:, :D].astype(f32)
        k_ref[half, :] = late[:, D : D + 512].astype(f32)
        v_ref[half, :] = late[:, D + 512 : 2048].astype(f32)
        late_extra[half, :] = late[:, 2048:].astype(f32)
        o_ref[half, :] = early[:, :D].astype(f32)
        early_extra[half, :] = early[:, D:].astype(f32)


def assemble(core, late, late_other, early, early_other):
    smem = pl.BlockSpec(memory_space=pltpu.SMEM)
    vmem = pl.BlockSpec(memory_space=pltpu.VMEM)
    return call(
        assemble_kernel,
        (
            struct((D, D), f32),
            struct((D, 512), f32),
            struct((D, 512), f32),
            struct((D, D), f32),
            struct((D, LANES), f32),
            struct((D, LANES), f32),
        ),
        1e6,
        1.9e7,
        in_specs=[smem] + [vmem] * 4,
        out_specs=(vmem,) * 6,
        name="assemble",
    )(core, late, late_other, early, early_other)


def after(x, *earlier):
    return lax.optimization_barrier((x, *earlier))[0]


def to_owners(x):
    return lax.all_to_all(x, "expert", split_axis=0, concat_axis=0, tiled=True)


def mirror(x):
    return lax.ppermute(x, "context", [(0, 3), (1, 2), (2, 1), (3, 0)])


def swap_cores(x):
    return lax.ppermute(x, "dp", [(0, 1), (1, 0)])


def shift(x, by):
    return lax.ppermute(x, "context", [(i, (i + by) % 4) for i in range(4)])


def sum_context(x, context):
    parts = x.reshape(4, x.shape[0] // 4, x.shape[1])
    pick = lambda by: lax.dynamic_index_in_dim(parts, (context + by) % 4, 0, False)
    got = [shift(pick(by), by) for by in (1, 2, 3)]
    total = pick(0).astype(f32)
    for piece in got:
        total = total + piece.astype(f32)
    return total.astype(bf16)


def gather_context(x, context):
    got = [x] + [shift(x, by) for by in (1, 2, 3)]
    rows = x.shape[0]
    wide = jnp.concatenate([got[i] for i in (3, 2, 1, 0, 3, 2, 1)], 0)
    return lax.dynamic_slice_in_dim(wide, (3 - context) * rows, 4 * rows, 0)


def reduce_half(half, context):
    rows, columns = half.shape
    pieces = to_owners(half.reshape(16, rows // 16, columns))
    return sum_context(jnp.sum(pieces.astype(f32), 0).astype(bf16), context)


def local(
    layer_input, grad_output, norm1_gain, norm2_gain, w_query, w_key, w_value, w_out, w_router, w_gate_up, w_down, routes
):
    context = lax.axis_index("context")
    expert = lax.axis_index("expert")
    x = layer_input[0, 0]
    top = grad_output[0, 0]

    positions = context * BLOCK + expert * TOK + jnp.arange(TOK, dtype=jnp.int32)
    frequency = rope_base ** (-jnp.arange(0, HEAD_DIM, 2, dtype=f32) / HEAD_DIM)
    angles = positions.astype(f32)[:, None] * frequency[None, :]
    cos, sin = jnp.cos(angles), jnp.sin(angles)
    cos = jnp.concatenate([cos] * 4, -1)
    sin = jnp.concatenate([-sin, sin] * 2, -1)

    hits = jnp.sum((routes[0, 0][:, :, None] == jnp.arange(EXPERTS, dtype=jnp.int32)).astype(f32), 1)
    lower = np.tril(np.ones((TOK, TOK), np.float32), -1)
    place = dot(jnp.asarray(lower, bf16), hits.astype(bf16))
    owner = np.repeat(np.eye(EXPERTS, dtype=np.float32), CAP, 0)
    owner16 = jnp.asarray(owner, bf16)
    slot_number = jnp.arange(SLOTS, dtype=jnp.int32) % CAP
    marked = jnp.where(hits > 0.5, place, 255.0).astype(bf16)
    spot = (dot_rows(marked, owner16) == slot_number[None, :].astype(f32)).astype(bf16)
    pick = (dot_rows(owner16, marked) == slot_number[:, None].astype(f32)).astype(bf16)

    core = lax.axis_index("dp").astype(jnp.int32).reshape(1)
    act1, q_send, kv_send = project(x, norm1_gain, w_query, w_key, w_value, cos, sin)
    kv_block = to_owners(kv_send)
    kv = lax.all_gather(kv_block.reshape(BLOCK, LANES), "context", axis=0, tiled=True)
    q_own = to_owners(after(q_send, kv_block)).reshape(2, CHUNK, LANES)
    q = jnp.stack([q_own[0], mirror(q_own[1])], 0)

    gate_up = lax.all_gather(w_gate_up, ("context", "dp"), axis=1, tiled=True)
    down = lax.all_gather(w_down, ("context", "dp"), axis=1, tiled=True)
    top_send = dot(pick, top).astype(bf16).reshape(16, 2, CAP, D)
    top_rows = to_owners(after(top_send, q_own))

    seat = jnp.stack([context, expert % 2]).astype(jnp.int32)
    o, o_low, lse = attend_forward(seat, q, kv)
    o_low = after(o_low, top_rows)
    o_own = jnp.stack([o_low[0], mirror(o_low[1])], 0)
    att = to_owners(o_own.reshape(16, TOK // 2, LANES))

    attended, hidden, send = middle(att, x, w_out, norm2_gain, pick)
    rows = to_owners(send.reshape(16, 2, CAP, D))
    first = (2 * expert).astype(jnp.int32).reshape(1)
    grad_rows, expert_hidden, mixed, gates, logits = experts(first, rows, top_rows, gate_up, down, w_router)
    back = to_owners(grad_rows)
    out_rows, dgu, ddown, router_grad = expert_grads(rows, top_rows, gates, logits, expert_hidden, mixed, down)
    back = after(back, dgu)
    grad_gate_up = lax.psum_scatter(dgu, ("context", "dp"), scatter_dimension=1, tiled=True)
    grad_down = lax.psum_scatter(ddown, ("context", "dp"), scatter_dimension=1, tiled=True)

    state, attn, do_send, norm2_column = turn_back(
        back.reshape(SLOTS, D), spot, hidden, norm2_gain, top, w_out
    )
    do_own = to_owners(do_send).reshape(2, CHUNK, LANES)
    do = jnp.stack([do_own[0], mirror(do_own[1])], 0)

    returned = to_owners(after(out_rows, do))
    router_wide = jnp.pad(router_grad[0] + router_grad[1], ((0, 0), (0, LANES - EXPERTS)))
    extra = jnp.where(lane_index((D, LANES)) < EXPERTS, router_wide, norm2_column).astype(bf16)
    early_mine, early_other = early_terms(core, attended, attn, extra)
    early_half = (early_mine.astype(f32) + swap_cores(early_other).astype(f32)).astype(bf16)

    dq, dkv = attend_backward(seat, q, do, o, lse, kv)
    dq, dkv, returned, grad_gate_up, grad_down = lax.optimization_barrier(
        (dq, dkv, returned, grad_gate_up, grad_down)
    )
    dq_own = jnp.stack([dq[0], mirror(dq[1])], 0).reshape(16, TOK // 2, LANES)
    dq_back = to_owners(dq_own)
    dkv_own = lax.psum_scatter(dkv, "context", scatter_dimension=0, tiled=True)
    early_piece = reduce_half(after(early_half, dq_back), context)
    dkv_back = to_owners(after(dkv_own, early_piece).reshape(16, TOK, LANES))
    early_block = gather_context(early_piece, context)
    early = lax.all_gather(early_block, "expert", axis=0, tiled=True)

    grad_input, late_mine, late_other = finish(
        core, dq_back, dkv_back, cos, sin, x, norm1_gain, w_query, w_key, w_value, state, act1
    )
    late_half = (late_mine.astype(f32) + swap_cores(late_other).astype(f32)).astype(bf16)
    late_block = gather_context(reduce_half(late_half, context), context)
    late = to_owners(jnp.broadcast_to(late_block[None], (16, *late_block.shape))).reshape(512, 2048 + LANES)

    mixture = dot(spot, returned.reshape(SLOTS, D))
    block_out = hidden + branch_scale * mixture
    dwq, dwk, dwv, dwo, late_extra, early_extra = assemble(core, late, swap_cores(late), early, swap_cores(early))
    return (
        block_out.reshape(1, 1, TOK, D),
        grad_input.reshape(1, 1, TOK, D),
        late_extra[:, 0],
        early_extra[:, EXPERTS],
        dwq,
        dwk,
        dwv,
        dwo,
        early_extra[:, :EXPERTS],
        grad_gate_up.astype(f32),
        grad_down.astype(f32),
    )


def solution(mesh):
    tokens = P("dp", "context", "expert", None)
    weights = P("expert", ("context", "dp"), None)
    return jax.shard_map(
        local,
        mesh=mesh,
        in_specs=(tokens, tokens, P(), P(), P(), P(), P(), P(), P(), weights, weights, tokens),
        out_specs=(tokens, tokens, P(), P(), P(), P(), P(), P(), P(), weights, weights),
        check_vma=False,
    )
```

```python
import jax
import jax.numpy as jnp
import numpy as np
from jax import lax
from jax.experimental import pallas as pl
from jax.experimental.pallas import tpu as pltpu
from jax.sharding import PartitionSpec as P

D = 1024
HEAD_DIM = 64
F = 512
EXPERTS = 32
CAP = 48
TOK = 128
BLOCK = 2048
LANES = 128
SLOTS = EXPERTS * CAP
PAIRS = 8
CHUNK = 512

norm_eps = 1e-06
score_scale = 0.015625
branch_scale = 0.22
rope_base = 10000.0
huge_negative = -1e30
bf16 = jnp.bfloat16
f32 = jnp.float32
VMEM_LIMIT = 56 * 1024 * 1024


def call(kernel, out_shape, flops, moved, **kw):
    return pl.pallas_call(
        kernel,
        out_shape=out_shape,
        compiler_params=pltpu.CompilerParams(vmem_limit_bytes=VMEM_LIMIT),
        cost_estimate=pl.CostEstimate(flops=int(flops), bytes_accessed=int(moved), transcendentals=0),
        **kw,
    )


def struct(shape, dtype):
    return jax.ShapeDtypeStruct(shape, dtype)


def dot(a, b):
    return jnp.dot(a, b, preferred_element_type=f32)


def dot_rows(a, b):
    return lax.dot_general(a, b, (((1,), (1,)), ((), ())), preferred_element_type=f32)


def dot_down(a, b):
    return lax.dot_general(a, b, (((0,), (0,)), ((), ())), preferred_element_type=f32)


def split2(x):
    hi = x.astype(bf16)
    return hi, (x - hi.astype(f32)).astype(bf16)


def lane_index(shape):
    return lax.broadcasted_iota(jnp.int32, shape, len(shape) - 1)


def project_kernel(x_ref, gain_ref, wq_ref, wk_ref, wv_ref, cos_ref, sin_ref, act_ref, q_ref, kv_ref):
    x = x_ref[...].astype(f32)
    inverse = lax.rsqrt(jnp.mean(x * x, axis=-1, keepdims=True) + norm_eps)
    act = (x * inverse * gain_ref[...]).astype(bf16)
    act_ref[...] = act
    cos = cos_ref[...]
    sin = sin_ref[...]
    lane = lane_index((TOK, LANES))
    first = lane % HEAD_DIM < HEAD_DIM // 2
    left = lane < HEAD_DIM

    def turn(v):
        moved = jnp.where(first, pltpu.roll(v, LANES - 32, 1), pltpu.roll(v, 32, 1))
        return v * cos + moved * sin

    q = dot(act, wq_ref[...])
    for j in range(PAIRS):
        rows = turn(q[:, j * LANES : (j + 1) * LANES]).astype(bf16)
        q_ref[2 * j] = rows[: TOK // 2]
        q_ref[2 * j + 1] = rows[TOK // 2 :]
    k = dot(act, wk_ref[...])
    v = dot(act, wv_ref[...])
    for b in range(PAIRS // 2):
        kb = turn(k[:, b * LANES : (b + 1) * LANES])
        vb = v[:, b * LANES : (b + 1) * LANES]
        even = jnp.where(left, kb, pltpu.roll(vb, HEAD_DIM, 1)).astype(bf16)
        odd = jnp.where(left, pltpu.roll(kb, HEAD_DIM, 1), vb).astype(bf16)
        kv_ref[4 * b] = even
        kv_ref[4 * b + 1] = even
        kv_ref[4 * b + 2] = odd
        kv_ref[4 * b + 3] = odd


def project(x, gain, wq, wk, wv, cos, sin):
    return call(
        project_kernel,
        (struct((TOK, D), bf16), struct((16, TOK // 2, LANES), bf16), struct((16, TOK, LANES), bf16)),
        2 * TOK * D * 2048,
        6e6,
        name="project",
    )(x, gain.reshape(1, D), wq, wk, wv, cos, sin)


def query_of_head(q, head, left):
    q = q.astype(f32) * score_scale
    if head:
        q = pltpu.roll(q, HEAD_DIM, 1)
    return jnp.where(left, q, 0.0).astype(bf16)


def forward_kernel(
    place_ref, q_ref, own_ref, left_ref, far_a_ref, far_b_ref, right_ref,
    o_ref, low_ref, lse_ref, kv_ref, qm_ref, top_ref, acc_ref,
):
    tile = 1024
    context = place_ref[0]
    half = place_ref[1]

    def block(back):
        return pl.multiple_of(lax.rem(context + 4 - back, 4) * BLOCK, BLOCK)

    kv_ref[pl.ds(block(0), BLOCK), :] = own_ref[...]
    kv_ref[pl.ds(block(1), BLOCK), :] = left_ref[...]
    kv_ref[pl.ds(block(2), BLOCK // 2), :] = far_a_ref[...]
    kv_ref[pl.ds(pl.multiple_of(block(2) + BLOCK // 2, BLOCK // 2), BLOCK // 2), :] = far_b_ref[...]
    kv_ref[pl.ds(block(3), BLOCK), :] = right_ref[...]
    left = lane_index((CHUNK, LANES)) < HEAD_DIM
    left_keys = lane_index((tile, LANES)) < HEAD_DIM
    for chunk in range(2):
        whole = 2 * (context if chunk == 0 else 3 - context) + chunk
        for head in range(2):
            qm_ref[head] = query_of_head(q_ref[chunk], head, left)
            top_ref[head] = jnp.full((CHUNK, LANES), huge_negative, f32)
            acc_ref[head] = jnp.zeros((CHUNK, LANES), f32)

        def step(index, masked):
            keys = kv_ref[pl.ds(pl.multiple_of(index * tile, tile), tile), :]
            values = jnp.where(left_keys, jnp.ones_like(keys), keys)
            for head in range(2):
                for part in range(2):
                    rows = slice(part * 256, part * 256 + 256)
                    s = dot_rows(qm_ref[head, rows], keys)
                    if masked:
                        r = lax.broadcasted_iota(jnp.int32, s.shape, 0) + part * 256
                        place = r + (r // 64) * 64 + half * 64
                        s = jnp.where(lane_index(s.shape) <= place, s, huge_negative)
                    old = top_ref[head, rows]
                    new = jnp.maximum(old, jnp.max(s, axis=1, keepdims=True))
                    p = jnp.exp(s - new[:, :1]).astype(bf16)
                    acc_ref[head, rows] = acc_ref[head, rows] * jnp.exp(old - new) + dot(p, values)
                    top_ref[head, rows] = new

        def visit(index, carry):
            step(index, False)
            return carry

        lax.fori_loop(0, whole, visit, 0)
        step(whole, True)
        outs = []
        for head in range(2):
            acc = acc_ref[head]
            outs.append(pltpu.roll(acc, HEAD_DIM, 1) / acc)
            total = top_ref[head] + jnp.log(jnp.where(left, acc, 1.0))
            lse_ref[2 * chunk + head] = jnp.transpose(total)[0:8]
        o = jnp.where(left, outs[0], pltpu.roll(outs[1], HEAD_DIM, 1))
        o_ref[chunk] = o
        low_ref[chunk] = o.astype(bf16)


def attend_forward(place, q, kv_parts):
    smem = pl.BlockSpec(memory_space=pltpu.SMEM)
    vmem = pl.BlockSpec(memory_space=pltpu.VMEM)
    return call(
        forward_kernel,
        (
            struct((2, CHUNK, LANES), f32),
            struct((2, CHUNK, LANES), bf16),
            struct((4, 8, CHUNK), f32),
            struct((4 * BLOCK, LANES), bf16),
        ),
        2e10,
        4e6,
        in_specs=[smem] + [vmem] * 6,
        out_specs=(vmem,) * 4,
        scratch_shapes=[
            pltpu.VMEM((2, CHUNK, LANES), bf16),
            pltpu.VMEM((2, CHUNK, LANES), f32),
            pltpu.VMEM((2, CHUNK, LANES), f32),
        ],
        name="attend",
    )(place, q, *kv_parts)


def backward_kernel(
    place_ref, q_ref, do_ref, o_ref, lse_ref, kv_ref,
    dq_ref, d0_ref, d1a_ref, d1b_ref, d2a_ref, d2b_ref, d3a_ref, d3b_ref,
    qm_ref, dom_ref, row_ref, dqt_ref, acc_ref,
):
    tile = 512
    context = place_ref[0]
    half = place_ref[1]
    left = lane_index((CHUNK, LANES)) < HEAD_DIM
    acc_ref[...] = jnp.zeros_like(acc_ref)
    for chunk in range(2):
        whole = 2 * (2 * (context if chunk == 0 else 3 - context) + chunk)
        do = do_ref[chunk].astype(f32)
        product = jnp.transpose(do * o_ref[chunk])
        for head in range(2):
            qm_ref[head] = query_of_head(q_ref[chunk], head, left)
            moved = do if head else pltpu.roll(do, HEAD_DIM, 1)
            dom_ref[head] = jnp.where(left, 0.0, moved).astype(bf16)
            dqt_ref[head] = jnp.zeros((LANES, CHUNK), f32)
            rows = product[head * HEAD_DIM : (head + 1) * HEAD_DIM]
            row_ref[head] = jnp.broadcast_to(jnp.sum(rows, axis=0, keepdims=True), (8, CHUNK))

        def step(index, offset):
            span = pl.ds(pl.multiple_of(index * tile, tile), tile)
            keys = kv_ref[span, :]
            for head in range(2):
                qm = qm_ref[head]
                dom = dom_ref[head]
                s = dot_rows(keys, qm)
                dp = dot_rows(keys, dom)
                p = jnp.exp(s - lse_ref[2 * chunk + head, 0:1])
                if offset is not None:
                    r = lane_index(s.shape)
                    place = r + (r // 64) * 64 + half * 64
                    key = lax.broadcasted_iota(jnp.int32, s.shape, 0) + offset
                    p = jnp.where(key <= place, p, 0.0)
                ds = (p * (dp - row_ref[head, 0:1])).astype(bf16)
                acc_ref[span, :] += dot(ds, qm) + dot(p.astype(bf16), dom)
                dqt_ref[head] += dot_down(keys, ds)

        def visit(index, carry):
            step(index, None)
            return carry

        lax.fori_loop(0, whole, visit, 0)
        step(whole, 0)
        step(whole + 1, tile)
        parts = [jnp.transpose(dqt_ref[head]) * score_scale for head in range(2)]
        dq_ref[chunk] = jnp.where(left, parts[0], pltpu.roll(parts[1], HEAD_DIM, 1)).astype(bf16)
    d0_ref[...] = acc_ref[pl.ds(pl.multiple_of(context * BLOCK, BLOCK), BLOCK), :]
    for back, first, second in ((1, d1a_ref, d1b_ref), (2, d2a_ref, d2b_ref), (3, d3a_ref, d3b_ref)):
        start = pl.multiple_of(lax.rem(context + 4 - back, 4) * BLOCK, BLOCK)
        first[...] = acc_ref[pl.ds(start, BLOCK // 2), :].astype(bf16)
        second[...] = acc_ref[pl.ds(pl.multiple_of(start + BLOCK // 2, BLOCK // 2), BLOCK // 2), :].astype(bf16)


def attend_backward(place, q, do, o, lse, kv):
    smem = pl.BlockSpec(memory_space=pltpu.SMEM)
    vmem = pl.BlockSpec(memory_space=pltpu.VMEM)
    rows = kv.shape[0]
    return call(
        backward_kernel,
        (struct((2, CHUNK, LANES), bf16), struct((BLOCK, LANES), f32))
        + (struct((BLOCK // 2, LANES), bf16),) * 6,
        5e10,
        8e6,
        in_specs=[smem] + [vmem] * 5,
        out_specs=(vmem,) * 8,
        scratch_shapes=[
            pltpu.VMEM((2, CHUNK, LANES), bf16),
            pltpu.VMEM((2, CHUNK, LANES), bf16),
            pltpu.VMEM((2, 8, CHUNK), f32),
            pltpu.VMEM((2, LANES, CHUNK), f32),
            pltpu.VMEM((rows, LANES), f32),
        ],
        name="attend_back",
    )(place, q, do, o, lse, kv)


def middle_kernel(att_ref, x_ref, wo_ref, gain_ref, pick_ref, hidden_ref, send_ref, attended_ref):
    for j in range(PAIRS):
        for h in range(2):
            attended_ref[h * 64 : h * 64 + 64, j * LANES : (j + 1) * LANES] = att_ref[2 * j + h]
    hidden = x_ref[...].astype(f32) + branch_scale * dot(attended_ref[...], wo_ref[...])
    hidden_ref[...] = hidden
    inverse = lax.rsqrt(jnp.mean(hidden * hidden, axis=-1, keepdims=True) + norm_eps)
    act = (hidden * inverse * gain_ref[...]).astype(bf16)
    send_ref[...] = dot(pick_ref[...], act).astype(bf16)


def middle(att, x, wo, gain, pick):
    return call(
        middle_kernel,
        (struct((TOK, D), f32), struct((SLOTS, D), bf16)),
        2 * TOK * D * (D + SLOTS),
        8e6,
        scratch_shapes=[pltpu.VMEM((TOK, D), bf16)],
        name="middle",
    )(att, x, wo, gain.reshape(1, D), pick)


def raw_kernel(top_ref, down_ref, raw_ref):
    raw_ref[...] = branch_scale * dot_rows(top_ref[...].reshape(768, D), down_ref[...])


def raw_grads(top, down):
    per = pl.BlockSpec((16, None, CAP, D), lambda n: (0, n, 0, 0))
    return call(
        raw_kernel, struct((2, 768, F), f32), 2 * SLOTS * D * F, 8e6, grid=(2,), in_specs=[per, owned(F, D)],
        out_specs=owned(768, F), name="raw",
    )(top, down)


def expert_kernel(
    first_ref, x_ref, raw_ref, gu_ref, wr_ref, back_ref, hidden_ref, mixed_ref, gate_ref, logit_ref
):
    number = first_ref[0] + pl.program_id(0)
    wr = wr_ref[...]
    for part in range(2):
        take = slice(8 * part, 8 * part + 8)
        rows = slice(384 * part, 384 * part + 384)
        x = x_ref[take].reshape(384, D)
        logits = dot(x, wr)
        raised = jnp.exp(logits - jnp.max(logits, axis=-1, keepdims=True))
        probs = raised / jnp.sum(raised, axis=-1, keepdims=True)
        chosen = (lane_index(probs.shape) == number).astype(f32)
        gate_value = jnp.sum(probs * chosen, axis=-1, keepdims=True)
        gate_ref[rows] = gate_value
        pre = dot(x, gu_ref[...])
        raw = raw_ref[rows]
        gate = pre[:, :F]
        up = pre[:, F:]
        sig = 1.0 / (1.0 + jnp.exp(-gate))
        act = gate * sig
        hidden = (act * up).astype(bf16)
        hidden_ref[rows] = hidden
        grad_gate = jnp.sum(hidden.astype(f32) * raw, axis=-1, keepdims=True)
        grad_logits = (gate_value * grad_gate) * (chosen - probs)
        logit_ref[rows] = grad_logits
        raw = raw * gate_value
        mixed_gate = (raw * up * sig * (1.0 + gate * (1.0 - sig))).astype(bf16)
        mixed_up = (raw * act).astype(bf16)
        mixed_ref[rows, :F] = mixed_gate
        mixed_ref[rows, F:] = mixed_up
        hi, lo = split2(grad_logits)
        back = dot_rows(mixed_gate, gu_ref[:, :F]) + dot_rows(mixed_up, gu_ref[:, F:])
        back = back + dot_rows(hi, wr) + dot_rows(lo, wr)
        back_ref[take] = back.astype(bf16).reshape(8, CAP, D)


def owned(*shape):
    return pl.BlockSpec((None, *shape), lambda n: (n, *([0] * len(shape))))


def experts(first, x, raw, gate_up, wr):
    per = pl.BlockSpec((16, None, CAP, D), lambda n: (0, n, 0, 0))
    return call(
        expert_kernel,
        (
            struct((16, 2, CAP, D), bf16),
            struct((2, 768, F), bf16),
            struct((2, 768, D), bf16),
            struct((2, 768, 1), f32),
            struct((2, 768, EXPERTS), f32),
        ),
        2 * SLOTS * D * 2560,
        2e7,
        grid=(2,),
        in_specs=[
            pl.BlockSpec(memory_space=pltpu.SMEM),
            per,
            owned(768, F),
            owned(D, D),
            pl.BlockSpec((D, EXPERTS), lambda n: (0, 0)),
        ],
        out_specs=(per, owned(768, F), owned(768, D), owned(768, 1), owned(768, EXPERTS)),
        name="experts",
    )(first, x, raw, gate_up, wr)


def expert_grads_kernel(
    x_ref, top_ref, gate_ref, logit_ref, hidden_ref, mixed_ref, down_ref, out_ref, dgu_ref, ddown_ref, router_ref
):
    hidden = hidden_ref[...]
    gate = gate_ref[...]
    x = x_ref[...].reshape(768, D)
    out_ref[...] = (gate * dot(hidden, down_ref[...])).astype(bf16).reshape(16, CAP, D)
    top = (branch_scale * gate * top_ref[...].reshape(768, D).astype(f32)).astype(bf16)
    ddown_ref[...] = dot_down(hidden, top).astype(bf16)
    dgu_ref[...] = dot_down(x, mixed_ref[...]).astype(bf16)
    hi, lo = split2(logit_ref[...])
    router_ref[...] = dot_down(hi, x) + dot_down(lo, x)


def expert_grads(x, top, gate, logits, hidden, mixed, down):
    per = pl.BlockSpec((16, None, CAP, D), lambda n: (0, n, 0, 0))
    return call(
        expert_grads_kernel,
        (
            struct((16, 2, CAP, D), bf16),
            struct((2, D, D), bf16),
            struct((2, F, D), bf16),
            struct((2, EXPERTS, D), f32),
        ),
        2 * SLOTS * D * 2048,
        2.4e7,
        grid=(2,),
        in_specs=[per, per, owned(768, 1), owned(768, EXPERTS), owned(768, F), owned(768, D), owned(F, D)],
        out_specs=(per, owned(D, D), owned(F, D), owned(EXPERTS, D)),
        name="expert_grads",
    )(x, top, gate, logits, hidden, mixed, down)


def turn_back_kernel(
    back_ref, spot_ref, hidden_ref, gain_ref, top_ref, wo_ref, state_ref, attn_ref, send_ref, norm_ref
):
    grad = dot(spot_ref[...], back_ref[...])
    hidden = hidden_ref[...]
    inverse = lax.rsqrt(jnp.mean(hidden * hidden, axis=-1, keepdims=True) + norm_eps)
    normed = hidden * inverse
    scaled = grad * gain_ref[...]
    state = top_ref[...].astype(f32) + inverse * (scaled - normed * jnp.mean(scaled * normed, axis=-1, keepdims=True))
    state_ref[...] = state
    attn = (branch_scale * state).astype(bf16)
    attn_ref[...] = attn
    attended = dot_rows(attn, wo_ref[...]).astype(bf16)
    for j in range(PAIRS):
        for h in range(2):
            send_ref[2 * j + h] = attended[h * 64 : h * 64 + 64, j * LANES : (j + 1) * LANES]
    norm_ref[...] = jnp.broadcast_to(jnp.sum(grad * normed, axis=0, keepdims=True), (8, D))


def turn_back(back, spot, hidden, gain, top, wo):
    return call(
        turn_back_kernel,
        (
            struct((TOK, D), f32),
            struct((TOK, D), bf16),
            struct((16, TOK // 2, LANES), bf16),
            struct((8, D), f32),
        ),
        2 * 256 * D * (D + SLOTS),
        8e6,
        name="turn_back",
    )(back, spot, hidden, gain.reshape(1, D), top, wo)


def unturn(v, cos, sin, first):
    scaled = v * sin
    return v * cos + jnp.where(first, pltpu.roll(scaled, LANES - 32, 1), pltpu.roll(scaled, 32, 1))


def head_kernel(
    core_ref, act_ref, attn_ref, o_ref, dq_ref, mine_in, other_in, cos_ref, sin_ref, mine_ref, other_ref, grads_ref,
    all_ref,
):
    rows = 1024
    lane = lane_index((rows, LANES))
    first = lane % HEAD_DIM < HEAD_DIM // 2
    cos = cos_ref[...]
    sin = sin_ref[...]
    grads_ref[:, :LANES] = unturn(dq_ref[...].astype(f32), cos, sin, first).astype(bf16)
    both = (mine_in[...] + other_in[...].astype(f32)).astype(bf16).astype(f32)
    grads_ref[:, LANES:] = jnp.where(lane < HEAD_DIM, unturn(both, cos, sin, first), both).astype(bf16)
    all_ref[:D] = dot_down(act_ref[...], grads_ref[...]).astype(bf16)
    out = dot_down(o_ref[...], attn_ref[...]).astype(bf16)
    for b in range(4):
        all_ref[D + LANES * b : D + LANES * (b + 1)] = out[:, 256 * b : 256 * (b + 1)]
    core = core_ref[0]
    mine_ref[...] = all_ref[pl.ds(pl.multiple_of(core * 768, 768), 768), :]
    other_ref[...] = all_ref[pl.ds(pl.multiple_of((1 - core) * 768, 768), 768), :]


def head_grads(core, act, attn, o, dq, mine, other, cos, sin):
    smem = pl.BlockSpec(memory_space=pltpu.SMEM)
    vmem = pl.BlockSpec(memory_space=pltpu.VMEM)
    half = struct((768, 256), bf16)
    return call(
        head_kernel,
        (half, half, struct((1024, 256), bf16)),
        2 * 1024 * 1024 * 512,
        8e6,
        in_specs=[smem] + [vmem] * 8,
        out_specs=(vmem,) * 3,
        scratch_shapes=[pltpu.VMEM((1536, 256), bf16)],
        name="head_grads",
    )(core, act, attn, o, dq, mine, other, cos, sin)


def finish_kernel(grads_ref, x_ref, gain_ref, wq_ref, wk_ref, wv_ref, state_ref, out_ref, flat_ref):
    left = lane_index((TOK // 2, LANES)) < HEAD_DIM
    for h in range(2):
        rows = slice(64 * h, 64 * h + 64)
        for j in range(PAIRS):
            flat_ref[rows, j * LANES : (j + 1) * LANES] = grads_ref[2 * j + h, :, :LANES]
        for b in range(PAIRS // 2):
            even = grads_ref[4 * b + h, :, LANES:].astype(f32)
            odd = grads_ref[4 * b + 2 + h, :, LANES:].astype(f32)
            k = jnp.where(left, even, pltpu.roll(odd, HEAD_DIM, 1))
            v = jnp.where(left, pltpu.roll(even, HEAD_DIM, 1), odd)
            flat_ref[rows, D + b * LANES : D + (b + 1) * LANES] = k.astype(bf16)
            flat_ref[rows, D + 512 + b * LANES : D + 512 + (b + 1) * LANES] = v.astype(bf16)
    grad = dot_rows(flat_ref[:, :D], wq_ref[...])
    grad = grad + dot_rows(flat_ref[:, D : D + 512], wk_ref[...])
    grad = grad + dot_rows(flat_ref[:, D + 512 :], wv_ref[...])
    x = x_ref[...].astype(f32)
    inverse = lax.rsqrt(jnp.mean(x * x, axis=-1, keepdims=True) + norm_eps)
    normed = x * inverse
    scaled = grad * gain_ref[...]
    out_ref[...] = state_ref[...] + inverse * (scaled - normed * jnp.mean(scaled * normed, axis=-1, keepdims=True))


def finish(grads, x, gain, wq, wk, wv, state):
    return call(
        finish_kernel,
        struct((TOK, D), f32),
        2 * 256 * D * 2048,
        8e6,
        scratch_shapes=[pltpu.VMEM((TOK, 2048), bf16)],
        name="finish",
    )(grads, x, gain.reshape(1, D), wq, wk, wv, state)


def assemble_kernel(core_ref, own_ref, other_ref, wq_ref, wk_ref, wv_ref, q_ref, k_ref, v_ref, o_ref, norm_ref):
    left = lane_index((384, LANES)) < HEAD_DIM

    def write(pieces):
        for core in range(2):
            piece = pieces[core]
            for h in range(2):
                start = 768 * core + 384 * h
                count = min(384, max(0, D - start))
                if count:
                    rows = slice(start, start + count)
                    total = jnp.zeros((count, LANES), f32)
                    for j in range(PAIRS):
                        lanes = slice(j * LANES, (j + 1) * LANES)
                        value = piece[2 * j + h, :count, :LANES].astype(f32)
                        q_ref[rows, lanes] = value
                        total = total + value * wq_ref[rows, lanes].astype(f32)
                    for b in range(PAIRS // 2):
                        lanes = slice(b * LANES, (b + 1) * LANES)
                        even = piece[4 * b + h, :count, LANES:].astype(f32)
                        odd = piece[4 * b + 2 + h, :count, LANES:].astype(f32)
                        k = jnp.where(left[:count], even, pltpu.roll(odd, HEAD_DIM, 1))
                        v = jnp.where(left[:count], pltpu.roll(even, HEAD_DIM, 1), odd)
                        k_ref[rows, lanes] = k
                        v_ref[rows, lanes] = v
                        total = total + k * wk_ref[rows, lanes].astype(f32) + v * wv_ref[rows, lanes].astype(f32)
                    norm_ref[rows] = jnp.sum(total, axis=-1, keepdims=True)
                for b in range(4):
                    at = D + LANES * b - start
                    if 0 <= at < 384:
                        for j in range(PAIRS):
                            o_ref[j * LANES : (j + 1) * LANES, 256 * b : 256 * (b + 1)] = piece[
                                2 * j + h, at : at + LANES, :
                            ].astype(f32)

    @pl.when(core_ref[0] == 0)
    def _():
        write((own_ref, other_ref))

    @pl.when(core_ref[0] == 1)
    def _():
        write((other_ref, own_ref))


def assemble(core, own, other, wq, wk, wv):
    smem = pl.BlockSpec(memory_space=pltpu.SMEM)
    vmem = pl.BlockSpec(memory_space=pltpu.VMEM)
    return call(
        assemble_kernel,
        (
            struct((D, D), f32),
            struct((D, 512), f32),
            struct((D, 512), f32),
            struct((D, D), f32),
            struct((D, 1), f32),
        ),
        1e6,
        2.2e7,
        in_specs=[smem] + [vmem] * 5,
        out_specs=(vmem,) * 5,
        name="assemble",
    )(core, own, other, wq, wk, wv)


def after(x, *earlier):
    return lax.optimization_barrier((x, *earlier))[0]


def to_owners(x):
    return lax.all_to_all(x, "expert", split_axis=0, concat_axis=0, tiled=True)


def mirror(x):
    return lax.ppermute(x, "context", [(0, 3), (1, 2), (2, 1), (3, 0)])


def swap_cores(x):
    return lax.ppermute(x, "dp", [(0, 1), (1, 0)])


def shift(x, by):
    return lax.ppermute(x, "context", [(i, (i + by) % 4) for i in range(4)])


def sum_context(x, context):
    parts = x.reshape(4, x.shape[0] // 4, x.shape[1])
    got = [shift(pick(parts, (context + by) % 4), by) for by in (1, 2, 3)]
    total = pick(parts, context).astype(f32)
    for piece in got:
        total = total + piece.astype(f32)
    return total.astype(bf16)


def gather_context(x, context):
    got = [x] + [shift(x, by) for by in (1, 2, 3)]
    rows = x.shape[0]
    wide = jnp.concatenate([got[i] for i in (3, 2, 1, 0, 3, 2, 1)], 0)
    return lax.dynamic_slice_in_dim(wide, (3 - context) * rows, 4 * rows, 0)


def swap_halves(x):
    return lax.ppermute(x, "expert", [(i, i ^ 1) for i in range(16)])


def pick(x, index, axis=0):
    return lax.dynamic_index_in_dim(x, index, axis, False)


def rope_tables(positions):
    frequency = rope_base ** (-jnp.arange(0, HEAD_DIM, 2, dtype=f32) / HEAD_DIM)
    angles = positions.astype(f32)[:, None] * frequency[None, :]
    cos, sin = jnp.cos(angles), jnp.sin(angles)
    return jnp.concatenate([cos] * 4, -1), jnp.concatenate([-sin, sin] * 2, -1)


def local(
    layer_input, grad_output, norm1_gain, norm2_gain, w_query, w_key, w_value, w_out, w_router, w_gate_up, w_down, routes
):
    context = lax.axis_index("context")
    expert = lax.axis_index("expert")
    x = layer_input[0, 0]
    top = grad_output[0, 0]

    half = expert % 2

    cos, sin = rope_tables(context * BLOCK + expert * TOK + jnp.arange(TOK, dtype=jnp.int32))
    order = jnp.arange(1024, dtype=jnp.int32)
    half_cos, half_sin = rope_tables(context * BLOCK + order + (order // 64) * 64 + half * 64)

    hits = jnp.sum((routes[0, 0][:, :, None] == jnp.arange(EXPERTS, dtype=jnp.int32)).astype(f32), 1)
    lower = np.tril(np.ones((TOK, TOK), np.float32), -1)
    place = dot(jnp.asarray(lower, bf16), hits.astype(bf16))
    owner = np.repeat(np.eye(EXPERTS, dtype=np.float32), CAP, 0)
    owner16 = jnp.asarray(owner, bf16)
    slot_number = jnp.arange(SLOTS, dtype=jnp.int32) % CAP
    marked = jnp.where(hits > 0.5, place, 255.0).astype(bf16)
    spot = (dot_rows(marked, owner16) == slot_number[None, :].astype(f32)).astype(bf16)
    selector = (dot_rows(owner16, marked) == slot_number[:, None].astype(f32)).astype(bf16)

    core_index = lax.axis_index("dp")
    core = core_index.astype(jnp.int32).reshape(1)
    act1, q_send, kv_send = project(x, norm1_gain, w_query, w_key, w_value, cos, sin)
    kv_block = to_owners(kv_send).reshape(BLOCK, LANES)
    kv_left = shift(kv_block, 1)
    kv_right = shift(kv_block, 3)
    kv_far_a = shift(kv_left[: BLOCK // 2], 1)
    kv_far_b = shift(kv_right[BLOCK // 2 :], 3)
    q_own = to_owners(after(q_send, kv_block)).reshape(2, CHUNK, LANES)
    q = jnp.stack([q_own[0], mirror(q_own[1])], 0)

    gate_up = lax.all_gather(after(w_gate_up, kv_far_a, kv_far_b), ("context", "dp"), axis=1, tiled=True)
    down = lax.all_gather(w_down, ("context", "dp"), axis=1, tiled=True)
    top_send = dot(selector, top).astype(bf16).reshape(16, 2, CAP, D)
    top_rows = to_owners(after(top_send, q_own))

    seat = jnp.stack([context, half]).astype(jnp.int32)
    o, o_low, lse, kv = attend_forward(seat, q, (kv_block, kv_left, kv_far_a, kv_far_b, kv_right))
    o_low = after(o_low, top_rows)
    o_own = jnp.stack([o_low[0], mirror(o_low[1])], 0).reshape(1024, LANES)
    att = to_owners(o_own.reshape(16, TOK // 2, LANES))

    hidden, send = middle(att, x, w_out, norm2_gain, selector)
    rows = to_owners(send.reshape(16, 2, CAP, D))
    raw = raw_grads(top_rows, down)
    first = (2 * expert).astype(jnp.int32).reshape(1)
    act_send = jnp.broadcast_to(after(act1, rows).reshape(1, 2, 64, D), (8, 2, 64, D)).reshape(16, 64, D)
    act_rows = to_owners(act_send).reshape(1024, D)
    grad_rows, expert_hidden, mixed, gates, logits = experts(first, rows, raw, gate_up, w_router)
    back = to_owners(after(grad_rows, act_rows))
    out_rows, dgu, ddown, router_grad = expert_grads(rows, top_rows, gates, logits, expert_hidden, mixed, down)

    state, attn, do_send, norm2_grad = turn_back(back.reshape(SLOTS, D), spot, hidden, norm2_gain, top, w_out)
    do_own = to_owners(do_send).reshape(2, CHUNK, LANES)
    do = jnp.stack([do_own[0], mirror(do_own[1])], 0)
    grad_gate_up = lax.psum_scatter(
        after(dgu, do_own), ("context", "dp"), scatter_dimension=1, tiled=True
    ).astype(f32)

    returned = to_owners(after(out_rows, do_own))
    small = jnp.concatenate([router_grad[0] + router_grad[1], norm2_grad, jnp.zeros((24, D), f32)], 0)
    small = small.reshape(64, 4, 256).transpose(1, 0, 2).reshape(2, 128, 256).astype(bf16)

    dq, d0, d1a, d1b, d2a, d2b, d3a, d3b = attend_backward(seat, q, do, o, lse, kv)
    dq, d0, d1a, d1b, d2a, d2b, d3a, d3b, returned = lax.optimization_barrier(
        (dq, d0, d1a, d1b, d2a, d2b, d3a, d3b, returned)
    )
    block_out = hidden + branch_scale * dot(spot, returned.reshape(SLOTS, D))
    attn_send = jnp.broadcast_to(after(attn, returned).reshape(1, 2, 64, D), (8, 2, 64, D)).reshape(16, 64, D)
    attn_rows = to_owners(attn_send).reshape(1024, D)

    far_a, far_b = shift(d2a, 1), shift(d2b, 3)
    from_left_b, from_right_a = shift(d3b, 1), shift(d1a, 3)
    dq_own = jnp.stack([dq[0], mirror(dq[1])], 0).reshape(1024, LANES)
    from_left_a = shift((d3a.astype(f32) + far_a.astype(f32)).astype(bf16), 1)
    from_right_b = shift((d1b.astype(f32) + far_b.astype(f32)).astype(bf16), 3)
    from_left = jnp.stack([from_left_a, from_left_b], 0).reshape(16, 2, 64, LANES)
    from_right = jnp.stack([from_right_a, from_right_b], 0).reshape(16, 2, 64, LANES)
    pieces = (d0.reshape(16, 2, 64, LANES), from_left, from_right)
    keep = sum(pick(piece, half, 1).astype(f32) for piece in pieces)
    give = sum(pick(piece, 1 - half, 1).astype(f32) for piece in pieces).astype(bf16)
    got = swap_halves(give)

    small_other = swap_cores(pick(small, 1 - core_index))
    small_half = (pick(small, core_index).astype(f32) + small_other.astype(f32)).astype(bf16)
    small_piece = jnp.sum(to_owners(after(small_half, attn_rows).reshape(16, 8, 256)).astype(f32), 0).astype(bf16)
    small_sum = small_piece.astype(f32)
    for by in (1, 2, 3):
        small_sum = small_sum + shift(small_piece, by).astype(f32)

    mine, other, grads = head_grads(
        core, act_rows, attn_rows, o_own, dq_own, keep.reshape(1024, LANES), got.reshape(1024, LANES), half_cos, half_sin
    )
    grads_back = to_owners(after(grads, small_piece).reshape(16, 64, 256))
    grad_input = finish(grads_back, x, norm1_gain, w_query, w_key, w_value, state)
    grad_down = lax.psum_scatter(
        after(ddown, got), ("context", "dp"), scatter_dimension=1, tiled=True
    ).astype(f32)

    total = (mine.astype(f32) + swap_cores(other).astype(f32)).astype(bf16).reshape(2, 384, 256)
    total = pick(total, half).astype(f32) + swap_halves(pick(total, 1 - half)).astype(f32)
    block = gather_context(sum_context(total.astype(bf16), context), context)
    block = jnp.concatenate([block, small_sum.astype(bf16), jnp.zeros((8, 256), bf16)], 0)
    block, grad_input, block_out, grad_gate_up = lax.optimization_barrier(
        (block, grad_input, block_out, grad_gate_up)
    )
    whole = to_owners(jnp.broadcast_to(block[None], (16, *block.shape)))
    whole_other = swap_cores(whole)
    dwq, dwk, dwv, dwo, norm1_sum = assemble(core, whole, whole_other, w_query, w_key, w_value)
    smalls = jnp.stack([whole[:, 384:392], whole_other[:, 384:392]], 0).reshape(2, 128, 256)
    smalls = jnp.concatenate([pick(smalls, core_index), pick(smalls, 1 - core_index)], 0)
    smalls = smalls.reshape(4, 64, 256).transpose(1, 0, 2).reshape(64, D).astype(f32)
    return (
        block_out.reshape(1, 1, TOK, D),
        grad_input.reshape(1, 1, TOK, D),
        norm1_sum[:, 0] / norm1_gain,
        smalls[EXPERTS],
        dwq,
        dwk,
        dwv,
        dwo,
        smalls[:EXPERTS].T,
        grad_gate_up,
        grad_down,
    )


def solution(mesh):
    tokens = P("dp", "context", "expert", None)
    weights = P("expert", ("context", "dp"), None)
    return jax.shard_map(
        local,
        mesh=mesh,
        in_specs=(tokens, tokens, P(), P(), P(), P(), P(), P(), P(), weights, weights, tokens),
        out_specs=(tokens, tokens, P(), P(), P(), P(), P(), P(), P(), weights, weights),
        check_vma=False,
    )
```

```python
import jax
import jax.numpy as jnp
import numpy as np
from jax import lax
from jax.experimental import pallas as pl
from jax.experimental.pallas import tpu as pltpu
from jax.sharding import PartitionSpec as P

D = 1024
HEAD_DIM = 64
F = 512
EXPERTS = 32
CAP = 48
TOK = 128
BLOCK = 2048
LANES = 128
SLOTS = EXPERTS * CAP
PAIRS = 8
CHUNK = 512

norm_eps = 1e-06
score_scale = 0.015625
branch_scale = 0.22
rope_base = 10000.0
huge_negative = -1e30
bf16 = jnp.bfloat16
f32 = jnp.float32
VMEM_LIMIT = 56 * 1024 * 1024


def call(kernel, out_shape, flops, moved, **kw):
    return pl.pallas_call(
        kernel,
        out_shape=out_shape,
        compiler_params=pltpu.CompilerParams(vmem_limit_bytes=VMEM_LIMIT),
        cost_estimate=pl.CostEstimate(flops=int(flops), bytes_accessed=int(moved), transcendentals=0),
        **kw,
    )


def struct(shape, dtype):
    return jax.ShapeDtypeStruct(shape, dtype)


def dot(a, b):
    return jnp.dot(a, b, preferred_element_type=f32)


def dot_rows(a, b):
    return lax.dot_general(a, b, (((1,), (1,)), ((), ())), preferred_element_type=f32)


def dot_down(a, b):
    return lax.dot_general(a, b, (((0,), (0,)), ((), ())), preferred_element_type=f32)


def split2(x):
    hi = x.astype(bf16)
    return hi, (x - hi.astype(f32)).astype(bf16)


def lane_index(shape):
    return lax.broadcasted_iota(jnp.int32, shape, len(shape) - 1)


def project_kernel(x_ref, gain_ref, wq_ref, wk_ref, wv_ref, cos_ref, sin_ref, act_ref, q_ref, kv_ref):
    x = x_ref[...].astype(f32)
    inverse = lax.rsqrt(jnp.mean(x * x, axis=-1, keepdims=True) + norm_eps)
    act = (x * inverse * gain_ref[...]).astype(bf16)
    for e in range(16):
        act_ref[e] = act[64 * (e % 2) : 64 * (e % 2) + 64]
    cos = cos_ref[...]
    sin = sin_ref[...]
    lane = lane_index((TOK, LANES))
    first = lane % HEAD_DIM < HEAD_DIM // 2
    left = lane < HEAD_DIM

    def turn(v):
        moved = jnp.where(first, pltpu.roll(v, LANES - 32, 1), pltpu.roll(v, 32, 1))
        return v * cos + moved * sin

    q = dot(act, wq_ref[...])
    for j in range(PAIRS):
        rows = turn(q[:, j * LANES : (j + 1) * LANES]).astype(bf16)
        q_ref[2 * j] = rows[: TOK // 2]
        q_ref[2 * j + 1] = rows[TOK // 2 :]
    k = dot(act, wk_ref[...])
    v = dot(act, wv_ref[...])
    for b in range(PAIRS // 2):
        kb = turn(k[:, b * LANES : (b + 1) * LANES])
        vb = v[:, b * LANES : (b + 1) * LANES]
        even = jnp.where(left, kb, pltpu.roll(vb, HEAD_DIM, 1)).astype(bf16)
        odd = jnp.where(left, pltpu.roll(kb, HEAD_DIM, 1), vb).astype(bf16)
        kv_ref[4 * b] = even
        kv_ref[4 * b + 1] = even
        kv_ref[4 * b + 2] = odd
        kv_ref[4 * b + 3] = odd


def project(x, gain, wq, wk, wv, cos, sin):
    return call(
        project_kernel,
        (struct((16, 64, D), bf16), struct((16, 64, LANES), bf16), struct((16, TOK, LANES), bf16)),
        2 * TOK * D * 2048,
        6e6,
        name="project",
    )(x, gain.reshape(1, D), wq, wk, wv, cos, sin)


def query_of_head(q, head, left):
    q = q.astype(f32) * score_scale
    if head:
        q = pltpu.roll(q, HEAD_DIM, 1)
    return jnp.where(left, q, 0.0).astype(bf16)


def forward_kernel(
    place_ref, q_ref, q_far_ref, own_ref, left_a_ref, left_b_ref, far_a_ref, far_b_ref, right_a_ref, right_b_ref,
    o_ref, low_ref, low_far_ref, lse_ref, kv_ref, qm_ref, top_ref, acc_ref,
):
    tile = 1024
    context = place_ref[0]
    half = place_ref[1]

    def put(back, part, ref):
        start = lax.rem(context + 4 - back, 4) * BLOCK + part * (BLOCK // 2)
        rows = ref.shape[0] * TOK
        kv_ref[pl.ds(pl.multiple_of(start, BLOCK // 2), rows), :] = ref[...].reshape(rows, LANES)

    put(0, 0, own_ref)
    put(1, 0, left_a_ref)
    put(1, 1, left_b_ref)
    put(2, 0, far_a_ref)
    put(2, 1, far_b_ref)
    put(3, 0, right_a_ref)
    put(3, 1, right_b_ref)
    left = lane_index((CHUNK, LANES)) < HEAD_DIM
    left_keys = lane_index((tile, LANES)) < HEAD_DIM
    for chunk in range(2):
        whole = 2 * (context if chunk == 0 else 3 - context) + chunk
        queries = (q_far_ref[...] if chunk else q_ref[:8]).reshape(CHUNK, LANES)
        for head in range(2):
            qm_ref[head] = query_of_head(queries, head, left)
            top_ref[head] = jnp.full((CHUNK, LANES), huge_negative, f32)
            acc_ref[head] = jnp.zeros((CHUNK, LANES), f32)

        def step(index, masked):
            keys = kv_ref[pl.ds(pl.multiple_of(index * tile, tile), tile), :]
            values = jnp.where(left_keys, jnp.ones_like(keys), keys)
            for head in range(2):
                for part in range(2):
                    rows = slice(part * 256, part * 256 + 256)
                    s = dot_rows(qm_ref[head, rows], keys)
                    if masked:
                        r = lax.broadcasted_iota(jnp.int32, s.shape, 0) + part * 256
                        place = r + (r // 64) * 64 + half * 64
                        s = jnp.where(lane_index(s.shape) <= place, s, huge_negative)
                    old = top_ref[head, rows]
                    new = jnp.maximum(old, jnp.max(s, axis=1, keepdims=True))
                    p = jnp.exp(s - new[:, :1]).astype(bf16)
                    acc_ref[head, rows] = acc_ref[head, rows] * jnp.exp(old - new) + dot(p, values)
                    top_ref[head, rows] = new

        def visit(index, carry):
            step(index, False)
            return carry

        lax.fori_loop(0, whole, visit, 0)
        step(whole, True)
        outs = []
        for head in range(2):
            acc = acc_ref[head]
            outs.append(pltpu.roll(acc, HEAD_DIM, 1) / acc)
            total = top_ref[head] + jnp.log(jnp.where(left, acc, 1.0))
            lse_ref[2 * chunk + head] = jnp.transpose(total)[0:8]
        o = jnp.where(left, outs[0], pltpu.roll(outs[1], HEAD_DIM, 1))
        o_ref[chunk] = o
        (low_far_ref if chunk else low_ref)[...] = o.astype(bf16).reshape(8, 64, LANES)


def attend_forward(place, q, q_far, kv_parts):
    smem = pl.BlockSpec(memory_space=pltpu.SMEM)
    vmem = pl.BlockSpec(memory_space=pltpu.VMEM)
    return call(
        forward_kernel,
        (
            struct((2, CHUNK, LANES), f32),
            struct((8, 64, LANES), bf16),
            struct((8, 64, LANES), bf16),
            struct((4, 8, CHUNK), f32),
            struct((4 * BLOCK, LANES), bf16),
        ),
        2e10,
        4e6,
        in_specs=[smem] + [vmem] * 9,
        out_specs=(vmem,) * 5,
        scratch_shapes=[
            pltpu.VMEM((2, CHUNK, LANES), bf16),
            pltpu.VMEM((2, CHUNK, LANES), f32),
            pltpu.VMEM((2, CHUNK, LANES), f32),
        ],
        name="attend",
    )(place, q, q_far, *kv_parts)


def backward_kernel(
    place_ref, q_ref, q_far_ref, do_ref, do_far_ref, o_ref, lse_ref, kv_ref,
    dq_ref, dq_far_ref, d0_ref, d1a_ref, d1b_ref, d2a_ref, d2b_ref, d3a_ref, d3b_ref,
    qm_ref, dom_ref, row_ref, dqt_ref, acc_ref,
):
    tile = 512
    context = place_ref[0]
    half = place_ref[1]
    left = lane_index((CHUNK, LANES)) < HEAD_DIM
    acc_ref[...] = jnp.zeros_like(acc_ref)
    for chunk in range(2):
        whole = 2 * (2 * (context if chunk == 0 else 3 - context) + chunk)
        queries = (q_far_ref[...] if chunk else q_ref[:8]).reshape(CHUNK, LANES)
        do = (do_far_ref[...] if chunk else do_ref[:8]).reshape(CHUNK, LANES).astype(f32)
        product = jnp.transpose(do * o_ref[chunk])
        for head in range(2):
            qm_ref[head] = query_of_head(queries, head, left)
            moved = do if head else pltpu.roll(do, HEAD_DIM, 1)
            dom_ref[head] = jnp.where(left, 0.0, moved).astype(bf16)
            dqt_ref[head] = jnp.zeros((LANES, CHUNK), f32)
            rows = product[head * HEAD_DIM : (head + 1) * HEAD_DIM]
            row_ref[head] = jnp.broadcast_to(jnp.sum(rows, axis=0, keepdims=True), (8, CHUNK))

        def step(index, offset):
            span = pl.ds(pl.multiple_of(index * tile, tile), tile)
            keys = kv_ref[span, :]
            for head in range(2):
                qm = qm_ref[head]
                dom = dom_ref[head]
                s = dot_rows(keys, qm)
                dp = dot_rows(keys, dom)
                p = jnp.exp(s - lse_ref[2 * chunk + head, 0:1])
                if offset is not None:
                    r = lane_index(s.shape)
                    place = r + (r // 64) * 64 + half * 64
                    key = lax.broadcasted_iota(jnp.int32, s.shape, 0) + offset
                    p = jnp.where(key <= place, p, 0.0)
                ds = (p * (dp - row_ref[head, 0:1])).astype(bf16)
                acc_ref[span, :] += dot(ds, qm) + dot(p.astype(bf16), dom)
                dqt_ref[head] += dot_down(keys, ds)

        def visit(index, carry):
            step(index, None)
            return carry

        lax.fori_loop(0, whole, visit, 0)
        step(whole, 0)
        step(whole + 1, tile)
        parts = [jnp.transpose(dqt_ref[head]) * score_scale for head in range(2)]
        dq = jnp.where(left, parts[0], pltpu.roll(parts[1], HEAD_DIM, 1)).astype(bf16)
        (dq_far_ref if chunk else dq_ref)[...] = dq.reshape(8, 64, LANES)
    d0_ref[...] = acc_ref[pl.ds(pl.multiple_of(context * BLOCK, BLOCK), BLOCK), :]
    for back, first, second in ((1, d1a_ref, d1b_ref), (2, d2a_ref, d2b_ref), (3, d3a_ref, d3b_ref)):
        start = pl.multiple_of(lax.rem(context + 4 - back, 4) * BLOCK, BLOCK)
        first[...] = acc_ref[pl.ds(start, BLOCK // 2), :].astype(bf16)
        second[...] = acc_ref[pl.ds(pl.multiple_of(start + BLOCK // 2, BLOCK // 2), BLOCK // 2), :].astype(bf16)


def attend_backward(place, q, q_far, do, do_far, o, lse, kv):
    smem = pl.BlockSpec(memory_space=pltpu.SMEM)
    vmem = pl.BlockSpec(memory_space=pltpu.VMEM)
    rows = kv.shape[0]
    return call(
        backward_kernel,
        (struct((8, 64, LANES), bf16), struct((8, 64, LANES), bf16), struct((BLOCK, LANES), f32))
        + (struct((BLOCK // 2, LANES), bf16),) * 6,
        5e10,
        8e6,
        in_specs=[smem] + [vmem] * 7,
        out_specs=(vmem,) * 9,
        scratch_shapes=[
            pltpu.VMEM((2, CHUNK, LANES), bf16),
            pltpu.VMEM((2, CHUNK, LANES), bf16),
            pltpu.VMEM((2, 8, CHUNK), f32),
            pltpu.VMEM((2, LANES, CHUNK), f32),
            pltpu.VMEM((rows, LANES), f32),
        ],
        name="attend_back",
    )(place, q, q_far, do, do_far, o, lse, kv)


def middle_kernel(att_ref, x_ref, wo_ref, gain_ref, pick_ref, hidden_ref, send_ref, attended_ref):
    for j in range(PAIRS):
        for h in range(2):
            attended_ref[h * 64 : h * 64 + 64, j * LANES : (j + 1) * LANES] = att_ref[2 * j + h]
    hidden = x_ref[...].astype(f32) + branch_scale * dot(attended_ref[...], wo_ref[...])
    hidden_ref[...] = hidden
    inverse = lax.rsqrt(jnp.mean(hidden * hidden, axis=-1, keepdims=True) + norm_eps)
    act = (hidden * inverse * gain_ref[...]).astype(bf16)
    send_ref[...] = dot(pick_ref[...], act).astype(bf16)


def middle(att, x, wo, gain, pick):
    return call(
        middle_kernel,
        (struct((TOK, D), f32), struct((SLOTS, D), bf16)),
        2 * TOK * D * (D + SLOTS),
        8e6,
        scratch_shapes=[pltpu.VMEM((TOK, D), bf16)],
        name="middle",
    )(att, x, wo, gain.reshape(1, D), pick)


def raw_kernel(top_ref, down_ref, raw_ref):
    raw_ref[...] = branch_scale * dot_rows(top_ref[...].reshape(768, D), down_ref[...])


def raw_grads(top, down):
    per = pl.BlockSpec((16, None, CAP, D), lambda n: (0, n, 0, 0))
    return call(
        raw_kernel, struct((2, 768, F), f32), 2 * SLOTS * D * F, 8e6, grid=(2,), in_specs=[per, owned(F, D)],
        out_specs=owned(768, F), name="raw",
    )(top, down)


def expert_kernel(
    first_ref, x_ref, raw_ref, gu_ref, wr_ref, back_ref, hidden_ref, mixed_ref, gate_ref, logit_ref
):
    number = first_ref[0] + pl.program_id(0)
    wr = wr_ref[...]
    for part in range(2):
        take = slice(8 * part, 8 * part + 8)
        rows = slice(384 * part, 384 * part + 384)
        x = x_ref[take].reshape(384, D)
        logits = dot(x, wr)
        raised = jnp.exp(logits - jnp.max(logits, axis=-1, keepdims=True))
        probs = raised / jnp.sum(raised, axis=-1, keepdims=True)
        chosen = (lane_index(probs.shape) == number).astype(f32)
        gate_value = jnp.sum(probs * chosen, axis=-1, keepdims=True)
        gate_ref[rows] = gate_value
        pre = dot(x, gu_ref[...])
        raw = raw_ref[rows]
        gate = pre[:, :F]
        up = pre[:, F:]
        sig = 1.0 / (1.0 + jnp.exp(-gate))
        act = gate * sig
        hidden = (act * up).astype(bf16)
        hidden_ref[rows] = hidden
        grad_gate = jnp.sum(hidden.astype(f32) * raw, axis=-1, keepdims=True)
        grad_logits = (gate_value * grad_gate) * (chosen - probs)
        logit_ref[rows] = grad_logits
        raw = raw * gate_value
        mixed_gate = (raw * up * sig * (1.0 + gate * (1.0 - sig))).astype(bf16)
        mixed_up = (raw * act).astype(bf16)
        mixed_ref[rows, :F] = mixed_gate
        mixed_ref[rows, F:] = mixed_up
        hi, lo = split2(grad_logits)
        back = dot_rows(mixed_gate, gu_ref[:, :F]) + dot_rows(mixed_up, gu_ref[:, F:])
        back = back + dot_rows(hi, wr) + dot_rows(lo, wr)
        back_ref[take] = back.astype(bf16).reshape(8, CAP, D)


def owned(*shape):
    return pl.BlockSpec((None, *shape), lambda n: (n, *([0] * len(shape))))


def experts(first, x, raw, gate_up, wr):
    per = pl.BlockSpec((16, None, CAP, D), lambda n: (0, n, 0, 0))
    return call(
        expert_kernel,
        (
            struct((16, 2, CAP, D), bf16),
            struct((2, 768, F), bf16),
            struct((2, 768, D), bf16),
            struct((2, 768, 1), f32),
            struct((2, 768, EXPERTS), f32),
        ),
        2 * SLOTS * D * 2560,
        2e7,
        grid=(2,),
        in_specs=[
            pl.BlockSpec(memory_space=pltpu.SMEM),
            per,
            owned(768, F),
            owned(D, D),
            pl.BlockSpec((D, EXPERTS), lambda n: (0, 0)),
        ],
        out_specs=(per, owned(768, F), owned(768, D), owned(768, 1), owned(768, EXPERTS)),
        name="experts",
    )(first, x, raw, gate_up, wr)


def expert_grads_kernel(
    x_ref, top_ref, gate_ref, logit_ref, hidden_ref, mixed_ref, down_ref, out_ref, dgu_ref, ddown_ref, router_ref
):
    hidden = hidden_ref[...]
    gate = gate_ref[...]
    x = x_ref[...].reshape(768, D)
    out_ref[...] = (gate * dot(hidden, down_ref[...])).astype(bf16).reshape(16, CAP, D)
    top = (branch_scale * gate * top_ref[...].reshape(768, D).astype(f32)).astype(bf16)
    ddown_ref[...] = dot_down(hidden, top).astype(bf16)
    dgu_ref[...] = dot_down(x, mixed_ref[...]).astype(bf16)
    hi, lo = split2(logit_ref[...])
    router_ref[...] = dot_down(hi, x) + dot_down(lo, x)


def expert_grads(x, top, gate, logits, hidden, mixed, down):
    per = pl.BlockSpec((16, None, CAP, D), lambda n: (0, n, 0, 0))
    return call(
        expert_grads_kernel,
        (
            struct((16, 2, CAP, D), bf16),
            struct((2, D, D), bf16),
            struct((2, F, D), bf16),
            struct((2, EXPERTS, D), f32),
        ),
        2 * SLOTS * D * 2048,
        2.4e7,
        grid=(2,),
        in_specs=[per, per, owned(768, 1), owned(768, EXPERTS), owned(768, F), owned(768, D), owned(F, D)],
        out_specs=(per, owned(D, D), owned(F, D), owned(EXPERTS, D)),
        name="expert_grads",
    )(x, top, gate, logits, hidden, mixed, down)


def turn_back_kernel(
    back_ref, spot_ref, hidden_ref, gain_ref, top_ref, wo_ref, state_ref, attn_ref, send_ref, norm_ref
):
    grad = dot(spot_ref[...], back_ref[...])
    hidden = hidden_ref[...]
    inverse = lax.rsqrt(jnp.mean(hidden * hidden, axis=-1, keepdims=True) + norm_eps)
    normed = hidden * inverse
    scaled = grad * gain_ref[...]
    state = top_ref[...].astype(f32) + inverse * (scaled - normed * jnp.mean(scaled * normed, axis=-1, keepdims=True))
    state_ref[...] = state
    attn = (branch_scale * state).astype(bf16)
    for e in range(16):
        attn_ref[e] = attn[64 * (e % 2) : 64 * (e % 2) + 64]
    attended = dot_rows(attn, wo_ref[...]).astype(bf16)
    for j in range(PAIRS):
        for h in range(2):
            send_ref[2 * j + h] = attended[h * 64 : h * 64 + 64, j * LANES : (j + 1) * LANES]
    norm_ref[...] = jnp.broadcast_to(jnp.sum(grad * normed, axis=0, keepdims=True), (8, D))


def turn_back(back, spot, hidden, gain, top, wo):
    return call(
        turn_back_kernel,
        (
            struct((TOK, D), f32),
            struct((16, 64, D), bf16),
            struct((16, TOK // 2, LANES), bf16),
            struct((8, D), f32),
        ),
        2 * 256 * D * (D + SLOTS),
        8e6,
        name="turn_back",
    )(back, spot, hidden, gain.reshape(1, D), top, wo)


def unturn(v, cos, sin, first):
    scaled = v * sin
    return v * cos + jnp.where(first, pltpu.roll(scaled, LANES - 32, 1), pltpu.roll(scaled, 32, 1))


def head_kernel(
    core_ref, act_ref, attn_ref, o_ref, dq_ref, mine_in, other_in, cos_ref, sin_ref, mine_ref, other_ref, grads_ref,
    all_ref,
):
    rows = 1024
    lane = lane_index((rows, LANES))
    first = lane % HEAD_DIM < HEAD_DIM // 2
    cos = cos_ref[...]
    sin = sin_ref[...]
    grads_ref[:, :LANES] = unturn(dq_ref[...].astype(f32), cos, sin, first).astype(bf16)
    both = (mine_in[...] + other_in[...].astype(f32)).astype(bf16).astype(f32)
    grads_ref[:, LANES:] = jnp.where(lane < HEAD_DIM, unturn(both, cos, sin, first), both).astype(bf16)
    all_ref[:D] = dot_down(act_ref[...], grads_ref[...]).astype(bf16)
    out = dot_down(o_ref[...], attn_ref[...]).astype(bf16)
    for b in range(4):
        all_ref[D + LANES * b : D + LANES * (b + 1)] = out[:, 256 * b : 256 * (b + 1)]
    core = core_ref[0]
    mine_ref[...] = all_ref[pl.ds(pl.multiple_of(core * 768, 768), 768), :]
    other_ref[...] = all_ref[pl.ds(pl.multiple_of((1 - core) * 768, 768), 768), :]


def head_grads(core, act, attn, o, dq, mine, other, cos, sin):
    smem = pl.BlockSpec(memory_space=pltpu.SMEM)
    vmem = pl.BlockSpec(memory_space=pltpu.VMEM)
    half = struct((768, 256), bf16)
    return call(
        head_kernel,
        (half, half, struct((1024, 256), bf16)),
        2 * 1024 * 1024 * 512,
        8e6,
        in_specs=[smem] + [vmem] * 8,
        out_specs=(vmem,) * 3,
        scratch_shapes=[pltpu.VMEM((1536, 256), bf16)],
        name="head_grads",
    )(core, act, attn, o, dq, mine, other, cos, sin)


def finish_kernel(grads_ref, x_ref, gain_ref, wq_ref, wk_ref, wv_ref, state_ref, out_ref, flat_ref):
    left = lane_index((TOK // 2, LANES)) < HEAD_DIM
    for h in range(2):
        rows = slice(64 * h, 64 * h + 64)
        for j in range(PAIRS):
            flat_ref[rows, j * LANES : (j + 1) * LANES] = grads_ref[2 * j + h, :, :LANES]
        for b in range(PAIRS // 2):
            even = grads_ref[4 * b + h, :, LANES:].astype(f32)
            odd = grads_ref[4 * b + 2 + h, :, LANES:].astype(f32)
            k = jnp.where(left, even, pltpu.roll(odd, HEAD_DIM, 1))
            v = jnp.where(left, pltpu.roll(even, HEAD_DIM, 1), odd)
            flat_ref[rows, D + b * LANES : D + (b + 1) * LANES] = k.astype(bf16)
            flat_ref[rows, D + 512 + b * LANES : D + 512 + (b + 1) * LANES] = v.astype(bf16)
    grad = dot_rows(flat_ref[:, :D], wq_ref[...])
    grad = grad + dot_rows(flat_ref[:, D : D + 512], wk_ref[...])
    grad = grad + dot_rows(flat_ref[:, D + 512 :], wv_ref[...])
    x = x_ref[...].astype(f32)
    inverse = lax.rsqrt(jnp.mean(x * x, axis=-1, keepdims=True) + norm_eps)
    normed = x * inverse
    scaled = grad * gain_ref[...]
    out_ref[...] = state_ref[...] + inverse * (scaled - normed * jnp.mean(scaled * normed, axis=-1, keepdims=True))


def finish(grads, x, gain, wq, wk, wv, state):
    return call(
        finish_kernel,
        struct((TOK, D), f32),
        2 * 256 * D * 2048,
        8e6,
        scratch_shapes=[pltpu.VMEM((TOK, 2048), bf16)],
        name="finish",
    )(grads, x, gain.reshape(1, D), wq, wk, wv, state)


def assemble_kernel(
    core_ref, own_ref, other_ref, wq_ref, wk_ref, wv_ref, gain_ref, q_ref, k_ref, v_ref, o_ref, norm_ref
):
    left = lane_index((384, LANES)) < HEAD_DIM

    def write(pieces):
        for core in range(2):
            piece = pieces[core]
            for h in range(2):
                start = 768 * core + 384 * h
                count = min(384, max(0, D - start))
                if count:
                    rows = slice(start, start + count)
                    total = jnp.zeros((count, LANES), f32)
                    for j in range(PAIRS):
                        lanes = slice(j * LANES, (j + 1) * LANES)
                        value = piece[2 * j + h, :count, :LANES].astype(f32)
                        q_ref[rows, lanes] = value
                        total = total + value * wq_ref[rows, lanes].astype(f32)
                    for b in range(PAIRS // 2):
                        lanes = slice(b * LANES, (b + 1) * LANES)
                        even = piece[4 * b + h, :count, LANES:].astype(f32)
                        odd = piece[4 * b + 2 + h, :count, LANES:].astype(f32)
                        k = jnp.where(left[:count], even, pltpu.roll(odd, HEAD_DIM, 1))
                        v = jnp.where(left[:count], pltpu.roll(even, HEAD_DIM, 1), odd)
                        k_ref[rows, lanes] = k
                        v_ref[rows, lanes] = v
                        total = total + k * wk_ref[rows, lanes].astype(f32) + v * wv_ref[rows, lanes].astype(f32)
                    summed = jnp.sum(jnp.transpose(total), axis=0, keepdims=True)
                    norm_ref[:, rows] = summed / gain_ref[:, rows]
                for b in range(4):
                    at = D + LANES * b - start
                    if 0 <= at < 384:
                        for j in range(PAIRS):
                            o_ref[j * LANES : (j + 1) * LANES, 256 * b : 256 * (b + 1)] = piece[
                                2 * j + h, at : at + LANES, :
                            ].astype(f32)

    @pl.when(core_ref[0] == 0)
    def _():
        write((own_ref, other_ref))

    @pl.when(core_ref[0] == 1)
    def _():
        write((other_ref, own_ref))


def assemble(core, own, other, wq, wk, wv, gain):
    smem = pl.BlockSpec(memory_space=pltpu.SMEM)
    vmem = pl.BlockSpec(memory_space=pltpu.VMEM)
    return call(
        assemble_kernel,
        (
            struct((D, D), f32),
            struct((D, 512), f32),
            struct((D, 512), f32),
            struct((D, D), f32),
            struct((1, D), f32),
        ),
        1e6,
        2.2e7,
        in_specs=[smem] + [vmem] * 6,
        out_specs=(vmem,) * 5,
        name="assemble",
    )(core, own, other, wq, wk, wv, gain.reshape(1, D))


def after(x, *earlier):
    return lax.optimization_barrier((x, *earlier))[0]


def to_owners(x):
    return lax.all_to_all(x, "expert", split_axis=0, concat_axis=0, tiled=True)


def mirror(x):
    return lax.ppermute(x, "context", [(0, 3), (1, 2), (2, 1), (3, 0)])


def swap_cores(x):
    return lax.ppermute(x, "dp", [(0, 1), (1, 0)])


def shift(x, by):
    return lax.ppermute(x, "context", [(i, (i + by) % 4) for i in range(4)])


def neighbour(x):
    return lax.ppermute(x, "context", [(0, 1), (1, 0), (2, 3), (3, 2)])


def swap_halves(x):
    return lax.ppermute(x, "expert", [(i, i ^ 1) for i in range(16)])


def pick(x, index, axis=0):
    return lax.dynamic_index_in_dim(x, index, axis, False)


def rope_tables(positions):
    frequency = rope_base ** (-jnp.arange(0, HEAD_DIM, 2, dtype=f32) / HEAD_DIM)
    angles = positions.astype(f32)[:, None] * frequency[None, :]
    cos, sin = jnp.cos(angles), jnp.sin(angles)
    return jnp.concatenate([cos] * 4, -1), jnp.concatenate([-sin, sin] * 2, -1)


def local(
    layer_input, grad_output, norm1_gain, norm2_gain, w_query, w_key, w_value, w_out, w_router, w_gate_up, w_down, routes
):
    context = lax.axis_index("context")
    expert = lax.axis_index("expert")
    x = layer_input[0, 0]
    top = grad_output[0, 0]

    half = expert % 2

    cos, sin = rope_tables(context * BLOCK + expert * TOK + jnp.arange(TOK, dtype=jnp.int32))
    order = jnp.arange(1024, dtype=jnp.int32)
    half_cos, half_sin = rope_tables(context * BLOCK + order + (order // 64) * 64 + half * 64)

    hits = jnp.sum((routes[0, 0][:, :, None] == jnp.arange(EXPERTS, dtype=jnp.int32)).astype(f32), 1)
    lower = np.tril(np.ones((TOK, TOK), np.float32), -1)
    place = dot(jnp.asarray(lower, bf16), hits.astype(bf16))
    owner = np.repeat(np.eye(EXPERTS, dtype=np.float32), CAP, 0)
    owner16 = jnp.asarray(owner, bf16)
    slot_number = jnp.arange(SLOTS, dtype=jnp.int32) % CAP
    marked = jnp.where(hits > 0.5, place, 255.0).astype(bf16)
    spot = (dot_rows(marked, owner16) == slot_number[None, :].astype(f32)).astype(bf16)
    selector = (dot_rows(owner16, marked) == slot_number[:, None].astype(f32)).astype(bf16)

    core_index = lax.axis_index("dp")
    core = core_index.astype(jnp.int32).reshape(1)
    act_send, q_send, kv_send = project(x, norm1_gain, w_query, w_key, w_value, cos, sin)
    kv_own = to_owners(kv_send)
    kv_a, kv_b = kv_own[:8], kv_own[8:]
    left_a, right_b = shift(kv_a, 1), shift(kv_b, 3)
    left_b, right_a = shift(kv_b, 1), shift(kv_a, 3)
    q_own = to_owners(after(q_send, kv_own))
    q_far = mirror(q_own[8:])
    far_a, far_b = shift(left_a, 1), shift(right_b, 3)

    gate_up = lax.all_gather(after(w_gate_up, far_a, far_b), ("context", "dp"), axis=1, tiled=True)
    down = lax.all_gather(w_down, ("context", "dp"), axis=1, tiled=True)
    top_send = dot(selector, top).astype(bf16).reshape(16, 2, CAP, D)
    top_rows = to_owners(after(top_send, q_far))

    seat = jnp.stack([context, half]).astype(jnp.int32)
    o, o_low, o_far, lse, kv = attend_forward(
        seat, q_own, q_far, (kv_own, left_a, left_b, far_a, far_b, right_a, right_b)
    )
    o_far = after(o_far, top_rows)
    o_own = jnp.concatenate([o_low, mirror(o_far)], 0)
    att = to_owners(o_own)
    raw = raw_grads(top_rows, down)
    att = after(att, raw)

    hidden, send = middle(att, x, w_out, norm2_gain, selector)
    rows = to_owners(send.reshape(16, 2, CAP, D))
    first = (2 * expert).astype(jnp.int32).reshape(1)
    act_rows = to_owners(after(act_send, rows)).reshape(1024, D)
    grad_rows, expert_hidden, mixed, gates, logits = experts(first, rows, raw, gate_up, w_router)
    back = to_owners(after(grad_rows, act_rows))
    out_rows, dgu, ddown, router_grad = expert_grads(rows, top_rows, gates, logits, expert_hidden, mixed, down)
    back = after(back, dgu)

    state, attn_send, do_send, norm2_grad = turn_back(back.reshape(SLOTS, D), spot, hidden, norm2_gain, top, w_out)
    do_own = to_owners(do_send)
    do_far = mirror(do_own[8:])
    attn_rows = to_owners(after(attn_send, do_own)).reshape(1024, D)
    small = lax.psum(
        jnp.concatenate([router_grad[0] + router_grad[1], norm2_grad], 0), ("expert", "context", "dp")
    )
    grad_gate_up = lax.psum_scatter(
        after(dgu, do_own), ("context", "dp"), scatter_dimension=1, tiled=True
    ).astype(f32)

    dq, dq_far, d0, d1a, d1b, d2a, d2b, d3a, d3b = attend_backward(seat, q_own, q_far, do_own, do_far, o, lse, kv)
    dq, dq_far, d0, d1a, d1b, d2a, d2b, d3a, d3b, attn_rows = lax.optimization_barrier(
        (dq, dq_far, d0, d1a, d1b, d2a, d2b, d3a, d3b, attn_rows)
    )

    far_a, far_b = shift(d2a, 1), shift(d2b, 3)
    from_left_b, from_right_a = shift(d3b, 1), shift(d1a, 3)
    dq_far = mirror(dq_far)
    dq_own = jnp.concatenate([dq, dq_far], 0).reshape(1024, LANES)
    returned = to_owners(after(out_rows, dq_far))
    from_left_a = shift((d3a.astype(f32) + far_a.astype(f32)).astype(bf16), 1)
    from_right_b = shift((d1b.astype(f32) + far_b.astype(f32)).astype(bf16), 3)
    own = d0.reshape(2, 8, 2, 64, LANES)

    def half_sum(which):
        first_part = pick(own[0], which, 1)
        second_part = pick(own[1], which, 1)
        for piece in (from_left_a, from_right_a):
            first_part = first_part + pick(piece.reshape(8, 2, 64, LANES), which, 1).astype(f32)
        for piece in (from_left_b, from_right_b):
            second_part = second_part + pick(piece.reshape(8, 2, 64, LANES), which, 1).astype(f32)
        return jnp.concatenate([first_part, second_part], 0).reshape(1024, LANES)

    got = swap_halves(half_sum(1 - half).astype(bf16))
    mine, other, grads = head_grads(
        core, act_rows, attn_rows, o_own.reshape(1024, LANES), dq_own, half_sum(half), got, half_cos, half_sin
    )
    other = swap_cores(other).reshape(2, 384, 256)
    mine = mine.reshape(2, 384, 256)
    give = (pick(mine, 1 - half).astype(f32) + pick(other, 1 - half).astype(f32)).astype(bf16)
    keep = pick(mine, half).astype(f32) + pick(other, half).astype(f32)
    grads_back = to_owners(after(grads, returned).reshape(16, 64, 256))
    total = (keep + swap_halves(give).astype(f32)).astype(bf16)
    total = (total.astype(f32) + neighbour(total).astype(f32)).astype(bf16)
    total = (total.astype(f32) + mirror(total).astype(f32)).astype(bf16)
    block = after(jnp.broadcast_to(total[None], (16, 384, 256)), grads_back, small)
    whole = to_owners(block)

    grad_input = finish(grads_back, x, norm1_gain, w_query, w_key, w_value, state)
    block_out = hidden + branch_scale * dot(spot, returned.reshape(SLOTS, D))
    grad_down = lax.psum_scatter(after(ddown, got), ("context", "dp"), scatter_dimension=1, tiled=True).astype(f32)
    whole, grad_input, block_out, grad_gate_up = lax.optimization_barrier(
        (whole, grad_input, block_out, grad_gate_up)
    )
    dwq, dwk, dwv, dwo, norm1_grad = assemble(
        core, whole, swap_cores(whole), w_query, w_key, w_value, norm1_gain
    )
    return (
        block_out.reshape(1, 1, TOK, D),
        grad_input.reshape(1, 1, TOK, D),
        norm1_grad[0],
        small[EXPERTS],
        dwq,
        dwk,
        dwv,
        dwo,
        small[:EXPERTS].T,
        grad_gate_up,
        grad_down,
    )


def solution(mesh):
    tokens = P("dp", "context", "expert", None)
    weights = P("expert", ("context", "dp"), None)
    return jax.shard_map(
        local,
        mesh=mesh,
        in_specs=(tokens, tokens, P(), P(), P(), P(), P(), P(), P(), weights, weights, tokens),
        out_specs=(tokens, tokens, P(), P(), P(), P(), P(), P(), P(), weights, weights),
        check_vma=False,
    )
```

```python
import jax
import jax.numpy as jnp
import numpy as np
from jax import lax
from jax.experimental import pallas as pl
from jax.experimental.pallas import tpu as pltpu
from jax.sharding import PartitionSpec as P

D = 1024
HEAD_DIM = 64
F = 512
EXPERTS = 32
CAP = 48
TOK = 128
BLOCK = 2048
LANES = 128
SLOTS = EXPERTS * CAP
PAIRS = 8
CHUNK = 512

norm_eps = 1e-06
score_scale = 0.015625
branch_scale = 0.22
rope_base = 10000.0
huge_negative = -1e30
bf16 = jnp.bfloat16
f32 = jnp.float32
VMEM_LIMIT = 56 * 1024 * 1024


def call(kernel, out_shape, flops, moved, **kw):
    return pl.pallas_call(
        kernel,
        out_shape=out_shape,
        compiler_params=pltpu.CompilerParams(vmem_limit_bytes=VMEM_LIMIT),
        cost_estimate=pl.CostEstimate(flops=int(flops), bytes_accessed=int(moved), transcendentals=0),
        **kw,
    )


def struct(shape, dtype):
    return jax.ShapeDtypeStruct(shape, dtype)


def dot(a, b):
    return jnp.dot(a, b, preferred_element_type=f32)


def dot_rows(a, b):
    return lax.dot_general(a, b, (((1,), (1,)), ((), ())), preferred_element_type=f32)


def dot_down(a, b):
    return lax.dot_general(a, b, (((0,), (0,)), ((), ())), preferred_element_type=f32)


def split2(x):
    hi = x.astype(bf16)
    return hi, (x - hi.astype(f32)).astype(bf16)


def lane_index(shape):
    return lax.broadcasted_iota(jnp.int32, shape, len(shape) - 1)


def project_kernel(x_ref, gain_ref, wq_ref, wk_ref, wv_ref, cos_ref, sin_ref, act_ref, q_ref, kv_ref):
    x = x_ref[...].astype(f32)
    inverse = lax.rsqrt(jnp.mean(x * x, axis=-1, keepdims=True) + norm_eps)
    act = (x * inverse * gain_ref[...]).astype(bf16)
    for e in range(16):
        act_ref[e] = act[64 * (e % 2) : 64 * (e % 2) + 64]
    cos = cos_ref[...]
    sin = sin_ref[...]
    lane = lane_index((TOK, LANES))
    first = lane % HEAD_DIM < HEAD_DIM // 2
    left = lane < HEAD_DIM

    def turn(v):
        moved = jnp.where(first, pltpu.roll(v, LANES - 32, 1), pltpu.roll(v, 32, 1))
        return v * cos + moved * sin

    q = dot(act, wq_ref[...])
    for j in range(PAIRS):
        rows = turn(q[:, j * LANES : (j + 1) * LANES]).astype(bf16)
        q_ref[2 * j] = rows[: TOK // 2]
        q_ref[2 * j + 1] = rows[TOK // 2 :]
    k = dot(act, wk_ref[...])
    v = dot(act, wv_ref[...])
    for b in range(PAIRS // 2):
        kb = turn(k[:, b * LANES : (b + 1) * LANES])
        vb = v[:, b * LANES : (b + 1) * LANES]
        even = jnp.where(left, kb, pltpu.roll(vb, HEAD_DIM, 1)).astype(bf16)
        odd = jnp.where(left, pltpu.roll(kb, HEAD_DIM, 1), vb).astype(bf16)
        kv_ref[4 * b] = even
        kv_ref[4 * b + 1] = even
        kv_ref[4 * b + 2] = odd
        kv_ref[4 * b + 3] = odd


def project(x, gain, wq, wk, wv, cos, sin):
    return call(
        project_kernel,
        (struct((16, 64, D), bf16), struct((16, 64, LANES), bf16), struct((16, TOK, LANES), bf16)),
        2 * TOK * D * 2048,
        6e6,
        name="project",
    )(x, gain.reshape(1, D), wq, wk, wv, cos, sin)


def query_of_head(q, head, left):
    q = q.astype(f32) * score_scale
    if head:
        q = pltpu.roll(q, HEAD_DIM, 1)
    return jnp.where(left, q, 0.0).astype(bf16)


def forward_kernel(
    place_ref, q_ref, q_far_ref, own_ref, left_ref, far_a_ref, far_b_ref, right_ref,
    o_ref, low_ref, low_far_ref, lse_ref, kv_ref, qm_ref, top_ref, acc_ref,
):
    tile = 1024
    context = place_ref[0]
    half = place_ref[1]

    def put(back, part, ref):
        start = lax.rem(context + 4 - back, 4) * BLOCK + part * (BLOCK // 2)
        rows = ref.shape[0]
        kv_ref[pl.ds(pl.multiple_of(start, BLOCK // 2), rows), :] = ref[...]

    put(0, 0, own_ref)
    put(1, 0, left_ref)
    put(2, 0, far_a_ref)
    put(2, 1, far_b_ref)
    put(3, 0, right_ref)
    left = lane_index((CHUNK, LANES)) < HEAD_DIM
    left_keys = lane_index((tile, LANES)) < HEAD_DIM
    for chunk in range(2):
        whole = 2 * (context if chunk == 0 else 3 - context) + chunk
        queries = (q_far_ref[...] if chunk else q_ref[:8]).reshape(CHUNK, LANES)
        for head in range(2):
            qm_ref[head] = query_of_head(queries, head, left)
            top_ref[head] = jnp.full((CHUNK, LANES), huge_negative, f32)
            acc_ref[head] = jnp.zeros((CHUNK, LANES), f32)

        def step(index, masked):
            keys = kv_ref[pl.ds(pl.multiple_of(index * tile, tile), tile), :]
            values = jnp.where(left_keys, jnp.ones_like(keys), keys)
            for head in range(2):
                for part in range(2):
                    rows = slice(part * 256, part * 256 + 256)
                    s = dot_rows(qm_ref[head, rows], keys)
                    if masked:
                        r = lax.broadcasted_iota(jnp.int32, s.shape, 0) + part * 256
                        place = r + (r // 64) * 64 + half * 64
                        s = jnp.where(lane_index(s.shape) <= place, s, huge_negative)
                    old = top_ref[head, rows]
                    new = jnp.maximum(old, jnp.max(s, axis=1, keepdims=True))
                    p = jnp.exp(s - new[:, :1]).astype(bf16)
                    acc_ref[head, rows] = acc_ref[head, rows] * jnp.exp(old - new) + dot(p, values)
                    top_ref[head, rows] = new

        def visit(index, carry):
            step(index, False)
            return carry

        lax.fori_loop(0, whole, visit, 0)
        step(whole, True)
        outs = []
        for head in range(2):
            acc = acc_ref[head]
            outs.append(pltpu.roll(acc, HEAD_DIM, 1) / acc)
            total = top_ref[head] + jnp.log(jnp.where(left, acc, 1.0))
            lse_ref[2 * chunk + head] = jnp.transpose(total)[0:8]
        o = jnp.where(left, outs[0], pltpu.roll(outs[1], HEAD_DIM, 1))
        o_ref[chunk] = o
        (low_far_ref if chunk else low_ref)[...] = o.astype(bf16).reshape(8, 64, LANES)


def attend_forward(place, q, q_far, kv_parts):
    smem = pl.BlockSpec(memory_space=pltpu.SMEM)
    vmem = pl.BlockSpec(memory_space=pltpu.VMEM)
    return call(
        forward_kernel,
        (
            struct((2, CHUNK, LANES), f32),
            struct((8, 64, LANES), bf16),
            struct((8, 64, LANES), bf16),
            struct((4, 8, CHUNK), f32),
            struct((4 * BLOCK, LANES), bf16),
        ),
        2e10,
        4e6,
        in_specs=[smem] + [vmem] * 7,
        out_specs=(vmem,) * 5,
        scratch_shapes=[
            pltpu.VMEM((2, CHUNK, LANES), bf16),
            pltpu.VMEM((2, CHUNK, LANES), f32),
            pltpu.VMEM((2, CHUNK, LANES), f32),
        ],
        name="attend",
    )(place, q, q_far, *kv_parts)


def backward_kernel(
    place_ref, q_ref, q_far_ref, do_ref, do_far_ref, o_ref, lse_ref, kv_ref,
    dq_ref, dq_far_ref, d0_ref, d1a_ref, d1b_ref, d2a_ref, d2b_ref, d3a_ref, d3b_ref,
    qm_ref, dom_ref, row_ref, dqt_ref, acc_ref,
):
    tile = 512
    context = place_ref[0]
    half = place_ref[1]
    left = lane_index((CHUNK, LANES)) < HEAD_DIM
    acc_ref[...] = jnp.zeros_like(acc_ref)
    for chunk in range(2):
        whole = 2 * (2 * (context if chunk == 0 else 3 - context) + chunk)
        queries = (q_far_ref[...] if chunk else q_ref[:8]).reshape(CHUNK, LANES)
        do = (do_far_ref[...] if chunk else do_ref[:8]).reshape(CHUNK, LANES).astype(f32)
        product = jnp.transpose(do * o_ref[chunk])
        for head in range(2):
            qm_ref[head] = query_of_head(queries, head, left)
            moved = do if head else pltpu.roll(do, HEAD_DIM, 1)
            dom_ref[head] = jnp.where(left, 0.0, moved).astype(bf16)
            dqt_ref[head] = jnp.zeros((LANES, CHUNK), f32)
            rows = product[head * HEAD_DIM : (head + 1) * HEAD_DIM]
            row_ref[head] = jnp.broadcast_to(jnp.sum(rows, axis=0, keepdims=True), (8, CHUNK))

        def step(index, offset):
            span = pl.ds(pl.multiple_of(index * tile, tile), tile)
            keys = kv_ref[span, :]
            for head in range(2):
                qm = qm_ref[head]
                dom = dom_ref[head]
                s = dot_rows(keys, qm)
                dp = dot_rows(keys, dom)
                p = jnp.exp(s - lse_ref[2 * chunk + head, 0:1])
                if offset is not None:
                    r = lane_index(s.shape)
                    place = r + (r // 64) * 64 + half * 64
                    key = lax.broadcasted_iota(jnp.int32, s.shape, 0) + offset
                    p = jnp.where(key <= place, p, 0.0)
                ds = (p * (dp - row_ref[head, 0:1])).astype(bf16)
                acc_ref[span, :] += dot(ds, qm) + dot(p.astype(bf16), dom)
                dqt_ref[head] += dot_down(keys, ds)

        def visit(index, carry):
            step(index, None)
            return carry

        lax.fori_loop(0, whole, visit, 0)
        step(whole, 0)
        step(whole + 1, tile)
        parts = [jnp.transpose(dqt_ref[head]) * score_scale for head in range(2)]
        dq = jnp.where(left, parts[0], pltpu.roll(parts[1], HEAD_DIM, 1)).astype(bf16)
        (dq_far_ref if chunk else dq_ref)[...] = dq.reshape(8, 64, LANES)
    d0_ref[...] = acc_ref[pl.ds(pl.multiple_of(context * BLOCK, BLOCK), BLOCK), :]
    for back, first, second in ((1, d1a_ref, d1b_ref), (2, d2a_ref, d2b_ref), (3, d3a_ref, d3b_ref)):
        start = pl.multiple_of(lax.rem(context + 4 - back, 4) * BLOCK, BLOCK)
        first[...] = acc_ref[pl.ds(start, BLOCK // 2), :].astype(bf16)
        second[...] = acc_ref[pl.ds(pl.multiple_of(start + BLOCK // 2, BLOCK // 2), BLOCK // 2), :].astype(bf16)


def attend_backward(place, q, q_far, do, do_far, o, lse, kv):
    smem = pl.BlockSpec(memory_space=pltpu.SMEM)
    vmem = pl.BlockSpec(memory_space=pltpu.VMEM)
    rows = kv.shape[0]
    return call(
        backward_kernel,
        (struct((8, 64, LANES), bf16), struct((8, 64, LANES), bf16), struct((BLOCK, LANES), f32))
        + (struct((BLOCK // 2, LANES), bf16),) * 6,
        5e10,
        8e6,
        in_specs=[smem] + [vmem] * 7,
        out_specs=(vmem,) * 9,
        scratch_shapes=[
            pltpu.VMEM((2, CHUNK, LANES), bf16),
            pltpu.VMEM((2, CHUNK, LANES), bf16),
            pltpu.VMEM((2, 8, CHUNK), f32),
            pltpu.VMEM((2, LANES, CHUNK), f32),
            pltpu.VMEM((rows, LANES), f32),
        ],
        name="attend_back",
    )(place, q, q_far, do, do_far, o, lse, kv)


def middle_kernel(att_ref, x_ref, wo_ref, gain_ref, pick_ref, hidden_ref, send_ref, attended_ref):
    for j in range(PAIRS):
        for h in range(2):
            attended_ref[h * 64 : h * 64 + 64, j * LANES : (j + 1) * LANES] = att_ref[2 * j + h]
    hidden = x_ref[...].astype(f32) + branch_scale * dot(attended_ref[...], wo_ref[...])
    hidden_ref[...] = hidden
    inverse = lax.rsqrt(jnp.mean(hidden * hidden, axis=-1, keepdims=True) + norm_eps)
    act = (hidden * inverse * gain_ref[...]).astype(bf16)
    send_ref[...] = dot(pick_ref[...], act).astype(bf16)


def middle(att, x, wo, gain, pick):
    return call(
        middle_kernel,
        (struct((TOK, D), f32), struct((SLOTS, D), bf16)),
        2 * TOK * D * (D + SLOTS),
        8e6,
        scratch_shapes=[pltpu.VMEM((TOK, D), bf16)],
        name="middle",
    )(att, x, wo, gain.reshape(1, D), pick)


def raw_kernel(top_ref, down_ref, raw_ref):
    raw_ref[...] = branch_scale * dot_rows(top_ref[...].reshape(768, D), down_ref[...])


def raw_grads(top, down):
    per = pl.BlockSpec((16, None, CAP, D), lambda n: (0, n, 0, 0))
    return call(
        raw_kernel, struct((2, 768, F), f32), 2 * SLOTS * D * F, 8e6, grid=(2,), in_specs=[per, owned(F, D)],
        out_specs=owned(768, F), name="raw",
    )(top, down)


def expert_kernel(
    first_ref, x_ref, raw_ref, gu_ref, wr_ref, back_ref, hidden_ref, mixed_ref, gate_ref, logit_ref
):
    number = first_ref[0] + pl.program_id(0)
    wr = wr_ref[...]
    for part in range(2):
        take = slice(8 * part, 8 * part + 8)
        rows = slice(384 * part, 384 * part + 384)
        x = x_ref[take].reshape(384, D)
        logits = dot(x, wr)
        raised = jnp.exp(logits - jnp.max(logits, axis=-1, keepdims=True))
        probs = raised / jnp.sum(raised, axis=-1, keepdims=True)
        chosen = (lane_index(probs.shape) == number).astype(f32)
        gate_value = jnp.sum(probs * chosen, axis=-1, keepdims=True)
        gate_ref[rows] = gate_value
        pre = dot(x, gu_ref[...])
        raw = raw_ref[rows]
        gate = pre[:, :F]
        up = pre[:, F:]
        sig = 1.0 / (1.0 + jnp.exp(-gate))
        act = gate * sig
        hidden = (act * up).astype(bf16)
        hidden_ref[rows] = hidden
        grad_gate = jnp.sum(hidden.astype(f32) * raw, axis=-1, keepdims=True)
        grad_logits = (gate_value * grad_gate) * (chosen - probs)
        logit_ref[rows] = grad_logits
        raw = raw * gate_value
        mixed_gate = (raw * up * sig * (1.0 + gate * (1.0 - sig))).astype(bf16)
        mixed_up = (raw * act).astype(bf16)
        mixed_ref[rows, :F] = mixed_gate
        mixed_ref[rows, F:] = mixed_up
        hi, lo = split2(grad_logits)
        back = dot_rows(mixed_gate, gu_ref[:, :F]) + dot_rows(mixed_up, gu_ref[:, F:])
        back = back + dot_rows(hi, wr) + dot_rows(lo, wr)
        back_ref[take] = back.astype(bf16).reshape(8, CAP, D)


def owned(*shape):
    return pl.BlockSpec((None, *shape), lambda n: (n, *([0] * len(shape))))


def experts(first, x, raw, gate_up, wr):
    per = pl.BlockSpec((16, None, CAP, D), lambda n: (0, n, 0, 0))
    return call(
        expert_kernel,
        (
            struct((16, 2, CAP, D), bf16),
            struct((2, 768, F), bf16),
            struct((2, 768, D), bf16),
            struct((2, 768, 1), f32),
            struct((2, 768, EXPERTS), f32),
        ),
        2 * SLOTS * D * 2560,
        2e7,
        grid=(2,),
        in_specs=[
            pl.BlockSpec(memory_space=pltpu.SMEM),
            per,
            owned(768, F),
            owned(D, D),
            pl.BlockSpec((D, EXPERTS), lambda n: (0, 0)),
        ],
        out_specs=(per, owned(768, F), owned(768, D), owned(768, 1), owned(768, EXPERTS)),
        name="experts",
    )(first, x, raw, gate_up, wr)


def expert_grads_kernel(
    x_ref, top_ref, gate_ref, logit_ref, hidden_ref, mixed_ref, down_ref, out_ref, dgu_ref, ddown_ref, router_ref
):
    hidden = hidden_ref[...]
    gate = gate_ref[...]
    x = x_ref[...].reshape(768, D)
    out_ref[...] = (gate * dot(hidden, down_ref[...])).astype(bf16).reshape(16, CAP, D)
    top = (branch_scale * gate * top_ref[...].reshape(768, D).astype(f32)).astype(bf16)
    ddown_ref[...] = dot_down(hidden, top).astype(bf16)
    dgu_ref[...] = dot_down(x, mixed_ref[...]).astype(bf16)
    hi, lo = split2(logit_ref[...])
    router_ref[...] = dot_down(hi, x) + dot_down(lo, x)


def expert_grads(x, top, gate, logits, hidden, mixed, down):
    per = pl.BlockSpec((16, None, CAP, D), lambda n: (0, n, 0, 0))
    return call(
        expert_grads_kernel,
        (
            struct((16, 2, CAP, D), bf16),
            struct((2, D, D), bf16),
            struct((2, F, D), bf16),
            struct((2, EXPERTS, D), f32),
        ),
        2 * SLOTS * D * 2048,
        2.4e7,
        grid=(2,),
        in_specs=[per, per, owned(768, 1), owned(768, EXPERTS), owned(768, F), owned(768, D), owned(F, D)],
        out_specs=(per, owned(D, D), owned(F, D), owned(EXPERTS, D)),
        name="expert_grads",
    )(x, top, gate, logits, hidden, mixed, down)


def turn_back_kernel(
    back_ref, spot_ref, hidden_ref, gain_ref, top_ref, wo_ref, router_ref, state_ref, attn_ref, send_ref
):
    grad = dot(spot_ref[...], back_ref[...])
    hidden = hidden_ref[...]
    inverse = lax.rsqrt(jnp.mean(hidden * hidden, axis=-1, keepdims=True) + norm_eps)
    normed = hidden * inverse
    scaled = grad * gain_ref[...]
    state = top_ref[...].astype(f32) + inverse * (scaled - normed * jnp.mean(scaled * normed, axis=-1, keepdims=True))
    state_ref[...] = state
    attn = (branch_scale * state).astype(bf16)
    router = router_ref[0] + router_ref[1]
    norm = jnp.sum(grad * normed, axis=0, keepdims=True)
    for e in range(16):
        attn_ref[e, :64] = attn[64 * (e % 2) : 64 * (e % 2) + 64]
        if e < 8:
            extra = jnp.concatenate([router[4 * e : 4 * e + 4], jnp.zeros((12, D), f32)], axis=0)
        elif e == 8:
            extra = jnp.concatenate([norm, jnp.zeros((15, D), f32)], axis=0)
        else:
            extra = jnp.zeros((16, D), f32)
        attn_ref[e, 64:] = extra.astype(bf16)
    attended = dot_rows(attn, wo_ref[...]).astype(bf16)
    for j in range(PAIRS):
        for h in range(2):
            send_ref[2 * j + h] = attended[h * 64 : h * 64 + 64, j * LANES : (j + 1) * LANES]


def turn_back(back, spot, hidden, gain, top, wo, router):
    return call(
        turn_back_kernel,
        (
            struct((TOK, D), f32),
            struct((16, 80, D), bf16),
            struct((16, TOK // 2, LANES), bf16),
        ),
        2 * 256 * D * (D + SLOTS),
        8e6,
        name="turn_back",
    )(back, spot, hidden, gain.reshape(1, D), top, wo, router)


def unturn(v, cos, sin, first):
    scaled = v * sin
    return v * cos + jnp.where(first, pltpu.roll(scaled, LANES - 32, 1), pltpu.roll(scaled, 32, 1))


def merge_kernel(
    place_ref, d0_ref, left_a_ref, left_b_ref, right_a_ref, right_b_ref, keep_ref, give_ref, sum_ref
):
    half = place_ref[1]
    for part, left, right in ((0, left_a_ref, right_a_ref), (1, left_b_ref, right_b_ref)):
        rows = slice(part * 1024, part * 1024 + 1024)
        total = d0_ref[rows] + left[...].astype(f32) + right[...].astype(f32)
        sum_ref[8 * part : 8 * part + 8] = total.reshape(8, TOK, LANES)
    keep_ref[...] = sum_ref[:, pl.ds(pl.multiple_of(half * 64, 64), 64), :]
    give_ref[...] = sum_ref[:, pl.ds(pl.multiple_of((1 - half) * 64, 64), 64), :].astype(bf16)


def merge(place, *pieces):
    smem = pl.BlockSpec(memory_space=pltpu.SMEM)
    vmem = pl.BlockSpec(memory_space=pltpu.VMEM)
    return call(
        merge_kernel,
        (struct((16, 64, LANES), f32), struct((16, 64, LANES), bf16)),
        1e6,
        3e6,
        in_specs=[smem] + [vmem] * 5,
        out_specs=(vmem, vmem),
        scratch_shapes=[pltpu.VMEM((16, TOK, LANES), f32)],
        name="merge",
    )(place, *pieces)


def unturn_kernel(dq_ref, dq_far_ref, keep_ref, got_ref, cos_ref, sin_ref, grads_ref):
    lane = lane_index((512, LANES))
    first = lane % HEAD_DIM < HEAD_DIM // 2
    for part, dq in ((0, dq_ref), (1, dq_far_ref)):
        rows = slice(512 * part, 512 * part + 512)
        take = slice(8 * part, 8 * part + 8)
        cos = cos_ref[rows]
        sin = sin_ref[rows]
        grads_ref[rows, :LANES] = unturn(dq[...].reshape(512, LANES).astype(f32), cos, sin, first).astype(bf16)
        both = (keep_ref[take] + got_ref[take].astype(f32)).reshape(512, LANES).astype(bf16).astype(f32)
        grads_ref[rows, LANES:] = jnp.where(lane < HEAD_DIM, unturn(both, cos, sin, first), both).astype(bf16)


def unturn_rows(dq, dq_far, keep, got, cos, sin):
    return call(unturn_kernel, struct((1024, 256), bf16), 1e6, 3e6, name="unturn")(dq, dq_far, keep, got, cos, sin)


def head_kernel(core_ref, act_ref, attn_ref, o_ref, grads_ref, mine_ref, other_ref, all_ref):
    all_ref[:D] = dot_down(act_ref[...], grads_ref[...]).astype(bf16)
    out = dot_down(o_ref[...], attn_ref[:, :64, :].reshape(1024, D)).astype(bf16)
    for b in range(4):
        all_ref[D + LANES * b : D + LANES * (b + 1)] = out[:, 256 * b : 256 * (b + 1)]
    extra = attn_ref[0, 64:].astype(f32)
    for e in range(1, 16):
        extra = extra + attn_ref[e, 64:].astype(f32)
    packed = extra[:, :256]
    for b in range(1, 4):
        packed = packed + pltpu.roll(extra[:, 256 * b : 256 * (b + 1)], 4 * b, 0)
    packed = packed.astype(bf16)
    core = core_ref[0]
    for which, out_ref in ((1 - core, other_ref), (core, mine_ref)):
        out_ref[:768] = all_ref[pl.ds(pl.multiple_of(which * 768, 768), 768), :]
        out_ref[768:] = packed


def head_grads(core, act, attn, o, grads):
    smem = pl.BlockSpec(memory_space=pltpu.SMEM)
    vmem = pl.BlockSpec(memory_space=pltpu.VMEM)
    half = struct((784, 256), bf16)
    return call(
        head_kernel,
        (half, half),
        2 * 1024 * 1024 * 512,
        8e6,
        in_specs=[smem] + [vmem] * 4,
        out_specs=(vmem,) * 2,
        scratch_shapes=[pltpu.VMEM((1536, 256), bf16)],
        name="head_grads",
    )(core, act, attn, o, grads)


def split_kernel(place_ref, mine_ref, other_ref, keep_ref, give_ref):
    half = place_ref[1]
    rows = pl.ds(pl.multiple_of(half * 384, 384), 384)
    keep_ref[:384] = mine_ref[rows, :].astype(f32) + other_ref[rows, :].astype(f32)
    keep_ref[384:] = mine_ref[768:, :].astype(f32) + other_ref[768:, :].astype(f32)
    rows = pl.ds(pl.multiple_of((1 - half) * 384, 384), 384)
    give_ref[...] = (mine_ref[rows, :].astype(f32) + other_ref[rows, :].astype(f32)).astype(bf16)


def split_halves(place, mine, other):
    smem = pl.BlockSpec(memory_space=pltpu.SMEM)
    vmem = pl.BlockSpec(memory_space=pltpu.VMEM)
    return call(
        split_kernel,
        (struct((400, 256), f32), struct((384, 256), bf16)),
        1e6,
        2e6,
        in_specs=[smem, vmem, vmem],
        out_specs=(vmem, vmem),
        name="split",
    )(place, mine, other)


def finish_kernel(grads_ref, x_ref, gain_ref, wq_ref, wk_ref, wv_ref, state_ref, out_ref, flat_ref):
    left = lane_index((TOK // 2, LANES)) < HEAD_DIM
    for h in range(2):
        rows = slice(64 * h, 64 * h + 64)
        for j in range(PAIRS):
            flat_ref[rows, j * LANES : (j + 1) * LANES] = grads_ref[2 * j + h, :, :LANES]
        for b in range(PAIRS // 2):
            even = grads_ref[4 * b + h, :, LANES:].astype(f32)
            odd = grads_ref[4 * b + 2 + h, :, LANES:].astype(f32)
            k = jnp.where(left, even, pltpu.roll(odd, HEAD_DIM, 1))
            v = jnp.where(left, pltpu.roll(even, HEAD_DIM, 1), odd)
            flat_ref[rows, D + b * LANES : D + (b + 1) * LANES] = k.astype(bf16)
            flat_ref[rows, D + 512 + b * LANES : D + 512 + (b + 1) * LANES] = v.astype(bf16)
    grad = dot_rows(flat_ref[:, :D], wq_ref[...])
    grad = grad + dot_rows(flat_ref[:, D : D + 512], wk_ref[...])
    grad = grad + dot_rows(flat_ref[:, D + 512 :], wv_ref[...])
    x = x_ref[...].astype(f32)
    inverse = lax.rsqrt(jnp.mean(x * x, axis=-1, keepdims=True) + norm_eps)
    normed = x * inverse
    scaled = grad * gain_ref[...]
    out_ref[...] = state_ref[...] + inverse * (scaled - normed * jnp.mean(scaled * normed, axis=-1, keepdims=True))


def finish(grads, x, gain, wq, wk, wv, state):
    return call(
        finish_kernel,
        struct((TOK, D), f32),
        2 * 256 * D * 2048,
        8e6,
        scratch_shapes=[pltpu.VMEM((TOK, 2048), bf16)],
        name="finish",
    )(grads, x, gain.reshape(1, D), wq, wk, wv, state)


def assemble_kernel(
    core_ref, own_ref, other_ref, wq_ref, wk_ref, wv_ref, gain_ref, q_ref, k_ref, v_ref, o_ref, norm_ref
):
    left = lane_index((384, LANES)) < HEAD_DIM

    def write(pieces):
        for core in range(2):
            piece = pieces[core]
            for h in range(2):
                start = 768 * core + 384 * h
                count = min(384, max(0, D - start))
                if count:
                    rows = slice(start, start + count)
                    total = jnp.zeros((count, LANES), f32)
                    for j in range(PAIRS):
                        lanes = slice(j * LANES, (j + 1) * LANES)
                        value = piece[2 * j + h, :count, :LANES].astype(f32)
                        q_ref[rows, lanes] = value
                        total = total + value * wq_ref[rows, lanes].astype(f32)
                    for b in range(PAIRS // 2):
                        lanes = slice(b * LANES, (b + 1) * LANES)
                        even = piece[4 * b + h, :count, LANES:].astype(f32)
                        odd = piece[4 * b + 2 + h, :count, LANES:].astype(f32)
                        k = jnp.where(left[:count], even, pltpu.roll(odd, HEAD_DIM, 1))
                        v = jnp.where(left[:count], pltpu.roll(even, HEAD_DIM, 1), odd)
                        k_ref[rows, lanes] = k
                        v_ref[rows, lanes] = v
                        total = total + k * wk_ref[rows, lanes].astype(f32) + v * wv_ref[rows, lanes].astype(f32)
                    summed = jnp.sum(jnp.transpose(total), axis=0, keepdims=True)
                    norm_ref[:, rows] = summed / gain_ref[:, rows]
                for b in range(4):
                    at = D + LANES * b - start
                    if 0 <= at < 384:
                        for j in range(PAIRS):
                            o_ref[j * LANES : (j + 1) * LANES, 256 * b : 256 * (b + 1)] = piece[
                                2 * j + h, at : at + LANES, :
                            ].astype(f32)

    @pl.when(core_ref[0] == 0)
    def _():
        write((own_ref, other_ref))

    @pl.when(core_ref[0] == 1)
    def _():
        write((other_ref, own_ref))


def assemble(core, own, other, wq, wk, wv, gain):
    smem = pl.BlockSpec(memory_space=pltpu.SMEM)
    vmem = pl.BlockSpec(memory_space=pltpu.VMEM)
    return call(
        assemble_kernel,
        (
            struct((D, D), f32),
            struct((D, 512), f32),
            struct((D, 512), f32),
            struct((D, D), f32),
            struct((1, D), f32),
        ),
        1e6,
        2.2e7,
        in_specs=[smem] + [vmem] * 6,
        out_specs=(vmem,) * 5,
        name="assemble",
    )(core, own, other, wq, wk, wv, gain.reshape(1, D))


def after(x, *earlier):
    return lax.optimization_barrier((x, *earlier))[0]


def to_owners(x):
    return lax.all_to_all(x, "expert", split_axis=0, concat_axis=0, tiled=True)


def mirror(x):
    return lax.ppermute(x, "context", [(0, 3), (1, 2), (2, 1), (3, 0)])


def swap_cores(x):
    return lax.ppermute(x, "dp", [(0, 1), (1, 0)])


def shift(x, by):
    return lax.ppermute(x, "context", [(i, (i + by) % 4) for i in range(4)])


def neighbour(x):
    return lax.ppermute(x, "context", [(0, 1), (1, 0), (2, 3), (3, 2)])


def swap_halves(x):
    return lax.ppermute(x, "expert", [(i, i ^ 1) for i in range(16)])


def pick(x, index, axis=0):
    return lax.dynamic_index_in_dim(x, index, axis, False)


def rope_tables(positions):
    frequency = rope_base ** (-jnp.arange(0, HEAD_DIM, 2, dtype=f32) / HEAD_DIM)
    angles = positions.astype(f32)[:, None] * frequency[None, :]
    cos, sin = jnp.cos(angles), jnp.sin(angles)
    return jnp.concatenate([cos] * 4, -1), jnp.concatenate([-sin, sin] * 2, -1)


def local(
    layer_input, grad_output, norm1_gain, norm2_gain, w_query, w_key, w_value, w_out, w_router, w_gate_up, w_down, routes
):
    context = lax.axis_index("context")
    expert = lax.axis_index("expert")
    x = layer_input[0, 0]
    top = grad_output[0, 0]

    half = expert % 2

    cos, sin = rope_tables(context * BLOCK + expert * TOK + jnp.arange(TOK, dtype=jnp.int32))
    order = jnp.arange(1024, dtype=jnp.int32)
    half_cos, half_sin = rope_tables(context * BLOCK + order + (order // 64) * 64 + half * 64)

    hits = jnp.sum((routes[0, 0][:, :, None] == jnp.arange(EXPERTS, dtype=jnp.int32)).astype(f32), 1)
    lower = np.tril(np.ones((TOK, TOK), np.float32), -1)
    place = dot(jnp.asarray(lower, bf16), hits.astype(bf16))
    owner = np.repeat(np.eye(EXPERTS, dtype=np.float32), CAP, 0)
    owner16 = jnp.asarray(owner, bf16)
    slot_number = jnp.arange(SLOTS, dtype=jnp.int32) % CAP
    marked = jnp.where(hits > 0.5, place, 255.0).astype(bf16)
    spot = (dot_rows(marked, owner16) == slot_number[None, :].astype(f32)).astype(bf16)
    selector = (dot_rows(owner16, marked) == slot_number[:, None].astype(f32)).astype(bf16)

    core_index = lax.axis_index("dp")
    core = core_index.astype(jnp.int32).reshape(1)
    act_send, q_send, kv_send = project(x, norm1_gain, w_query, w_key, w_value, cos, sin)
    kv_own = to_owners(kv_send).reshape(BLOCK, LANES)
    kv_left, kv_right = shift(kv_own, 1), shift(kv_own, 3)
    q_own = to_owners(after(q_send, kv_own))
    q_far = mirror(q_own[8:])
    far_a, far_b = shift(kv_left[: BLOCK // 2], 1), shift(kv_right[BLOCK // 2 :], 3)

    gate_up = lax.all_gather(after(w_gate_up, far_a, far_b), ("context", "dp"), axis=1, tiled=True)
    down = lax.all_gather(w_down, ("context", "dp"), axis=1, tiled=True)
    top_send = dot(selector, top).astype(bf16).reshape(16, 2, CAP, D)
    top_rows = to_owners(after(top_send, q_far))

    seat = jnp.stack([context, half]).astype(jnp.int32)
    o, o_low, o_far, lse, kv = attend_forward(
        seat, q_own, q_far, (kv_own, kv_left, far_a, far_b, kv_right)
    )
    o_far = after(o_far, top_rows)
    o_own = jnp.concatenate([o_low, mirror(o_far)], 0)
    att = to_owners(o_own)
    raw = raw_grads(top_rows, down)
    att = after(att, raw)

    hidden, send = middle(att, x, w_out, norm2_gain, selector)
    rows = to_owners(send.reshape(16, 2, CAP, D))
    first = (2 * expert).astype(jnp.int32).reshape(1)
    act_rows = to_owners(after(act_send, rows)).reshape(1024, D)
    grad_rows, expert_hidden, mixed, gates, logits = experts(first, rows, raw, gate_up, w_router)
    back = to_owners(after(grad_rows, act_rows))
    out_rows, dgu, ddown, router_grad = expert_grads(rows, top_rows, gates, logits, expert_hidden, mixed, down)
    back = after(back, dgu)

    state, attn_send, do_send = turn_back(
        back.reshape(SLOTS, D), spot, hidden, norm2_gain, top, w_out, router_grad
    )
    do_own = to_owners(do_send)
    do_far = mirror(do_own[8:])
    attn_rows = to_owners(after(attn_send, do_own))
    grad_gate_up = lax.psum_scatter(
        after(dgu, do_own), ("context", "dp"), scatter_dimension=1, tiled=True
    ).astype(f32)

    dq, dq_far, d0, d1a, d1b, d2a, d2b, d3a, d3b = attend_backward(seat, q_own, q_far, do_own, do_far, o, lse, kv)
    dq, dq_far, d0, d1a, d1b, d2a, d2b, d3a, d3b, attn_rows = lax.optimization_barrier(
        (dq, dq_far, d0, d1a, d1b, d2a, d2b, d3a, d3b, attn_rows)
    )

    far_a, far_b = shift(d2a, 1), shift(d2b, 3)
    from_left_b, from_right_a = shift(d3b, 1), shift(d1a, 3)
    dq_far = mirror(dq_far)
    returned = to_owners(after(out_rows, dq_far))
    from_left_a = shift((d3a.astype(f32) + far_a.astype(f32)).astype(bf16), 1)
    from_right_b = shift((d1b.astype(f32) + far_b.astype(f32)).astype(bf16), 3)
    keep, give = merge(seat, d0, from_left_a, from_left_b, from_right_a, from_right_b)
    got = swap_halves(give)
    grads = unturn_rows(dq, dq_far, keep, got, half_cos, half_sin)
    mine, other = head_grads(core, act_rows, attn_rows, o_own.reshape(1024, LANES), grads)
    keep, give = split_halves(seat, mine, swap_cores(other))
    grads_back = to_owners(after(grads, returned).reshape(16, 64, 256))
    total = keep + jnp.pad(swap_halves(give), ((0, 16), (0, 0))).astype(f32)
    total = total.astype(bf16)
    total = (total.astype(f32) + neighbour(total).astype(f32)).astype(bf16)
    total = (total.astype(f32) + mirror(total).astype(f32)).astype(bf16)
    block = after(jnp.broadcast_to(total[None], (16, 400, 256)), grads_back)
    whole = to_owners(block)

    grad_input = finish(grads_back, x, norm1_gain, w_query, w_key, w_value, state)
    block_out = hidden + branch_scale * dot(spot, returned.reshape(SLOTS, D))
    grad_down = lax.psum_scatter(after(ddown, got), ("context", "dp"), scatter_dimension=1, tiled=True).astype(f32)
    whole, grad_input, block_out, grad_gate_up = lax.optimization_barrier(
        (whole, grad_input, block_out, grad_gate_up)
    )
    dwq, dwk, dwv, dwo, norm1_grad = assemble(
        core, whole, swap_cores(whole), w_query, w_key, w_value, norm1_gain
    )
    small = whole[:, 384:].reshape(16, 4, 4, 256).transpose(0, 2, 1, 3).reshape(64, D).astype(f32)
    return (
        block_out.reshape(1, 1, TOK, D),
        grad_input.reshape(1, 1, TOK, D),
        norm1_grad[0],
        small[EXPERTS],
        dwq,
        dwk,
        dwv,
        dwo,
        small[:EXPERTS].T,
        grad_gate_up,
        grad_down,
    )


def solution(mesh):
    tokens = P("dp", "context", "expert", None)
    weights = P("expert", ("context", "dp"), None)
    return jax.shard_map(
        local,
        mesh=mesh,
        in_specs=(tokens, tokens, P(), P(), P(), P(), P(), P(), P(), weights, weights, tokens),
        out_specs=(tokens, tokens, P(), P(), P(), P(), P(), P(), P(), weights, weights),
        check_vma=False,
    )
```

```python
import jax
import jax.numpy as jnp
import numpy as np
from jax import lax
from jax.experimental import pallas as pl
from jax.experimental.pallas import tpu as pltpu
from jax.sharding import PartitionSpec as P

D = 1024
HEAD_DIM = 64
F = 512
EXPERTS = 32
CAP = 48
TOK = 128
BLOCK = 2048
LANES = 128
SLOTS = EXPERTS * CAP
PAIRS = 8
CHUNK = 512

norm_eps = 1e-06
score_scale = 0.015625
branch_scale = 0.22
rope_base = 10000.0
huge_negative = -1e30
bf16 = jnp.bfloat16
f32 = jnp.float32
VMEM_LIMIT = 56 * 1024 * 1024


def call(kernel, out_shape, flops, moved, **kw):
    return pl.pallas_call(
        kernel,
        out_shape=out_shape,
        compiler_params=pltpu.CompilerParams(vmem_limit_bytes=VMEM_LIMIT),
        cost_estimate=pl.CostEstimate(flops=int(flops), bytes_accessed=int(moved), transcendentals=0),
        **kw,
    )


def struct(shape, dtype):
    return jax.ShapeDtypeStruct(shape, dtype)


def dot(a, b):
    return jnp.dot(a, b, preferred_element_type=f32)


def dot_rows(a, b):
    return lax.dot_general(a, b, (((1,), (1,)), ((), ())), preferred_element_type=f32)


def dot_down(a, b):
    return lax.dot_general(a, b, (((0,), (0,)), ((), ())), preferred_element_type=f32)


def split2(x):
    hi = x.astype(bf16)
    return hi, (x - hi.astype(f32)).astype(bf16)


def lane_index(shape):
    return lax.broadcasted_iota(jnp.int32, shape, len(shape) - 1)


def project_kernel(x_ref, gain_ref, wq_ref, wk_ref, wv_ref, cos_ref, sin_ref, act_ref, q_ref, kv_ref):
    x = x_ref[...].astype(f32)
    inverse = lax.rsqrt(jnp.mean(x * x, axis=-1, keepdims=True) + norm_eps)
    act = (x * inverse * gain_ref[...]).astype(bf16)
    for e in range(16):
        act_ref[e] = act[64 * (e % 2) : 64 * (e % 2) + 64]
    cos = cos_ref[...]
    sin = sin_ref[...]
    lane = lane_index((TOK, LANES))
    first = lane % HEAD_DIM < HEAD_DIM // 2
    left = lane < HEAD_DIM

    def turn(v):
        moved = jnp.where(first, pltpu.roll(v, LANES - 32, 1), pltpu.roll(v, 32, 1))
        return v * cos + moved * sin

    q = dot(act, wq_ref[...])
    for j in range(PAIRS):
        rows = turn(q[:, j * LANES : (j + 1) * LANES]).astype(bf16)
        q_ref[2 * j] = rows[: TOK // 2]
        q_ref[2 * j + 1] = rows[TOK // 2 :]
    k = dot(act, wk_ref[...])
    v = dot(act, wv_ref[...])
    for b in range(PAIRS // 2):
        kb = turn(k[:, b * LANES : (b + 1) * LANES])
        vb = v[:, b * LANES : (b + 1) * LANES]
        even = jnp.where(left, kb, pltpu.roll(vb, HEAD_DIM, 1)).astype(bf16)
        odd = jnp.where(left, pltpu.roll(kb, HEAD_DIM, 1), vb).astype(bf16)
        kv_ref[4 * b] = even
        kv_ref[4 * b + 1] = even
        kv_ref[4 * b + 2] = odd
        kv_ref[4 * b + 3] = odd


def project(x, gain, wq, wk, wv, cos, sin):
    return call(
        project_kernel,
        (struct((16, 64, D), bf16), struct((16, 64, LANES), bf16), struct((16, TOK, LANES), bf16)),
        2 * TOK * D * 2048,
        6e6,
        name="project",
    )(x, gain.reshape(1, D), wq, wk, wv, cos, sin)


def query_of_head(q, head, left):
    q = q.astype(f32) * score_scale
    if head:
        q = pltpu.roll(q, HEAD_DIM, 1)
    return jnp.where(left, q, 0.0).astype(bf16)


def forward_kernel(
    place_ref, q_ref, q_far_ref, own_ref, left_ref, far_a_ref, far_b_ref, right_ref,
    o_ref, low_ref, low_far_ref, lse_ref, kv_ref, qm_ref, top_ref, acc_ref,
):
    tile = 1024
    context = place_ref[0]
    half = place_ref[1]

    def put(back, part, ref):
        start = lax.rem(context + 4 - back, 4) * BLOCK + part * (BLOCK // 2)
        rows = ref.shape[0]
        kv_ref[pl.ds(pl.multiple_of(start, BLOCK // 2), rows), :] = ref[...]

    put(0, 0, own_ref)
    put(1, 0, left_ref)
    put(2, 0, far_a_ref)
    put(2, 1, far_b_ref)
    put(3, 0, right_ref)
    left = lane_index((CHUNK, LANES)) < HEAD_DIM
    left_keys = lane_index((tile, LANES)) < HEAD_DIM
    for chunk in range(2):
        whole = 2 * (context if chunk == 0 else 3 - context) + chunk
        queries = (q_far_ref[...] if chunk else q_ref[:8]).reshape(CHUNK, LANES)
        for head in range(2):
            qm_ref[head] = query_of_head(queries, head, left)
            top_ref[head] = jnp.full((CHUNK, LANES), huge_negative, f32)
            acc_ref[head] = jnp.zeros((CHUNK, LANES), f32)

        def step(index, masked):
            keys = kv_ref[pl.ds(pl.multiple_of(index * tile, tile), tile), :]
            values = jnp.where(left_keys, jnp.ones_like(keys), keys)
            for head in range(2):
                for part in range(2):
                    rows = slice(part * 256, part * 256 + 256)
                    s = dot_rows(qm_ref[head, rows], keys)
                    if masked:
                        r = lax.broadcasted_iota(jnp.int32, s.shape, 0) + part * 256
                        place = r + (r // 64) * 64 + half * 64
                        s = jnp.where(lane_index(s.shape) <= place, s, huge_negative)
                    old = top_ref[head, rows]
                    new = jnp.maximum(old, jnp.max(s, axis=1, keepdims=True))
                    p = jnp.exp(s - new[:, :1]).astype(bf16)
                    acc_ref[head, rows] = acc_ref[head, rows] * jnp.exp(old - new) + dot(p, values)
                    top_ref[head, rows] = new

        def visit(index, carry):
            step(index, False)
            return carry

        lax.fori_loop(0, whole, visit, 0)
        step(whole, True)
        outs = []
        for head in range(2):
            acc = acc_ref[head]
            outs.append(pltpu.roll(acc, HEAD_DIM, 1) / acc)
            total = top_ref[head] + jnp.log(jnp.where(left, acc, 1.0))
            lse_ref[2 * chunk + head] = jnp.transpose(total)[0:8]
        o = jnp.where(left, outs[0], pltpu.roll(outs[1], HEAD_DIM, 1))
        o_ref[chunk] = o
        (low_far_ref if chunk else low_ref)[...] = o.astype(bf16).reshape(8, 64, LANES)


def attend_forward(place, q, q_far, kv_parts):
    smem = pl.BlockSpec(memory_space=pltpu.SMEM)
    vmem = pl.BlockSpec(memory_space=pltpu.VMEM)
    return call(
        forward_kernel,
        (
            struct((2, CHUNK, LANES), f32),
            struct((8, 64, LANES), bf16),
            struct((8, 64, LANES), bf16),
            struct((4, 8, CHUNK), f32),
            struct((4 * BLOCK, LANES), bf16),
        ),
        2e10,
        4e6,
        in_specs=[smem] + [vmem] * 7,
        out_specs=(vmem,) * 5,
        scratch_shapes=[
            pltpu.VMEM((2, CHUNK, LANES), bf16),
            pltpu.VMEM((2, CHUNK, LANES), f32),
            pltpu.VMEM((2, CHUNK, LANES), f32),
        ],
        name="attend",
    )(place, q, q_far, *kv_parts)


def backward_kernel(
    place_ref, q_ref, q_far_ref, do_ref, do_far_ref, o_ref, lse_ref, kv_ref,
    dq_ref, dq_far_ref, d0_ref, d1a_ref, d1b_ref, d2a_ref, d2b_ref, d3a_ref, d3b_ref,
    qm_ref, dom_ref, row_ref, dqt_ref, acc_ref,
):
    tile = 512
    context = place_ref[0]
    half = place_ref[1]
    left = lane_index((CHUNK, LANES)) < HEAD_DIM
    acc_ref[...] = jnp.zeros_like(acc_ref)
    for chunk in range(2):
        whole = 2 * (2 * (context if chunk == 0 else 3 - context) + chunk)
        queries = (q_far_ref[...] if chunk else q_ref[:8]).reshape(CHUNK, LANES)
        do = (do_far_ref[...] if chunk else do_ref[:8]).reshape(CHUNK, LANES).astype(f32)
        product = jnp.transpose(do * o_ref[chunk])
        for head in range(2):
            qm_ref[head] = query_of_head(queries, head, left)
            moved = do if head else pltpu.roll(do, HEAD_DIM, 1)
            dom_ref[head] = jnp.where(left, 0.0, moved).astype(bf16)
            dqt_ref[head] = jnp.zeros((LANES, CHUNK), f32)
            rows = product[head * HEAD_DIM : (head + 1) * HEAD_DIM]
            row_ref[head] = jnp.broadcast_to(jnp.sum(rows, axis=0, keepdims=True), (8, CHUNK))

        def step(index, offset):
            span = pl.ds(pl.multiple_of(index * tile, tile), tile)
            keys = kv_ref[span, :]
            for head in range(2):
                qm = qm_ref[head]
                dom = dom_ref[head]
                s = dot_rows(keys, qm)
                dp = dot_rows(keys, dom)
                p = jnp.exp(s - lse_ref[2 * chunk + head, 0:1])
                if offset is not None:
                    r = lane_index(s.shape)
                    place = r + (r // 64) * 64 + half * 64
                    key = lax.broadcasted_iota(jnp.int32, s.shape, 0) + offset
                    p = jnp.where(key <= place, p, 0.0)
                ds = (p * (dp - row_ref[head, 0:1])).astype(bf16)
                acc_ref[span, :] += dot(ds, qm) + dot(p.astype(bf16), dom)
                dqt_ref[head] += dot_down(keys, ds)

        def visit(index, carry):
            step(index, None)
            return carry

        lax.fori_loop(0, whole, visit, 0)
        step(whole, 0)
        step(whole + 1, tile)
        parts = [jnp.transpose(dqt_ref[head]) * score_scale for head in range(2)]
        dq = jnp.where(left, parts[0], pltpu.roll(parts[1], HEAD_DIM, 1)).astype(bf16)
        (dq_far_ref if chunk else dq_ref)[...] = dq.reshape(8, 64, LANES)
    d0_ref[...] = acc_ref[pl.ds(pl.multiple_of(context * BLOCK, BLOCK), BLOCK), :]
    for back, first, second in ((1, d1a_ref, d1b_ref), (2, d2a_ref, d2b_ref), (3, d3a_ref, d3b_ref)):
        start = pl.multiple_of(lax.rem(context + 4 - back, 4) * BLOCK, BLOCK)
        first[...] = acc_ref[pl.ds(start, BLOCK // 2), :].astype(bf16)
        second[...] = acc_ref[pl.ds(pl.multiple_of(start + BLOCK // 2, BLOCK // 2), BLOCK // 2), :].astype(bf16)


def attend_backward(place, q, q_far, do, do_far, o, lse, kv):
    smem = pl.BlockSpec(memory_space=pltpu.SMEM)
    vmem = pl.BlockSpec(memory_space=pltpu.VMEM)
    rows = kv.shape[0]
    return call(
        backward_kernel,
        (struct((8, 64, LANES), bf16), struct((8, 64, LANES), bf16), struct((BLOCK, LANES), f32))
        + (struct((BLOCK // 2, LANES), bf16),) * 6,
        5e10,
        8e6,
        in_specs=[smem] + [vmem] * 7,
        out_specs=(vmem,) * 9,
        scratch_shapes=[
            pltpu.VMEM((2, CHUNK, LANES), bf16),
            pltpu.VMEM((2, CHUNK, LANES), bf16),
            pltpu.VMEM((2, 8, CHUNK), f32),
            pltpu.VMEM((2, LANES, CHUNK), f32),
            pltpu.VMEM((rows, LANES), f32),
        ],
        name="attend_back",
    )(place, q, q_far, do, do_far, o, lse, kv)


def middle_kernel(att_ref, x_ref, wo_ref, gain_ref, pick_ref, hidden_ref, send_ref, attended_ref):
    for j in range(PAIRS):
        for h in range(2):
            attended_ref[h * 64 : h * 64 + 64, j * LANES : (j + 1) * LANES] = att_ref[2 * j + h]
    hidden = x_ref[...].astype(f32) + branch_scale * dot(attended_ref[...], wo_ref[...])
    hidden_ref[...] = hidden
    inverse = lax.rsqrt(jnp.mean(hidden * hidden, axis=-1, keepdims=True) + norm_eps)
    act = (hidden * inverse * gain_ref[...]).astype(bf16)
    send_ref[...] = dot(pick_ref[...], act).astype(bf16)


def middle(att, x, wo, gain, pick):
    return call(
        middle_kernel,
        (struct((TOK, D), f32), struct((SLOTS, D), bf16)),
        2 * TOK * D * (D + SLOTS),
        8e6,
        scratch_shapes=[pltpu.VMEM((TOK, D), bf16)],
        name="middle",
    )(att, x, wo, gain.reshape(1, D), pick)


def raw_kernel(first_ref, top_ref, down_ref, rows_ref, raw_ref):
    number = first_ref[0] + pl.program_id(0)
    chosen = (lane_index((8, LANES)) == number).astype(bf16)
    slot = lax.broadcasted_iota(jnp.int32, (CAP, TOK), 0).astype(f32)
    for n in range(16):
        place = dot_rows(chosen, top_ref[n, :, D:])[0:1]
        rows = dot((slot == place).astype(bf16), top_ref[n, :, :D])
        rows_ref[CAP * n : CAP * n + CAP] = rows.astype(bf16)
    raw_ref[...] = branch_scale * dot_rows(rows_ref[...], down_ref[...])


def raw_grads(first, top, down):
    return call(
        raw_kernel,
        (struct((2, 768, D), bf16), struct((2, 768, F), f32)),
        2 * SLOTS * D * F,
        1.2e7,
        grid=(2,),
        in_specs=[
            pl.BlockSpec(memory_space=pltpu.SMEM),
            pl.BlockSpec((16, TOK, D + LANES), lambda n: (0, 0, 0)),
            owned(F, D),
        ],
        out_specs=(owned(768, D), owned(768, F)),
        name="raw",
    )(first, top, down)


def expert_kernel(
    first_ref, x_ref, raw_ref, gu_ref, wr_ref, back_ref, hidden_ref, mixed_ref, gate_ref, logit_ref, norm_ref
):
    number = first_ref[0] + pl.program_id(0)
    wr = wr_ref[...]
    for part in range(2):
        take = slice(8 * part, 8 * part + 8)
        rows = slice(384 * part, 384 * part + 384)
        x = x_ref[take].reshape(384, D)
        logits = dot(x, wr)
        raised = jnp.exp(logits - jnp.max(logits, axis=-1, keepdims=True))
        probs = raised / jnp.sum(raised, axis=-1, keepdims=True)
        chosen = (lane_index(probs.shape) == number).astype(f32)
        gate_value = jnp.sum(probs * chosen, axis=-1, keepdims=True)
        gate_ref[rows] = gate_value
        pre = dot(x, gu_ref[...])
        raw = raw_ref[rows]
        gate = pre[:, :F]
        up = pre[:, F:]
        sig = 1.0 / (1.0 + jnp.exp(-gate))
        act = gate * sig
        hidden = (act * up).astype(bf16)
        hidden_ref[rows] = hidden
        grad_gate = jnp.sum(hidden.astype(f32) * raw, axis=-1, keepdims=True)
        grad_logits = (gate_value * grad_gate) * (chosen - probs)
        logit_ref[rows] = grad_logits
        raw = raw * gate_value
        mixed_gate = (raw * up * sig * (1.0 + gate * (1.0 - sig))).astype(bf16)
        mixed_up = (raw * act).astype(bf16)
        mixed_ref[rows, :F] = mixed_gate
        mixed_ref[rows, F:] = mixed_up
        hi, lo = split2(grad_logits)
        back = dot_rows(mixed_gate, gu_ref[:, :F]) + dot_rows(mixed_up, gu_ref[:, F:])
        back = back + dot_rows(hi, wr) + dot_rows(lo, wr)
        back_ref[take] = back.astype(bf16).reshape(8, CAP, D)
        product = jnp.sum(back * x.astype(f32), axis=0, keepdims=True)
        if part == 0:
            norm_ref[...] = jnp.broadcast_to(product, (8, D))
        else:
            norm_ref[...] += product


def owned(*shape):
    return pl.BlockSpec((None, *shape), lambda n: (n, *([0] * len(shape))))


def experts(first, x, raw, gate_up, wr):
    per = pl.BlockSpec((16, None, CAP, D), lambda n: (0, n, 0, 0))
    return call(
        expert_kernel,
        (
            struct((16, 2, CAP, D), bf16),
            struct((2, 768, F), bf16),
            struct((2, 768, D), bf16),
            struct((2, 768, 1), f32),
            struct((2, 768, EXPERTS), f32),
            struct((2, 8, D), f32),
        ),
        2 * SLOTS * D * 2560,
        2e7,
        grid=(2,),
        in_specs=[
            pl.BlockSpec(memory_space=pltpu.SMEM),
            per,
            owned(768, F),
            owned(D, D),
            pl.BlockSpec((D, EXPERTS), lambda n: (0, 0)),
        ],
        out_specs=(per, owned(768, F), owned(768, D), owned(768, 1), owned(768, EXPERTS), owned(8, D)),
        name="experts",
    )(first, x, raw, gate_up, wr)


def expert_grads_kernel(
    x_ref, top_ref, gate_ref, logit_ref, hidden_ref, mixed_ref, down_ref, out_ref, dgu_ref, ddown_ref, router_ref
):
    hidden = hidden_ref[...]
    gate = gate_ref[...]
    x = x_ref[...].reshape(768, D)
    out_ref[...] = (gate * dot(hidden, down_ref[...])).astype(bf16).reshape(16, CAP, D)
    top = (branch_scale * gate * top_ref[...].astype(f32)).astype(bf16)
    ddown_ref[...] = dot_down(hidden, top).astype(bf16)
    dgu_ref[...] = dot_down(x, mixed_ref[...]).astype(bf16)
    hi, lo = split2(logit_ref[...])
    router_ref[...] = dot_down(hi, x) + dot_down(lo, x)


def expert_grads(x, top, gate, logits, hidden, mixed, down):
    per = pl.BlockSpec((16, None, CAP, D), lambda n: (0, n, 0, 0))
    return call(
        expert_grads_kernel,
        (
            struct((16, 2, CAP, D), bf16),
            struct((2, D, D), bf16),
            struct((2, F, D), bf16),
            struct((2, EXPERTS, D), f32),
        ),
        2 * SLOTS * D * 2048,
        2.4e7,
        grid=(2,),
        in_specs=[per, owned(768, D), owned(768, 1), owned(768, EXPERTS), owned(768, F), owned(768, D), owned(F, D)],
        out_specs=(per, owned(D, D), owned(F, D), owned(EXPERTS, D)),
        name="expert_grads",
    )(x, top, gate, logits, hidden, mixed, down)


def turn_back_kernel(
    back_ref, spot_ref, hidden_ref, gain_ref, top_ref, wo_ref, state_ref, attn_ref, send_ref
):
    grad = dot(spot_ref[...], back_ref[...])
    hidden = hidden_ref[...]
    inverse = lax.rsqrt(jnp.mean(hidden * hidden, axis=-1, keepdims=True) + norm_eps)
    normed = hidden * inverse
    scaled = grad * gain_ref[...]
    state = top_ref[...].astype(f32) + inverse * (scaled - normed * jnp.mean(scaled * normed, axis=-1, keepdims=True))
    state_ref[...] = state
    attn = (branch_scale * state).astype(bf16)
    attn_ref[...] = attn
    attended = dot_rows(attn, wo_ref[...]).astype(bf16)
    for j in range(PAIRS):
        for h in range(2):
            send_ref[2 * j + h] = attended[h * 64 : h * 64 + 64, j * LANES : (j + 1) * LANES]


def turn_back(back, spot, hidden, gain, top, wo):
    return call(
        turn_back_kernel,
        (
            struct((TOK, D), f32),
            struct((TOK, D), bf16),
            struct((16, TOK // 2, LANES), bf16),
        ),
        2 * 256 * D * (D + SLOTS),
        8e6,
        name="turn_back",
    )(back, spot, hidden, gain.reshape(1, D), top, wo)


def unturn(v, cos, sin, first):
    scaled = v * sin
    return v * cos + jnp.where(first, pltpu.roll(scaled, LANES - 32, 1), pltpu.roll(scaled, 32, 1))


def merge_kernel(
    place_ref, d0_ref, left_a_ref, left_b_ref, right_a_ref, right_b_ref, keep_ref, give_ref, sum_ref
):
    half = place_ref[1]
    for part, left, right in ((0, left_a_ref, right_a_ref), (1, left_b_ref, right_b_ref)):
        rows = slice(part * 1024, part * 1024 + 1024)
        total = d0_ref[rows] + left[...].astype(f32) + right[...].astype(f32)
        sum_ref[8 * part : 8 * part + 8] = total.reshape(8, TOK, LANES)
    keep_ref[...] = sum_ref[:, pl.ds(pl.multiple_of(half * 64, 64), 64), :]
    give_ref[...] = sum_ref[:, pl.ds(pl.multiple_of((1 - half) * 64, 64), 64), :].astype(bf16)


def merge(place, *pieces):
    smem = pl.BlockSpec(memory_space=pltpu.SMEM)
    vmem = pl.BlockSpec(memory_space=pltpu.VMEM)
    return call(
        merge_kernel,
        (struct((16, 64, LANES), f32), struct((16, 64, LANES), bf16)),
        1e6,
        3e6,
        in_specs=[smem] + [vmem] * 5,
        out_specs=(vmem, vmem),
        scratch_shapes=[pltpu.VMEM((16, TOK, LANES), f32)],
        name="merge",
    )(place, *pieces)


def unturn_kernel(dq_ref, dq_far_ref, keep_ref, got_ref, cos_ref, sin_ref, grads_ref):
    lane = lane_index((512, LANES))
    first = lane % HEAD_DIM < HEAD_DIM // 2
    for part, dq in ((0, dq_ref), (1, dq_far_ref)):
        rows = slice(512 * part, 512 * part + 512)
        take = slice(8 * part, 8 * part + 8)
        cos = cos_ref[rows]
        sin = sin_ref[rows]
        grads_ref[rows, :LANES] = unturn(dq[...].reshape(512, LANES).astype(f32), cos, sin, first).astype(bf16)
        both = (keep_ref[take] + got_ref[take].astype(f32)).reshape(512, LANES).astype(bf16).astype(f32)
        grads_ref[rows, LANES:] = jnp.where(lane < HEAD_DIM, unturn(both, cos, sin, first), both).astype(bf16)


def unturn_rows(dq, dq_far, keep, got, cos, sin):
    return call(unturn_kernel, struct((1024, 256), bf16), 1e6, 3e6, name="unturn")(dq, dq_far, keep, got, cos, sin)


def head_kernel(place_ref, act_ref, attn_ref, o_ref, grads_ref, extra_ref, mine_ref, other_ref, all_ref):
    grads = dot_down(act_ref[...], grads_ref[...]).astype(bf16)
    out = dot_down(o_ref[...], attn_ref[...].reshape(1024, D)).astype(bf16)
    for quarter in range(4):
        start = 384 * quarter
        all_ref[start : start + 256] = grads[256 * quarter : 256 * quarter + 256]
        all_ref[start + 256 : start + 384] = out[:, 256 * quarter : 256 * quarter + 256]
    extra = extra_ref[0].astype(f32)
    for e in range(1, 16):
        extra = extra + extra_ref[e].astype(f32)
    packed = extra[:, :256]
    for b in range(1, 4):
        packed = packed + pltpu.roll(extra[:, 256 * b : 256 * (b + 1)], 4 * b, 0)
    packed = packed.astype(bf16)
    core = place_ref[2]
    for which, out_ref in ((1 - core, other_ref), (core, mine_ref)):
        out_ref[:768] = all_ref[pl.ds(pl.multiple_of(which * 768, 768), 768), :]
        out_ref[768:] = packed


def head_grads(place, act, attn, o, grads, returned):
    whole = lambda *shape: pl.BlockSpec(shape, lambda i, place: (0,) * len(shape))
    half = struct((784, 256), bf16)
    return call(
        head_kernel,
        (half, half),
        2 * 1024 * 1024 * 512,
        8e6,
        grid_spec=pltpu.PrefetchScalarGridSpec(
            num_scalar_prefetch=1,
            grid=(1,),
            in_specs=[
                whole(1024, D),
                pl.BlockSpec((16, None, 64, D), lambda i, place: (0, place[1], 0, 0)),
                whole(1024, LANES),
                whole(1024, 256),
                pl.BlockSpec((16, None, 16, D), lambda i, place: (0, 6, 0, 0)),
            ],
            out_specs=(whole(784, 256), whole(784, 256)),
            scratch_shapes=[pltpu.VMEM((1536, 256), bf16)],
        ),
        name="head_grads",
    )(place, act, attn, o, grads, returned)


def split_kernel(place_ref, mine_ref, other_ref, keep_ref, give_ref):
    half = place_ref[1]
    rows = pl.ds(pl.multiple_of(half * 384, 384), 384)
    keep_ref[:384] = mine_ref[rows, :].astype(f32) + other_ref[rows, :].astype(f32)
    keep_ref[384:] = mine_ref[768:, :].astype(f32) + other_ref[768:, :].astype(f32)
    rows = pl.ds(pl.multiple_of((1 - half) * 384, 384), 384)
    give_ref[...] = (mine_ref[rows, :].astype(f32) + other_ref[rows, :].astype(f32)).astype(bf16)


def split_halves(place, mine, other):
    smem = pl.BlockSpec(memory_space=pltpu.SMEM)
    vmem = pl.BlockSpec(memory_space=pltpu.VMEM)
    return call(
        split_kernel,
        (struct((400, 256), f32), struct((384, 256), bf16)),
        1e6,
        2e6,
        in_specs=[smem, vmem, vmem],
        out_specs=(vmem, vmem),
        name="split",
    )(place, mine, other)


def finish_kernel(grads_ref, x_ref, gain_ref, wq_ref, wk_ref, wv_ref, state_ref, out_ref, flat_ref):
    left = lane_index((TOK // 2, LANES)) < HEAD_DIM
    for h in range(2):
        rows = slice(64 * h, 64 * h + 64)
        for j in range(PAIRS):
            flat_ref[rows, j * LANES : (j + 1) * LANES] = grads_ref[2 * j + h, :, :LANES]
        for b in range(PAIRS // 2):
            even = grads_ref[4 * b + h, :, LANES:].astype(f32)
            odd = grads_ref[4 * b + 2 + h, :, LANES:].astype(f32)
            k = jnp.where(left, even, pltpu.roll(odd, HEAD_DIM, 1))
            v = jnp.where(left, pltpu.roll(even, HEAD_DIM, 1), odd)
            flat_ref[rows, D + b * LANES : D + (b + 1) * LANES] = k.astype(bf16)
            flat_ref[rows, D + 512 + b * LANES : D + 512 + (b + 1) * LANES] = v.astype(bf16)
    grad = dot_rows(flat_ref[:, :D], wq_ref[...])
    grad = grad + dot_rows(flat_ref[:, D : D + 512], wk_ref[...])
    grad = grad + dot_rows(flat_ref[:, D + 512 :], wv_ref[...])
    x = x_ref[...].astype(f32)
    inverse = lax.rsqrt(jnp.mean(x * x, axis=-1, keepdims=True) + norm_eps)
    normed = x * inverse
    scaled = grad * gain_ref[...]
    out_ref[...] = state_ref[...] + inverse * (scaled - normed * jnp.mean(scaled * normed, axis=-1, keepdims=True))


def finish(grads, x, gain, wq, wk, wv, state):
    return call(
        finish_kernel,
        struct((TOK, D), f32),
        2 * 256 * D * 2048,
        8e6,
        scratch_shapes=[pltpu.VMEM((TOK, 2048), bf16)],
        name="finish",
    )(grads, x, gain.reshape(1, D), wq, wk, wv, state)


def assemble_kernel(
    place_ref, own_ref, other_ref, wq_ref, wk_ref, wv_ref, gain_ref, q_ref, k_ref, v_ref, o_ref, norm_ref
):
    left = lane_index((256, LANES)) < HEAD_DIM

    def write(piece):
        total = jnp.zeros((256, LANES), f32)
        for j in range(PAIRS):
            lanes = slice(j * LANES, (j + 1) * LANES)
            value = piece[j, :256, :LANES].astype(f32)
            q_ref[:, lanes] = value
            total = total + value * wq_ref[:, lanes].astype(f32)
            o_ref[lanes, :] = piece[j, 256:384, :].astype(f32)
        for b in range(PAIRS // 2):
            lanes = slice(b * LANES, (b + 1) * LANES)
            even = piece[2 * b, :256, LANES:].astype(f32)
            odd = piece[2 * b + 1, :256, LANES:].astype(f32)
            k = jnp.where(left, even, pltpu.roll(odd, HEAD_DIM, 1))
            v = jnp.where(left, pltpu.roll(even, HEAD_DIM, 1), odd)
            k_ref[:, lanes] = k
            v_ref[:, lanes] = v
            total = total + k * wk_ref[:, lanes].astype(f32) + v * wv_ref[:, lanes].astype(f32)
        norm_ref[...] = jnp.sum(jnp.transpose(total), axis=0, keepdims=True) / gain_ref[...]

    @pl.when(pl.program_id(0) < 2)
    def _():
        write(own_ref)

    @pl.when(pl.program_id(0) >= 2)
    def _():
        write(other_ref)


def assemble(place, own, other, wq, wk, wv, gain):
    def quarter(i, place):
        return 2 * jnp.where(i < 2, place[2], 1 - place[2]) + i % 2

    rows = lambda width: pl.BlockSpec((256, width), lambda i, place: (quarter(i, place), 0))
    columns = lambda height: pl.BlockSpec((height, 256), lambda i, place: (0, quarter(i, place)))
    piece = (PAIRS, None, 400, 256)
    return call(
        assemble_kernel,
        (
            struct((D, D), f32),
            struct((D, 512), f32),
            struct((D, 512), f32),
            struct((D, D), f32),
            struct((1, D), f32),
        ),
        1e6,
        2.2e7,
        grid_spec=pltpu.PrefetchScalarGridSpec(
            num_scalar_prefetch=1,
            grid=(4,),
            in_specs=[
                pl.BlockSpec(piece, lambda i, place: (0, jnp.minimum(i, 1), 0, 0)),
                pl.BlockSpec(piece, lambda i, place: (0, jnp.maximum(i - 2, 0), 0, 0)),
                rows(D),
                rows(512),
                rows(512),
                columns(1),
            ],
            out_specs=(rows(D), rows(512), rows(512), columns(D), columns(1)),
        ),
        name="assemble",
    )(place, own.reshape(PAIRS, 2, 400, 256), other.reshape(PAIRS, 2, 400, 256), wq, wk, wv, gain.reshape(1, D))


def spread_kernel(a_ref, b_ref, out_ref):
    total = (a_ref[...].astype(f32) + b_ref[...].astype(f32)).astype(bf16)
    for e in range(16):
        out_ref[e] = total


def add_and_spread(a, b):
    return call(spread_kernel, struct((16, 400, 256), bf16), 1e6, 4e6, name="spread")(a, b)


def after(x, *earlier):
    return lax.optimization_barrier((x, *earlier))[0]


def to_owners(x):
    return lax.all_to_all(x, "expert", split_axis=0, concat_axis=0, tiled=True)


def mirror(x):
    return lax.ppermute(x, "context", [(0, 3), (1, 2), (2, 1), (3, 0)])


def swap_cores(x):
    return lax.ppermute(x, "dp", [(0, 1), (1, 0)])


def shift(x, by):
    return lax.ppermute(x, "context", [(i, (i + by) % 4) for i in range(4)])


def neighbour(x):
    return lax.ppermute(x, "context", [(0, 1), (1, 0), (2, 3), (3, 2)])


def swap_halves(x):
    return lax.ppermute(x, "expert", [(i, i ^ 1) for i in range(16)])


def pick(x, index, axis=0):
    return lax.dynamic_index_in_dim(x, index, axis, False)


def rope_tables(positions):
    frequency = rope_base ** (-jnp.arange(0, HEAD_DIM, 2, dtype=f32) / HEAD_DIM)
    angles = positions.astype(f32)[:, None] * frequency[None, :]
    cos, sin = jnp.cos(angles), jnp.sin(angles)
    return jnp.concatenate([cos] * 4, -1), jnp.concatenate([-sin, sin] * 2, -1)


def local(
    layer_input, grad_output, norm1_gain, norm2_gain, w_query, w_key, w_value, w_out, w_router, w_gate_up, w_down, routes
):
    context = lax.axis_index("context")
    expert = lax.axis_index("expert")
    x = layer_input[0, 0]
    top = grad_output[0, 0]

    half = expert % 2

    cos, sin = rope_tables(context * BLOCK + expert * TOK + jnp.arange(TOK, dtype=jnp.int32))
    order = jnp.arange(1024, dtype=jnp.int32)
    half_cos, half_sin = rope_tables(context * BLOCK + order + (order // 64) * 64 + half * 64)

    hits = jnp.sum((routes[0, 0][:, :, None] == jnp.arange(EXPERTS, dtype=jnp.int32)).astype(f32), 1)
    lower = np.tril(np.ones((TOK, TOK), np.float32), -1)
    place = dot(jnp.asarray(lower, bf16), hits.astype(bf16))
    owner = np.repeat(np.eye(EXPERTS, dtype=np.float32), CAP, 0)
    owner16 = jnp.asarray(owner, bf16)
    slot_number = jnp.arange(SLOTS, dtype=jnp.int32) % CAP
    marked = jnp.where(hits > 0.5, place, 255.0).astype(bf16)
    spot = (dot_rows(marked, owner16) == slot_number[None, :].astype(f32)).astype(bf16)
    selector = (dot_rows(owner16, marked) == slot_number[:, None].astype(f32)).astype(bf16)

    act_send, q_send, kv_send = project(x, norm1_gain, w_query, w_key, w_value, cos, sin)
    kv_own = to_owners(kv_send).reshape(BLOCK, LANES)
    kv_left, kv_right = shift(kv_own, 1), shift(kv_own, 3)
    q_own = to_owners(after(q_send, kv_own))
    q_far = mirror(q_own[8:])
    far_a, far_b = shift(kv_left[: BLOCK // 2], 1), shift(kv_right[BLOCK // 2 :], 3)

    down = lax.all_gather(w_down, ("context", "dp"), axis=1, tiled=True)
    wide = jnp.concatenate([top, jnp.pad(marked, ((0, 0), (0, LANES - EXPERTS)))], 1)
    top_all = lax.all_gather(after(wide, down), "expert", axis=0, tiled=True)
    gate_up = lax.all_gather(after(w_gate_up, top_all), ("context", "dp"), axis=1, tiled=True)
    act_rows = to_owners(after(act_send, q_far, far_a, far_b)).reshape(1024, D)

    seat = jnp.stack([context, half, lax.axis_index("dp")]).astype(jnp.int32)
    o, o_low, o_far, lse, kv = attend_forward(
        seat, q_own, q_far, (kv_own, kv_left, far_a, far_b, kv_right)
    )
    o_far = after(o_far, act_rows)
    o_own = jnp.concatenate([o_low, mirror(o_far)], 0)
    att = to_owners(o_own)
    first = (2 * expert).astype(jnp.int32).reshape(1)
    top_rows, raw = raw_grads(first, top_all.reshape(16, TOK, D + LANES), down)
    att = after(att, raw)

    hidden, send = middle(att, x, w_out, norm2_gain, selector)
    rows = to_owners(send.reshape(16, 2, CAP, D))
    grad_rows, expert_hidden, mixed, gates, logits, norm2_sum = experts(first, rows, raw, gate_up, w_router)
    back = to_owners(grad_rows)
    out_rows, dgu, ddown, router_grad = expert_grads(rows, top_rows, gates, logits, expert_hidden, mixed, down)
    back = after(back, dgu)

    state, attn, do_send = turn_back(
        back.reshape(SLOTS, D), spot, hidden, norm2_gain, top, w_out
    )
    do_own = to_owners(do_send)
    do_far = mirror(do_own[8:])
    attn_all = lax.all_gather(attn, "expert", axis=0, tiled=True)
    norm2_row = (norm2_sum[0, :1] + norm2_sum[1, :1]) / norm2_gain[None]
    extra = jnp.concatenate([router_grad[0] + router_grad[1], norm2_row, jnp.zeros((31, D), f32)], 0)
    extra = jnp.pad(extra.reshape(16, 4, D), ((0, 0), (0, 12), (0, 0))).astype(bf16)
    out_send = jnp.concatenate([out_rows.reshape(16, 96, D), extra], 1)
    returned = to_owners(after(out_send, do_own))
    grad_gate_up = lax.psum_scatter(
        after(dgu, attn_all), ("context", "dp"), scatter_dimension=1, tiled=True
    ).astype(f32)

    dq, dq_far, d0, d1a, d1b, d2a, d2b, d3a, d3b = attend_backward(seat, q_own, q_far, do_own, do_far, o, lse, kv)

    far_a, far_b = shift(d2a, 1), shift(d2b, 3)
    from_left_b, from_right_a = shift(d3b, 1), shift(d1a, 3)
    dq_far = mirror(after(dq_far, far_a, far_b))
    from_left_a = shift((d3a.astype(f32) + far_a.astype(f32)).astype(bf16), 1)
    from_right_b = shift((d1b.astype(f32) + far_b.astype(f32)).astype(bf16), 3)
    keep, give = merge(seat, after(d0, returned), from_left_a, from_left_b, from_right_a, from_right_b)
    got = swap_halves(give)
    grads = unturn_rows(dq, dq_far, keep, got, half_cos, half_sin)
    mine, other = head_grads(
        seat,
        act_rows,
        attn_all.reshape(16, 2, 64, D),
        o_own.reshape(1024, LANES),
        grads,
        returned.reshape(16, 7, 16, D),
    )
    keep, give = split_halves(seat, mine, swap_cores(other))
    grads_back = to_owners(grads.reshape(16, 64, 256))
    total = keep + jnp.pad(swap_halves(give), ((0, 16), (0, 0))).astype(f32)
    total = total.astype(bf16)
    total = (total.astype(f32) + neighbour(total).astype(f32)).astype(bf16)
    block = after(add_and_spread(total, mirror(total)), grads_back)
    whole = to_owners(block)

    grad_input = finish(grads_back, x, norm1_gain, w_query, w_key, w_value, state)
    block_out = hidden + branch_scale * dot(spot, returned[:, :96].reshape(SLOTS, D))
    grad_down = lax.psum_scatter(after(ddown, grad_gate_up), ("context", "dp"), scatter_dimension=1, tiled=True).astype(f32)
    whole, grad_input, block_out, grad_gate_up = lax.optimization_barrier(
        (whole, grad_input, block_out, grad_gate_up)
    )
    dwq, dwk, dwv, dwo, norm1_grad = assemble(
        seat, whole, swap_cores(whole), w_query, w_key, w_value, norm1_gain
    )
    small = whole[:, 384:].reshape(16, 4, 4, 256).transpose(0, 2, 1, 3).reshape(64, D).astype(f32)
    return (
        block_out.reshape(1, 1, TOK, D),
        grad_input.reshape(1, 1, TOK, D),
        norm1_grad[0],
        small[EXPERTS],
        dwq,
        dwk,
        dwv,
        dwo,
        small[:EXPERTS].T,
        grad_gate_up,
        grad_down,
    )


def solution(mesh):
    tokens = P("dp", "context", "expert", None)
    weights = P("expert", ("context", "dp"), None)
    return jax.shard_map(
        local,
        mesh=mesh,
        in_specs=(tokens, tokens, P(), P(), P(), P(), P(), P(), P(), weights, weights, tokens),
        out_specs=(tokens, tokens, P(), P(), P(), P(), P(), P(), P(), weights, weights),
        check_vma=False,
    )
```

```python
import jax
import jax.numpy as jnp
import numpy as np
from jax import lax
from jax.experimental import pallas as pl
from jax.experimental.pallas import tpu as pltpu
from jax.sharding import PartitionSpec as P

D = 1024
HEAD_DIM = 64
F = 512
EXPERTS = 32
CAP = 48
TOK = 128
BLOCK = 2048
LANES = 128
SLOTS = EXPERTS * CAP
PAIRS = 8
CHUNK = 512

norm_eps = 1e-06
score_scale = 0.015625
branch_scale = 0.22
rope_base = 10000.0
huge_negative = -1e30
bf16 = jnp.bfloat16
f32 = jnp.float32
VMEM_LIMIT = 56 * 1024 * 1024


def call(kernel, out_shape, flops, moved, **kw):
    return pl.pallas_call(
        kernel,
        out_shape=out_shape,
        compiler_params=pltpu.CompilerParams(vmem_limit_bytes=VMEM_LIMIT),
        cost_estimate=pl.CostEstimate(flops=int(flops), bytes_accessed=int(moved), transcendentals=0),
        **kw,
    )


def struct(shape, dtype):
    return jax.ShapeDtypeStruct(shape, dtype)


def dot(a, b):
    return jnp.dot(a, b, preferred_element_type=f32)


def dot_rows(a, b):
    return lax.dot_general(a, b, (((1,), (1,)), ((), ())), preferred_element_type=f32)


def dot_down(a, b):
    return lax.dot_general(a, b, (((0,), (0,)), ((), ())), preferred_element_type=f32)


def split2(x):
    hi = x.astype(bf16)
    return hi, (x - hi.astype(f32)).astype(bf16)


def lane_index(shape):
    return lax.broadcasted_iota(jnp.int32, shape, len(shape) - 1)


def project_kernel(x_ref, gain_ref, wq_ref, wk_ref, wv_ref, cos_ref, sin_ref, act_ref, q_ref, kv_ref):
    x = x_ref[...].astype(f32)
    inverse = lax.rsqrt(jnp.mean(x * x, axis=-1, keepdims=True) + norm_eps)
    act = (x * inverse * gain_ref[...]).astype(bf16)
    for e in range(16):
        act_ref[e] = act[64 * (e % 2) : 64 * (e % 2) + 64]
    cos = cos_ref[...]
    sin = sin_ref[...]
    lane = lane_index((TOK, LANES))
    first = lane % HEAD_DIM < HEAD_DIM // 2
    left = lane < HEAD_DIM

    def turn(v):
        moved = jnp.where(first, pltpu.roll(v, LANES - 32, 1), pltpu.roll(v, 32, 1))
        return v * cos + moved * sin

    q = dot(act, wq_ref[...])
    for j in range(PAIRS):
        rows = turn(q[:, j * LANES : (j + 1) * LANES]).astype(bf16)
        q_ref[2 * j] = rows[: TOK // 2]
        q_ref[2 * j + 1] = rows[TOK // 2 :]
    k = dot(act, wk_ref[...])
    v = dot(act, wv_ref[...])
    for b in range(PAIRS // 2):
        kb = turn(k[:, b * LANES : (b + 1) * LANES])
        vb = v[:, b * LANES : (b + 1) * LANES]
        even = jnp.where(left, kb, pltpu.roll(vb, HEAD_DIM, 1)).astype(bf16)
        odd = jnp.where(left, pltpu.roll(kb, HEAD_DIM, 1), vb).astype(bf16)
        kv_ref[4 * b] = even
        kv_ref[4 * b + 1] = even
        kv_ref[4 * b + 2] = odd
        kv_ref[4 * b + 3] = odd


def project(x, gain, wq, wk, wv, cos, sin):
    return call(
        project_kernel,
        (struct((16, 64, D), bf16), struct((16, 64, LANES), bf16), struct((16, TOK, LANES), bf16)),
        2 * TOK * D * 2048,
        6e6,
        name="project",
    )(x, gain.reshape(1, D), wq, wk, wv, cos, sin)


def query_of_head(q, head, left):
    q = q.astype(f32) * score_scale
    if head:
        q = pltpu.roll(q, HEAD_DIM, 1)
    return jnp.where(left, q, 0.0).astype(bf16)


def forward_kernel(
    place_ref, q_ref, q_far_ref, own_ref, left_ref, far_a_ref, far_b_ref, right_ref,
    o_ref, low_ref, low_far_ref, lse_ref, kv_ref, qm_ref, top_ref, acc_ref,
):
    tile = 1024
    context = place_ref[0]
    half = place_ref[1]

    def put(back, part, ref):
        start = lax.rem(context + 4 - back, 4) * BLOCK + part * (BLOCK // 2)
        rows = ref.shape[0]
        kv_ref[pl.ds(pl.multiple_of(start, BLOCK // 2), rows), :] = ref[...]

    put(0, 0, own_ref)
    put(1, 0, left_ref)
    put(2, 0, far_a_ref)
    put(2, 1, far_b_ref)
    put(3, 0, right_ref)
    left = lane_index((CHUNK, LANES)) < HEAD_DIM
    left_keys = lane_index((tile, LANES)) < HEAD_DIM
    for chunk in range(2):
        whole = 2 * (context if chunk == 0 else 3 - context) + chunk
        queries = (q_far_ref[...] if chunk else q_ref[:8]).reshape(CHUNK, LANES)
        for head in range(2):
            qm_ref[head] = query_of_head(queries, head, left)
            top_ref[head] = jnp.full((CHUNK, LANES), huge_negative, f32)
            acc_ref[head] = jnp.zeros((CHUNK, LANES), f32)

        def step(index, masked):
            keys = kv_ref[pl.ds(pl.multiple_of(index * tile, tile), tile), :]
            values = jnp.where(left_keys, jnp.ones_like(keys), keys)
            for head in range(2):
                for part in range(2):
                    rows = slice(part * 256, part * 256 + 256)
                    s = dot_rows(qm_ref[head, rows], keys)
                    if masked:
                        r = lax.broadcasted_iota(jnp.int32, s.shape, 0) + part * 256
                        place = r + (r // 64) * 64 + half * 64
                        s = jnp.where(lane_index(s.shape) <= place, s, huge_negative)
                    old = top_ref[head, rows]
                    new = jnp.maximum(old, jnp.max(s, axis=1, keepdims=True))
                    p = jnp.exp(s - new[:, :1]).astype(bf16)
                    acc_ref[head, rows] = acc_ref[head, rows] * jnp.exp(old - new) + dot(p, values)
                    top_ref[head, rows] = new

        def visit(index, carry):
            step(index, False)
            return carry

        lax.fori_loop(0, whole, visit, 0)
        step(whole, True)
        outs = []
        for head in range(2):
            acc = acc_ref[head]
            outs.append(pltpu.roll(acc, HEAD_DIM, 1) / acc)
            total = top_ref[head] + jnp.log(jnp.where(left, acc, 1.0))
            lse_ref[2 * chunk + head] = jnp.transpose(total)[0:8]
        o = jnp.where(left, outs[0], pltpu.roll(outs[1], HEAD_DIM, 1))
        o_ref[chunk] = o
        (low_far_ref if chunk else low_ref)[...] = o.astype(bf16).reshape(8, 64, LANES)


def attend_forward(place, q, q_far, kv_parts):
    smem = pl.BlockSpec(memory_space=pltpu.SMEM)
    vmem = pl.BlockSpec(memory_space=pltpu.VMEM)
    return call(
        forward_kernel,
        (
            struct((2, CHUNK, LANES), f32),
            struct((8, 64, LANES), bf16),
            struct((8, 64, LANES), bf16),
            struct((4, 8, CHUNK), f32),
            struct((4 * BLOCK, LANES), bf16),
        ),
        2e10,
        4e6,
        in_specs=[smem] + [vmem] * 7,
        out_specs=(vmem,) * 5,
        scratch_shapes=[
            pltpu.VMEM((2, CHUNK, LANES), bf16),
            pltpu.VMEM((2, CHUNK, LANES), f32),
            pltpu.VMEM((2, CHUNK, LANES), f32),
        ],
        name="attend",
    )(place, q, q_far, *kv_parts)


def backward_kernel(
    place_ref, q_ref, q_far_ref, do_ref, do_far_ref, o_ref, lse_ref, kv_ref,
    dq_ref, dq_far_ref, d0_ref, d1a_ref, d1b_ref, d2a_ref, d2b_ref, d3a_ref, d3b_ref,
    qm_ref, dom_ref, row_ref, dqt_ref, acc_ref,
):
    tile = 512
    context = place_ref[0]
    half = place_ref[1]
    left = lane_index((CHUNK, LANES)) < HEAD_DIM
    acc_ref[...] = jnp.zeros_like(acc_ref)
    for chunk in range(2):
        whole = 2 * (2 * (context if chunk == 0 else 3 - context) + chunk)
        queries = (q_far_ref[...] if chunk else q_ref[:8]).reshape(CHUNK, LANES)
        do = (do_far_ref[...] if chunk else do_ref[:8]).reshape(CHUNK, LANES).astype(f32)
        product = jnp.transpose(do * o_ref[chunk])
        for head in range(2):
            qm_ref[head] = query_of_head(queries, head, left)
            moved = do if head else pltpu.roll(do, HEAD_DIM, 1)
            dom_ref[head] = jnp.where(left, 0.0, moved).astype(bf16)
            dqt_ref[head] = jnp.zeros((LANES, CHUNK), f32)
            rows = product[head * HEAD_DIM : (head + 1) * HEAD_DIM]
            row_ref[head] = jnp.broadcast_to(jnp.sum(rows, axis=0, keepdims=True), (8, CHUNK))

        def step(index, offset):
            span = pl.ds(pl.multiple_of(index * tile, tile), tile)
            keys = kv_ref[span, :]
            for head in range(2):
                qm = qm_ref[head]
                dom = dom_ref[head]
                s = dot_rows(keys, qm)
                dp = dot_rows(keys, dom)
                p = jnp.exp(s - lse_ref[2 * chunk + head, 0:1])
                if offset is not None:
                    r = lane_index(s.shape)
                    place = r + (r // 64) * 64 + half * 64
                    key = lax.broadcasted_iota(jnp.int32, s.shape, 0) + offset
                    p = jnp.where(key <= place, p, 0.0)
                ds = (p * (dp - row_ref[head, 0:1])).astype(bf16)
                acc_ref[span, :] += dot(ds, qm) + dot(p.astype(bf16), dom)
                dqt_ref[head] += dot_down(keys, ds)

        def visit(index, carry):
            step(index, None)
            return carry

        lax.fori_loop(0, whole, visit, 0)
        step(whole, 0)
        step(whole + 1, tile)
        parts = [jnp.transpose(dqt_ref[head]) * score_scale for head in range(2)]
        dq = jnp.where(left, parts[0], pltpu.roll(parts[1], HEAD_DIM, 1)).astype(bf16)
        (dq_far_ref if chunk else dq_ref)[...] = dq.reshape(8, 64, LANES)
    d0_ref[...] = acc_ref[pl.ds(pl.multiple_of(context * BLOCK, BLOCK), BLOCK), :]
    for back, first, second in ((1, d1a_ref, d1b_ref), (2, d2a_ref, d2b_ref), (3, d3a_ref, d3b_ref)):
        start = pl.multiple_of(lax.rem(context + 4 - back, 4) * BLOCK, BLOCK)
        first[...] = acc_ref[pl.ds(start, BLOCK // 2), :].astype(bf16)
        second[...] = acc_ref[pl.ds(pl.multiple_of(start + BLOCK // 2, BLOCK // 2), BLOCK // 2), :].astype(bf16)


def attend_backward(place, q, q_far, do, do_far, o, lse, kv):
    smem = pl.BlockSpec(memory_space=pltpu.SMEM)
    vmem = pl.BlockSpec(memory_space=pltpu.VMEM)
    rows = kv.shape[0]
    return call(
        backward_kernel,
        (struct((8, 64, LANES), bf16), struct((8, 64, LANES), bf16), struct((BLOCK, LANES), f32))
        + (struct((BLOCK // 2, LANES), bf16),) * 6,
        5e10,
        8e6,
        in_specs=[smem] + [vmem] * 7,
        out_specs=(vmem,) * 9,
        scratch_shapes=[
            pltpu.VMEM((2, CHUNK, LANES), bf16),
            pltpu.VMEM((2, CHUNK, LANES), bf16),
            pltpu.VMEM((2, 8, CHUNK), f32),
            pltpu.VMEM((2, LANES, CHUNK), f32),
            pltpu.VMEM((rows, LANES), f32),
        ],
        name="attend_back",
    )(place, q, q_far, do, do_far, o, lse, kv)


def middle_kernel(att_ref, x_ref, wo_ref, gain_ref, pick_ref, hidden_ref, send_ref, attended_ref):
    for j in range(PAIRS):
        for h in range(2):
            attended_ref[h * 64 : h * 64 + 64, j * LANES : (j + 1) * LANES] = att_ref[2 * j + h]
    hidden = x_ref[...].astype(f32) + branch_scale * dot(attended_ref[...], wo_ref[...])
    hidden_ref[...] = hidden
    inverse = lax.rsqrt(jnp.mean(hidden * hidden, axis=-1, keepdims=True) + norm_eps)
    act = (hidden * inverse * gain_ref[...]).astype(bf16)
    send_ref[...] = dot(pick_ref[...], act).astype(bf16)


def middle(att, x, wo, gain, pick):
    return call(
        middle_kernel,
        (struct((TOK, D), f32), struct((SLOTS, D), bf16)),
        2 * TOK * D * (D + SLOTS),
        8e6,
        scratch_shapes=[pltpu.VMEM((TOK, D), bf16)],
        name="middle",
    )(att, x, wo, gain.reshape(1, D), pick)


def raw_kernel(first_ref, top_ref, down_ref, rows_ref, raw_ref):
    number = first_ref[0] + pl.program_id(0)
    chosen = (lane_index((8, LANES)) == number).astype(bf16)
    slot = lax.broadcasted_iota(jnp.int32, (CAP, TOK), 0).astype(f32)
    for n in range(16):
        place = dot_rows(chosen, top_ref[n, :, D:])[0:1]
        rows = dot((slot == place).astype(bf16), top_ref[n, :, :D])
        rows_ref[CAP * n : CAP * n + CAP] = rows.astype(bf16)
    raw_ref[...] = branch_scale * dot_rows(rows_ref[...], down_ref[...])


def raw_grads(first, top, down):
    return call(
        raw_kernel,
        (struct((2, 768, D), bf16), struct((2, 768, F), f32)),
        2 * SLOTS * D * F,
        1.2e7,
        grid=(2,),
        in_specs=[
            pl.BlockSpec(memory_space=pltpu.SMEM),
            pl.BlockSpec((16, TOK, D + LANES), lambda n: (0, 0, 0)),
            owned(F, D),
        ],
        out_specs=(owned(768, D), owned(768, F)),
        name="raw",
    )(first, top, down)


def expert_kernel(
    first_ref, x_ref, raw_ref, gu_ref, wr_ref, back_ref, hidden_ref, mixed_ref, gate_ref, logit_ref, norm_ref
):
    number = first_ref[0] + pl.program_id(0)
    wr = wr_ref[...]
    for part in range(2):
        take = slice(8 * part, 8 * part + 8)
        rows = slice(384 * part, 384 * part + 384)
        x = x_ref[take].reshape(384, D)
        logits = dot(x, wr)
        raised = jnp.exp(logits - jnp.max(logits, axis=-1, keepdims=True))
        probs = raised / jnp.sum(raised, axis=-1, keepdims=True)
        chosen = (lane_index(probs.shape) == number).astype(f32)
        gate_value = jnp.sum(probs * chosen, axis=-1, keepdims=True)
        gate_ref[rows] = gate_value
        pre = dot(x, gu_ref[...])
        raw = raw_ref[rows]
        gate = pre[:, :F]
        up = pre[:, F:]
        sig = 1.0 / (1.0 + jnp.exp(-gate))
        act = gate * sig
        hidden = (act * up).astype(bf16)
        hidden_ref[rows] = hidden
        grad_gate = jnp.sum(hidden.astype(f32) * raw, axis=-1, keepdims=True)
        grad_logits = (gate_value * grad_gate) * (chosen - probs)
        logit_ref[rows] = grad_logits
        raw = raw * gate_value
        mixed_gate = (raw * up * sig * (1.0 + gate * (1.0 - sig))).astype(bf16)
        mixed_up = (raw * act).astype(bf16)
        mixed_ref[rows, :F] = mixed_gate
        mixed_ref[rows, F:] = mixed_up
        hi, lo = split2(grad_logits)
        back = dot_rows(mixed_gate, gu_ref[:, :F]) + dot_rows(mixed_up, gu_ref[:, F:])
        back = back + dot_rows(hi, wr) + dot_rows(lo, wr)
        back_ref[take] = back.astype(bf16).reshape(8, CAP, D)
        product = jnp.sum(back * x.astype(f32), axis=0, keepdims=True)
        if part == 0:
            norm_ref[...] = jnp.broadcast_to(product, (8, D))
        else:
            norm_ref[...] += product


def owned(*shape):
    return pl.BlockSpec((None, *shape), lambda n: (n, *([0] * len(shape))))


def experts(first, x, raw, gate_up, wr):
    per = pl.BlockSpec((16, None, CAP, D), lambda n: (0, n, 0, 0))
    return call(
        expert_kernel,
        (
            struct((16, 2, CAP, D), bf16),
            struct((2, 768, F), bf16),
            struct((2, 768, D), bf16),
            struct((2, 768, 1), f32),
            struct((2, 768, EXPERTS), f32),
            struct((2, 8, D), f32),
        ),
        2 * SLOTS * D * 2560,
        2e7,
        grid=(2,),
        in_specs=[
            pl.BlockSpec(memory_space=pltpu.SMEM),
            per,
            owned(768, F),
            owned(D, D),
            pl.BlockSpec((D, EXPERTS), lambda n: (0, 0)),
        ],
        out_specs=(per, owned(768, F), owned(768, D), owned(768, 1), owned(768, EXPERTS), owned(8, D)),
        name="experts",
    )(first, x, raw, gate_up, wr)


def expert_grads_kernel(
    x_ref, top_ref, gate_ref, logit_ref, hidden_ref, mixed_ref, down_ref, out_ref, dgu_ref, ddown_ref, router_ref
):
    hidden = hidden_ref[...]
    gate = gate_ref[...]
    x = x_ref[...].reshape(768, D)
    out_ref[...] = (gate * dot(hidden, down_ref[...])).astype(bf16).reshape(16, CAP, D)
    top = (branch_scale * gate * top_ref[...].astype(f32)).astype(bf16)
    ddown_ref[...] = dot_down(hidden, top).astype(bf16)
    dgu_ref[...] = dot_down(x, mixed_ref[...]).astype(bf16)
    hi, lo = split2(logit_ref[...])
    router_ref[...] = dot_down(hi, x) + dot_down(lo, x)


def expert_grads(x, top, gate, logits, hidden, mixed, down):
    per = pl.BlockSpec((16, None, CAP, D), lambda n: (0, n, 0, 0))
    return call(
        expert_grads_kernel,
        (
            struct((16, 2, CAP, D), bf16),
            struct((2, D, D), bf16),
            struct((2, F, D), bf16),
            struct((2, EXPERTS, D), f32),
        ),
        2 * SLOTS * D * 2048,
        2.4e7,
        grid=(2,),
        in_specs=[per, owned(768, D), owned(768, 1), owned(768, EXPERTS), owned(768, F), owned(768, D), owned(F, D)],
        out_specs=(per, owned(D, D), owned(F, D), owned(EXPERTS, D)),
        name="expert_grads",
    )(x, top, gate, logits, hidden, mixed, down)


def turn_back_kernel(
    back_ref, spot_ref, hidden_ref, gain_ref, top_ref, wo_ref, state_ref, attn_ref, send_ref
):
    grad = dot(spot_ref[...], back_ref[...])
    hidden = hidden_ref[...]
    inverse = lax.rsqrt(jnp.mean(hidden * hidden, axis=-1, keepdims=True) + norm_eps)
    normed = hidden * inverse
    scaled = grad * gain_ref[...]
    state = top_ref[...].astype(f32) + inverse * (scaled - normed * jnp.mean(scaled * normed, axis=-1, keepdims=True))
    state_ref[...] = state
    attn = (branch_scale * state).astype(bf16)
    for e in range(16):
        attn_ref[e] = attn[64 * (e % 2) : 64 * (e % 2) + 64]
    attended = dot_rows(attn, wo_ref[...]).astype(bf16)
    for j in range(PAIRS):
        for h in range(2):
            send_ref[2 * j + h] = attended[h * 64 : h * 64 + 64, j * LANES : (j + 1) * LANES]


def turn_back(back, spot, hidden, gain, top, wo):
    return call(
        turn_back_kernel,
        (
            struct((TOK, D), f32),
            struct((16, 64, D), bf16),
            struct((16, TOK // 2, LANES), bf16),
        ),
        2 * 256 * D * (D + SLOTS),
        8e6,
        name="turn_back",
    )(back, spot, hidden, gain.reshape(1, D), top, wo)


def unturn(v, cos, sin, first):
    scaled = v * sin
    return v * cos + jnp.where(first, pltpu.roll(scaled, LANES - 32, 1), pltpu.roll(scaled, 32, 1))


def merge_kernel(
    place_ref, d0_ref, left_a_ref, left_b_ref, right_a_ref, right_b_ref, keep_ref, give_ref, sum_ref
):
    half = place_ref[1]
    for part, left, right in ((0, left_a_ref, right_a_ref), (1, left_b_ref, right_b_ref)):
        rows = slice(part * 1024, part * 1024 + 1024)
        total = d0_ref[rows] + left[...].astype(f32) + right[...].astype(f32)
        sum_ref[8 * part : 8 * part + 8] = total.reshape(8, TOK, LANES)
    keep_ref[...] = sum_ref[:, pl.ds(pl.multiple_of(half * 64, 64), 64), :]
    give_ref[...] = sum_ref[:, pl.ds(pl.multiple_of((1 - half) * 64, 64), 64), :].astype(bf16)


def merge(place, *pieces):
    smem = pl.BlockSpec(memory_space=pltpu.SMEM)
    vmem = pl.BlockSpec(memory_space=pltpu.VMEM)
    return call(
        merge_kernel,
        (struct((16, 64, LANES), f32), struct((16, 64, LANES), bf16)),
        1e6,
        3e6,
        in_specs=[smem] + [vmem] * 5,
        out_specs=(vmem, vmem),
        scratch_shapes=[pltpu.VMEM((16, TOK, LANES), f32)],
        name="merge",
    )(place, *pieces)


def unturn_kernel(dq_ref, dq_far_ref, keep_ref, got_ref, cos_ref, sin_ref, grads_ref):
    lane = lane_index((512, LANES))
    first = lane % HEAD_DIM < HEAD_DIM // 2
    for part, dq in ((0, dq_ref), (1, dq_far_ref)):
        rows = slice(512 * part, 512 * part + 512)
        take = slice(8 * part, 8 * part + 8)
        cos = cos_ref[rows]
        sin = sin_ref[rows]
        grads_ref[rows, :LANES] = unturn(dq[...].reshape(512, LANES).astype(f32), cos, sin, first).astype(bf16)
        both = (keep_ref[take] + got_ref[take].astype(f32)).reshape(512, LANES).astype(bf16).astype(f32)
        grads_ref[rows, LANES:] = jnp.where(lane < HEAD_DIM, unturn(both, cos, sin, first), both).astype(bf16)


def unturn_rows(dq, dq_far, keep, got, cos, sin):
    return call(unturn_kernel, struct((1024, 256), bf16), 1e6, 3e6, name="unturn")(dq, dq_far, keep, got, cos, sin)


def head_kernel(
    place_ref, act_ref, o_ref, grads_ref, extra_ref, a0_ref, a1_ref, a2_ref, a3_ref, mine_ref, other_ref, all_ref, attn_ref
):
    grads = dot_down(act_ref[...], grads_ref[...]).astype(bf16)
    for part, ref in enumerate((a0_ref, a1_ref, a2_ref, a3_ref)):
        attn_ref[:, 16 * part : 16 * part + 16, :] = ref[...]
    out = dot_down(o_ref[...], attn_ref[...].reshape(1024, D)).astype(bf16)
    for quarter in range(4):
        start = 384 * quarter
        all_ref[start : start + 256] = grads[256 * quarter : 256 * quarter + 256]
        all_ref[start + 256 : start + 384] = out[:, 256 * quarter : 256 * quarter + 256]
    extra = extra_ref[0].astype(f32)
    for e in range(1, 16):
        extra = extra + extra_ref[e].astype(f32)
    packed = extra[:, :256]
    for b in range(1, 4):
        packed = packed + pltpu.roll(extra[:, 256 * b : 256 * (b + 1)], 4 * b, 0)
    packed = packed.astype(bf16)
    core = place_ref[2]
    for which, out_ref in ((1 - core, other_ref), (core, mine_ref)):
        out_ref[:768] = all_ref[pl.ds(pl.multiple_of(which * 768, 768), 768), :]
        out_ref[768:] = packed


def head_grads(place, act, o, grads, returned):
    whole = lambda *shape: pl.BlockSpec(shape, lambda i, place: (0,) * len(shape))
    half = struct((784, 256), bf16)
    return call(
        head_kernel,
        (half, half),
        2 * 1024 * 1024 * 512,
        8e6,
        grid_spec=pltpu.PrefetchScalarGridSpec(
            num_scalar_prefetch=1,
            grid=(1,),
            in_specs=[
                whole(1024, D),
                whole(1024, LANES),
                whole(1024, 256),
                pl.BlockSpec((16, 16, D), lambda i, place: (0, 6, 0)),
                pl.BlockSpec((16, 16, D), lambda i, place: (0, 7, 0)),
                pl.BlockSpec((16, 16, D), lambda i, place: (0, 8, 0)),
                pl.BlockSpec((16, 16, D), lambda i, place: (0, 9, 0)),
                pl.BlockSpec((16, 16, D), lambda i, place: (0, 10, 0)),
            ],
            out_specs=(whole(784, 256), whole(784, 256)),
            scratch_shapes=[pltpu.VMEM((1536, 256), bf16), pltpu.VMEM((16, 64, D), bf16)],
        ),
        name="head_grads",
    )(place, act, o, grads, *([returned] * 5))


def split_kernel(place_ref, mine_ref, other_ref, keep_ref, give_ref):
    half = place_ref[1]
    rows = pl.ds(pl.multiple_of(half * 384, 384), 384)
    keep_ref[:384] = mine_ref[rows, :].astype(f32) + other_ref[rows, :].astype(f32)
    keep_ref[384:] = mine_ref[768:, :].astype(f32) + other_ref[768:, :].astype(f32)
    rows = pl.ds(pl.multiple_of((1 - half) * 384, 384), 384)
    give_ref[...] = (mine_ref[rows, :].astype(f32) + other_ref[rows, :].astype(f32)).astype(bf16)


def split_halves(place, mine, other):
    smem = pl.BlockSpec(memory_space=pltpu.SMEM)
    vmem = pl.BlockSpec(memory_space=pltpu.VMEM)
    return call(
        split_kernel,
        (struct((400, 256), f32), struct((384, 256), bf16)),
        1e6,
        2e6,
        in_specs=[smem, vmem, vmem],
        out_specs=(vmem, vmem),
        name="split",
    )(place, mine, other)


def finish_kernel(grads_ref, x_ref, gain_ref, wq_ref, wk_ref, wv_ref, state_ref, out_ref, flat_ref):
    left = lane_index((TOK // 2, LANES)) < HEAD_DIM
    for h in range(2):
        rows = slice(64 * h, 64 * h + 64)
        for j in range(PAIRS):
            flat_ref[rows, j * LANES : (j + 1) * LANES] = grads_ref[2 * j + h, :, :LANES]
        for b in range(PAIRS // 2):
            even = grads_ref[4 * b + h, :, LANES:].astype(f32)
            odd = grads_ref[4 * b + 2 + h, :, LANES:].astype(f32)
            k = jnp.where(left, even, pltpu.roll(odd, HEAD_DIM, 1))
            v = jnp.where(left, pltpu.roll(even, HEAD_DIM, 1), odd)
            flat_ref[rows, D + b * LANES : D + (b + 1) * LANES] = k.astype(bf16)
            flat_ref[rows, D + 512 + b * LANES : D + 512 + (b + 1) * LANES] = v.astype(bf16)
    grad = dot_rows(flat_ref[:, :D], wq_ref[...])
    grad = grad + dot_rows(flat_ref[:, D : D + 512], wk_ref[...])
    grad = grad + dot_rows(flat_ref[:, D + 512 :], wv_ref[...])
    x = x_ref[...].astype(f32)
    inverse = lax.rsqrt(jnp.mean(x * x, axis=-1, keepdims=True) + norm_eps)
    normed = x * inverse
    scaled = grad * gain_ref[...]
    out_ref[...] = state_ref[...] + inverse * (scaled - normed * jnp.mean(scaled * normed, axis=-1, keepdims=True))


def finish(grads, x, gain, wq, wk, wv, state):
    return call(
        finish_kernel,
        struct((TOK, D), f32),
        2 * 256 * D * 2048,
        8e6,
        scratch_shapes=[pltpu.VMEM((TOK, 2048), bf16)],
        name="finish",
    )(grads, x, gain.reshape(1, D), wq, wk, wv, state)


def assemble_kernel(place_ref, piece, wq_ref, wk_ref, wv_ref, gain_ref, *refs):
    q_ref, k_ref, v_ref, o_ref, norm_ref = refs[-5:]
    left = lane_index((256, LANES)) < HEAD_DIM
    total = jnp.zeros((256, LANES), f32)
    for j in range(PAIRS):
        lanes = slice(j * LANES, (j + 1) * LANES)
        value = piece[j, :256, :LANES].astype(f32)
        q_ref[:, lanes] = value
        total = total + value * wq_ref[:, lanes].astype(f32)
        o_ref[lanes, :] = piece[j, 256:384, :].astype(f32)
    for b in range(PAIRS // 2):
        lanes = slice(b * LANES, (b + 1) * LANES)
        even = piece[2 * b, :256, LANES:].astype(f32)
        odd = piece[2 * b + 1, :256, LANES:].astype(f32)
        k = jnp.where(left, even, pltpu.roll(odd, HEAD_DIM, 1))
        v = jnp.where(left, pltpu.roll(even, HEAD_DIM, 1), odd)
        k_ref[:, lanes] = k
        v_ref[:, lanes] = v
        total = total + k * wk_ref[:, lanes].astype(f32) + v * wv_ref[:, lanes].astype(f32)
    norm_ref[...] = jnp.sum(jnp.transpose(total), axis=0, keepdims=True) / gain_ref[...]


def assemble(place, core, pieces, wq, wk, wv, gain, before=()):
    def quarter(i, place):
        return 2 * (place[2] if core == 0 else 1 - place[2]) + i

    rows = lambda width: pl.BlockSpec((256, width), lambda i, place: (quarter(i, place), 0))
    columns = lambda height: pl.BlockSpec((height, 256), lambda i, place: (0, quarter(i, place)))
    return call(
        assemble_kernel,
        (
            struct((D, D), f32),
            struct((D, 512), f32),
            struct((D, 512), f32),
            struct((D, D), f32),
            struct((1, D), f32),
        ),
        1e6,
        1.1e7,
        grid_spec=pltpu.PrefetchScalarGridSpec(
            num_scalar_prefetch=1,
            grid=(2,),
            in_specs=[
                pl.BlockSpec((PAIRS, None, 400, 256), lambda i, place: (0, i, 0, 0)),
                rows(D),
                rows(512),
                rows(512),
                columns(1),
            ]
            + [pl.BlockSpec(memory_space=pl.ANY)] * len(before),
            out_specs=(rows(D), rows(512), rows(512), columns(D), columns(1)),
        ),
        input_output_aliases={6 + i: i for i in range(len(before))},
        name="assemble",
    )(place, pieces.reshape(PAIRS, 2, 400, 256), wq, wk, wv, gain.reshape(1, D), *before)


def spread_kernel(a_ref, b_ref, out_ref):
    total = (a_ref[...].astype(f32) + b_ref[...].astype(f32)).astype(bf16)
    for e in range(16):
        out_ref[e] = total


def add_and_spread(a, b):
    return call(spread_kernel, struct((16, 400, 256), bf16), 1e6, 4e6, name="spread")(a, b)


def after(x, *earlier):
    return lax.optimization_barrier((x, *earlier))[0]


def to_owners(x):
    return lax.all_to_all(x, "expert", split_axis=0, concat_axis=0, tiled=True)


def mirror(x):
    return lax.ppermute(x, "context", [(0, 3), (1, 2), (2, 1), (3, 0)])


def swap_cores(x):
    return lax.ppermute(x, "dp", [(0, 1), (1, 0)])


def shift(x, by):
    return lax.ppermute(x, "context", [(i, (i + by) % 4) for i in range(4)])


def neighbour(x):
    return lax.ppermute(x, "context", [(0, 1), (1, 0), (2, 3), (3, 2)])


def swap_halves(x):
    return lax.ppermute(x, "expert", [(i, i ^ 1) for i in range(16)])


def pick(x, index, axis=0):
    return lax.dynamic_index_in_dim(x, index, axis, False)


def rope_tables(positions):
    frequency = rope_base ** (-jnp.arange(0, HEAD_DIM, 2, dtype=f32) / HEAD_DIM)
    angles = positions.astype(f32)[:, None] * frequency[None, :]
    cos, sin = jnp.cos(angles), jnp.sin(angles)
    return jnp.concatenate([cos] * 4, -1), jnp.concatenate([-sin, sin] * 2, -1)


def local(
    layer_input, grad_output, norm1_gain, norm2_gain, w_query, w_key, w_value, w_out, w_router, w_gate_up, w_down, routes
):
    context = lax.axis_index("context")
    expert = lax.axis_index("expert")
    x = layer_input[0, 0]
    top = grad_output[0, 0]

    half = expert % 2

    cos, sin = rope_tables(context * BLOCK + expert * TOK + jnp.arange(TOK, dtype=jnp.int32))
    order = jnp.arange(1024, dtype=jnp.int32)
    half_cos, half_sin = rope_tables(context * BLOCK + order + (order // 64) * 64 + half * 64)

    hits = jnp.sum((routes[0, 0][:, :, None] == jnp.arange(EXPERTS, dtype=jnp.int32)).astype(f32), 1)
    lower = np.tril(np.ones((TOK, TOK), np.float32), -1)
    place = dot(jnp.asarray(lower, bf16), hits.astype(bf16))
    owner = np.repeat(np.eye(EXPERTS, dtype=np.float32), CAP, 0)
    owner16 = jnp.asarray(owner, bf16)
    slot_number = jnp.arange(SLOTS, dtype=jnp.int32) % CAP
    marked = jnp.where(hits > 0.5, place, 255.0).astype(bf16)
    spot = (dot_rows(marked, owner16) == slot_number[None, :].astype(f32)).astype(bf16)
    selector = (dot_rows(owner16, marked) == slot_number[:, None].astype(f32)).astype(bf16)

    act_send, q_send, kv_send = project(x, norm1_gain, w_query, w_key, w_value, cos, sin)
    kv_own = to_owners(kv_send).reshape(BLOCK, LANES)
    kv_left, kv_right = shift(kv_own, 1), shift(kv_own, 3)
    q_own = to_owners(after(q_send, kv_own))
    q_far = mirror(q_own[8:])
    far_a, far_b = shift(kv_left[: BLOCK // 2], 1), shift(kv_right[BLOCK // 2 :], 3)

    down = lax.all_gather(w_down, ("context", "dp"), axis=1, tiled=True)
    wide = jnp.concatenate([top, jnp.pad(marked, ((0, 0), (0, LANES - EXPERTS)))], 1)
    top_all = lax.all_gather(wide, "expert", axis=0, tiled=True)
    gate_up = lax.all_gather(w_gate_up, ("context", "dp"), axis=1, tiled=True)
    act_rows = to_owners(after(act_send, q_far, far_a, far_b)).reshape(1024, D)

    seat = jnp.stack([context, half, lax.axis_index("dp")]).astype(jnp.int32)
    o, o_low, o_far, lse, kv = attend_forward(
        seat, q_own, q_far, (kv_own, kv_left, far_a, far_b, kv_right)
    )
    o_far = after(o_far, act_rows)
    o_own = jnp.concatenate([o_low, mirror(o_far)], 0)
    att = to_owners(o_own)
    first = (2 * expert).astype(jnp.int32).reshape(1)
    top_rows, raw = raw_grads(first, top_all.reshape(16, TOK, D + LANES), down)

    hidden, send = middle(att, x, w_out, norm2_gain, selector)
    rows = after(to_owners(send.reshape(16, 2, CAP, D)), raw)
    grad_rows, expert_hidden, mixed, gates, logits, norm2_sum = experts(first, rows, raw, gate_up, w_router)
    back = to_owners(grad_rows)
    out_rows, dgu, ddown, router_grad = expert_grads(rows, top_rows, gates, logits, expert_hidden, mixed, down)
    norm2_row = (norm2_sum[0, :1] + norm2_sum[1, :1]) / norm2_gain[None]
    extra = jnp.concatenate([router_grad[0] + router_grad[1], norm2_row, jnp.zeros((31, D), f32)], 0)
    extra = jnp.pad(extra.reshape(16, 4, D), ((0, 0), (0, 12), (0, 0))).astype(bf16)
    out_send = jnp.concatenate([out_rows.reshape(16, 96, D), extra], 1)
    back = after(back, dgu, out_send)

    state, attn, do_send = turn_back(
        back.reshape(SLOTS, D), spot, hidden, norm2_gain, top, w_out
    )
    do_own = to_owners(do_send)
    do_far = mirror(do_own[8:])
    returned = to_owners(after(jnp.concatenate([out_send, attn], 1), do_own))
    grad_gate_up = lax.psum_scatter(
        after(dgu, do_own), ("context", "dp"), scatter_dimension=1, tiled=True
    ).astype(f32)

    dq, dq_far, d0, d1a, d1b, d2a, d2b, d3a, d3b = attend_backward(seat, q_own, q_far, do_own, do_far, o, lse, kv)

    far_a, far_b = shift(d2a, 1), shift(d2b, 3)
    from_left_b, from_right_a = shift(d3b, 1), shift(d1a, 3)
    dq_far = mirror(after(dq_far, far_a, far_b))
    from_left_a = shift((d3a.astype(f32) + far_a.astype(f32)).astype(bf16), 1)
    from_right_b = shift((d1b.astype(f32) + far_b.astype(f32)).astype(bf16), 3)
    keep, give = merge(seat, d0, from_left_a, from_left_b, from_right_a, from_right_b)
    got = after(swap_halves(give), returned)
    grads = unturn_rows(dq, dq_far, keep, got, half_cos, half_sin)
    mine, other = head_grads(
        seat,
        act_rows,
        o_own.reshape(1024, LANES),
        grads,
        returned,
    )
    keep, give = split_halves(seat, mine, swap_cores(other))
    grads_back = to_owners(grads.reshape(16, 64, 256))
    total = keep + jnp.pad(swap_halves(give), ((0, 16), (0, 0))).astype(f32)
    total = total.astype(bf16)
    total = (total.astype(f32) + neighbour(total).astype(f32)).astype(bf16)
    block = after(add_and_spread(total, mirror(total)), grads_back)
    whole = to_owners(block)

    grad_input = finish(grads_back, x, norm1_gain, w_query, w_key, w_value, state)
    block_out = hidden + branch_scale * dot(spot, returned[:, :96].reshape(SLOTS, D))
    grad_down = lax.psum_scatter(after(ddown, got), ("context", "dp"), scatter_dimension=1, tiled=True).astype(f32)
    whole, grad_input, block_out, grad_gate_up, grad_down = lax.optimization_barrier(
        (whole, grad_input, block_out, grad_gate_up, grad_down)
    )
    weights = (w_query, w_key, w_value, norm1_gain)
    own_part = assemble(seat, 0, whole, *weights)
    dwq, dwk, dwv, dwo, norm1_grad = assemble(seat, 1, swap_cores(whole), *weights, before=own_part)
    small = whole[:, 384:].reshape(16, 4, 4, 256).transpose(0, 2, 1, 3).reshape(64, D).astype(f32)
    return (
        block_out.reshape(1, 1, TOK, D),
        grad_input.reshape(1, 1, TOK, D),
        norm1_grad[0],
        small[EXPERTS],
        dwq,
        dwk,
        dwv,
        dwo,
        small[:EXPERTS].T,
        grad_gate_up,
        grad_down,
    )


def solution(mesh):
    tokens = P("dp", "context", "expert", None)
    weights = P("expert", ("context", "dp"), None)
    return jax.shard_map(
        local,
        mesh=mesh,
        in_specs=(tokens, tokens, P(), P(), P(), P(), P(), P(), P(), weights, weights, tokens),
        out_specs=(tokens, tokens, P(), P(), P(), P(), P(), P(), P(), weights, weights),
        check_vma=False,
    )
```

```python
import jax
import jax.numpy as jnp
import numpy as np
from jax import lax
from jax.experimental import pallas as pl
from jax.experimental.pallas import tpu as pltpu
from jax.sharding import PartitionSpec as P

D = 1024
HEAD_DIM = 64
F = 512
EXPERTS = 32
CAP = 48
TOK = 128
BLOCK = 2048
LANES = 128
SLOTS = EXPERTS * CAP
PAIRS = 8
CHUNK = 512

norm_eps = 1e-06
score_scale = 0.015625
branch_scale = 0.22
rope_base = 10000.0
huge_negative = -1e30
bf16 = jnp.bfloat16
f32 = jnp.float32
VMEM_LIMIT = 56 * 1024 * 1024


def call(kernel, out_shape, flops, moved, **kw):
    return pl.pallas_call(
        kernel,
        out_shape=out_shape,
        compiler_params=pltpu.CompilerParams(vmem_limit_bytes=VMEM_LIMIT),
        cost_estimate=pl.CostEstimate(flops=int(flops), bytes_accessed=int(moved), transcendentals=0),
        **kw,
    )


def struct(shape, dtype):
    return jax.ShapeDtypeStruct(shape, dtype)


def dot(a, b):
    return jnp.dot(a, b, preferred_element_type=f32)


def dot_rows(a, b):
    return lax.dot_general(a, b, (((1,), (1,)), ((), ())), preferred_element_type=f32)


def dot_down(a, b):
    return lax.dot_general(a, b, (((0,), (0,)), ((), ())), preferred_element_type=f32)


def split2(x):
    hi = x.astype(bf16)
    return hi, (x - hi.astype(f32)).astype(bf16)


def lane_index(shape):
    return lax.broadcasted_iota(jnp.int32, shape, len(shape) - 1)


def project_kernel(x_ref, gain_ref, wq_ref, wk_ref, wv_ref, cos_ref, sin_ref, act_ref, q_ref, kv_ref):
    x = x_ref[...].astype(f32)
    inverse = lax.rsqrt(jnp.mean(x * x, axis=-1, keepdims=True) + norm_eps)
    act = (x * inverse * gain_ref[...]).astype(bf16)
    for e in range(16):
        act_ref[e] = act[64 * (e % 2) : 64 * (e % 2) + 64]
    cos = cos_ref[...]
    sin = sin_ref[...]
    lane = lane_index((TOK, LANES))
    first = lane % HEAD_DIM < HEAD_DIM // 2
    left = lane < HEAD_DIM

    def turn(v):
        moved = jnp.where(first, pltpu.roll(v, LANES - 32, 1), pltpu.roll(v, 32, 1))
        return v * cos + moved * sin

    q = dot(act, wq_ref[...])
    for j in range(PAIRS):
        rows = turn(q[:, j * LANES : (j + 1) * LANES]).astype(bf16)
        q_ref[2 * j] = rows[: TOK // 2]
        q_ref[2 * j + 1] = rows[TOK // 2 :]
    k = dot(act, wk_ref[...])
    v = dot(act, wv_ref[...])
    for b in range(PAIRS // 2):
        kb = turn(k[:, b * LANES : (b + 1) * LANES])
        vb = v[:, b * LANES : (b + 1) * LANES]
        even = jnp.where(left, kb, pltpu.roll(vb, HEAD_DIM, 1)).astype(bf16)
        odd = jnp.where(left, pltpu.roll(kb, HEAD_DIM, 1), vb).astype(bf16)
        kv_ref[4 * b] = even
        kv_ref[4 * b + 1] = even
        kv_ref[4 * b + 2] = odd
        kv_ref[4 * b + 3] = odd


def project(x, gain, wq, wk, wv, cos, sin):
    return call(
        project_kernel,
        (struct((16, 64, D), bf16), struct((16, 64, LANES), bf16), struct((16, TOK, LANES), bf16)),
        2 * TOK * D * 2048,
        6e6,
        name="project",
    )(x, gain.reshape(1, D), wq, wk, wv, cos, sin)


def query_of_head(q, head, left):
    q = q.astype(f32) * score_scale
    if head:
        q = pltpu.roll(q, HEAD_DIM, 1)
    return jnp.where(left, q, 0.0).astype(bf16)


def forward_kernel(
    place_ref, q_ref, q_far_ref, own_ref, left_ref, far_a_ref, far_b_ref, right_ref,
    o_ref, low_ref, low_far_ref, lse_ref, kv_ref, qm_ref, top_ref, acc_ref,
):
    tile = 1024
    context = place_ref[0]
    half = place_ref[1]

    def put(back, part, ref):
        start = lax.rem(context + 4 - back, 4) * BLOCK + part * (BLOCK // 2)
        rows = ref.shape[0]
        kv_ref[pl.ds(pl.multiple_of(start, BLOCK // 2), rows), :] = ref[...]

    put(0, 0, own_ref)
    put(1, 0, left_ref)
    put(2, 0, far_a_ref)
    put(2, 1, far_b_ref)
    put(3, 0, right_ref)
    left = lane_index((CHUNK, LANES)) < HEAD_DIM
    left_keys = lane_index((tile, LANES)) < HEAD_DIM
    for chunk in range(2):
        whole = 2 * (context if chunk == 0 else 3 - context) + chunk
        queries = (q_far_ref[...] if chunk else q_ref[:8]).reshape(CHUNK, LANES)
        for head in range(2):
            qm_ref[head] = query_of_head(queries, head, left)
            top_ref[head] = jnp.full((CHUNK, LANES), huge_negative, f32)
            acc_ref[head] = jnp.zeros((CHUNK, LANES), f32)

        def step(index, masked):
            keys = kv_ref[pl.ds(pl.multiple_of(index * tile, tile), tile), :]
            values = jnp.where(left_keys, jnp.ones_like(keys), keys)
            for head in range(2):
                for part in range(2):
                    rows = slice(part * 256, part * 256 + 256)
                    s = dot_rows(qm_ref[head, rows], keys)
                    if masked:
                        r = lax.broadcasted_iota(jnp.int32, s.shape, 0) + part * 256
                        place = r + (r // 64) * 64 + half * 64
                        s = jnp.where(lane_index(s.shape) <= place, s, huge_negative)
                    old = top_ref[head, rows]
                    new = jnp.maximum(old, jnp.max(s, axis=1, keepdims=True))
                    p = jnp.exp(s - new[:, :1]).astype(bf16)
                    acc_ref[head, rows] = acc_ref[head, rows] * jnp.exp(old - new) + dot(p, values)
                    top_ref[head, rows] = new

        def visit(index, carry):
            step(index, False)
            return carry

        lax.fori_loop(0, whole, visit, 0)
        step(whole, True)
        outs = []
        for head in range(2):
            acc = acc_ref[head]
            outs.append(pltpu.roll(acc, HEAD_DIM, 1) / acc)
            total = top_ref[head] + jnp.log(jnp.where(left, acc, 1.0))
            lse_ref[2 * chunk + head] = jnp.transpose(total)[0:8]
        o = jnp.where(left, outs[0], pltpu.roll(outs[1], HEAD_DIM, 1))
        o_ref[chunk] = o
        (low_far_ref if chunk else low_ref)[...] = o.astype(bf16).reshape(8, 64, LANES)


def attend_forward(place, q, q_far, kv_parts):
    smem = pl.BlockSpec(memory_space=pltpu.SMEM)
    vmem = pl.BlockSpec(memory_space=pltpu.VMEM)
    return call(
        forward_kernel,
        (
            struct((2, CHUNK, LANES), f32),
            struct((8, 64, LANES), bf16),
            struct((8, 64, LANES), bf16),
            struct((4, 8, CHUNK), f32),
            struct((4 * BLOCK, LANES), bf16),
        ),
        2e10,
        4e6,
        in_specs=[smem] + [vmem] * 7,
        out_specs=(vmem,) * 5,
        scratch_shapes=[
            pltpu.VMEM((2, CHUNK, LANES), bf16),
            pltpu.VMEM((2, CHUNK, LANES), f32),
            pltpu.VMEM((2, CHUNK, LANES), f32),
        ],
        name="attend",
    )(place, q, q_far, *kv_parts)


def backward_kernel(
    place_ref, q_ref, q_far_ref, do_ref, do_far_ref, o_ref, lse_ref, kv_ref,
    dq_ref, dq_far_ref, d0_ref, d1a_ref, d1b_ref, d2a_ref, d2b_ref, d3a_ref, d3b_ref,
    qm_ref, dom_ref, row_ref, dqt_ref, acc_ref,
):
    tile = 512
    context = place_ref[0]
    half = place_ref[1]
    left = lane_index((CHUNK, LANES)) < HEAD_DIM
    acc_ref[...] = jnp.zeros_like(acc_ref)
    for chunk in range(2):
        whole = 2 * (2 * (context if chunk == 0 else 3 - context) + chunk)
        queries = (q_far_ref[...] if chunk else q_ref[:8]).reshape(CHUNK, LANES)
        do = (do_far_ref[...] if chunk else do_ref[:8]).reshape(CHUNK, LANES).astype(f32)
        product = jnp.transpose(do * o_ref[chunk])
        for head in range(2):
            qm_ref[head] = query_of_head(queries, head, left)
            moved = do if head else pltpu.roll(do, HEAD_DIM, 1)
            dom_ref[head] = jnp.where(left, 0.0, moved).astype(bf16)
            dqt_ref[head] = jnp.zeros((LANES, CHUNK), f32)
            rows = product[head * HEAD_DIM : (head + 1) * HEAD_DIM]
            row_ref[head] = jnp.broadcast_to(jnp.sum(rows, axis=0, keepdims=True), (8, CHUNK))

        def step(index, offset):
            span = pl.ds(pl.multiple_of(index * tile, tile), tile)
            keys = kv_ref[span, :]
            for head in range(2):
                qm = qm_ref[head]
                dom = dom_ref[head]
                s = dot_rows(keys, qm)
                dp = dot_rows(keys, dom)
                p = jnp.exp(s - lse_ref[2 * chunk + head, 0:1])
                if offset is not None:
                    r = lane_index(s.shape)
                    place = r + (r // 64) * 64 + half * 64
                    key = lax.broadcasted_iota(jnp.int32, s.shape, 0) + offset
                    p = jnp.where(key <= place, p, 0.0)
                ds = (p * (dp - row_ref[head, 0:1])).astype(bf16)
                acc_ref[span, :] += dot(ds, qm) + dot(p.astype(bf16), dom)
                dqt_ref[head] += dot_down(keys, ds)

        def visit(index, carry):
            step(index, None)
            return carry

        lax.fori_loop(0, whole, visit, 0)
        step(whole, 0)
        step(whole + 1, tile)
        parts = [jnp.transpose(dqt_ref[head]) * score_scale for head in range(2)]
        dq = jnp.where(left, parts[0], pltpu.roll(parts[1], HEAD_DIM, 1)).astype(bf16)
        (dq_far_ref if chunk else dq_ref)[...] = dq.reshape(8, 64, LANES)
    d0_ref[...] = acc_ref[pl.ds(pl.multiple_of(context * BLOCK, BLOCK), BLOCK), :]
    for back, first, second in ((1, d1a_ref, d1b_ref), (2, d2a_ref, d2b_ref), (3, d3a_ref, d3b_ref)):
        start = pl.multiple_of(lax.rem(context + 4 - back, 4) * BLOCK, BLOCK)
        first[...] = acc_ref[pl.ds(start, BLOCK // 2), :].astype(bf16)
        second[...] = acc_ref[pl.ds(pl.multiple_of(start + BLOCK // 2, BLOCK // 2), BLOCK // 2), :].astype(bf16)


def attend_backward(place, q, q_far, do, do_far, o, lse, kv):
    smem = pl.BlockSpec(memory_space=pltpu.SMEM)
    vmem = pl.BlockSpec(memory_space=pltpu.VMEM)
    rows = kv.shape[0]
    return call(
        backward_kernel,
        (struct((8, 64, LANES), bf16), struct((8, 64, LANES), bf16), struct((BLOCK, LANES), f32))
        + (struct((BLOCK // 2, LANES), bf16),) * 6,
        5e10,
        8e6,
        in_specs=[smem] + [vmem] * 7,
        out_specs=(vmem,) * 9,
        scratch_shapes=[
            pltpu.VMEM((2, CHUNK, LANES), bf16),
            pltpu.VMEM((2, CHUNK, LANES), bf16),
            pltpu.VMEM((2, 8, CHUNK), f32),
            pltpu.VMEM((2, LANES, CHUNK), f32),
            pltpu.VMEM((rows, LANES), f32),
        ],
        name="attend_back",
    )(place, q, q_far, do, do_far, o, lse, kv)


def middle_kernel(att_ref, x_ref, wo_ref, gain_ref, pick_ref, hidden_ref, send_ref, attended_ref):
    for j in range(PAIRS):
        for h in range(2):
            attended_ref[h * 64 : h * 64 + 64, j * LANES : (j + 1) * LANES] = att_ref[2 * j + h]
    hidden = x_ref[...].astype(f32) + branch_scale * dot(attended_ref[...], wo_ref[...])
    hidden_ref[...] = hidden
    inverse = lax.rsqrt(jnp.mean(hidden * hidden, axis=-1, keepdims=True) + norm_eps)
    act = (hidden * inverse * gain_ref[...]).astype(bf16)
    send_ref[...] = dot(pick_ref[...], act).astype(bf16)


def middle(att, x, wo, gain, pick):
    return call(
        middle_kernel,
        (struct((TOK, D), f32), struct((SLOTS, D), bf16)),
        2 * TOK * D * (D + SLOTS),
        8e6,
        scratch_shapes=[pltpu.VMEM((TOK, D), bf16)],
        name="middle",
    )(att, x, wo, gain.reshape(1, D), pick)


def raw_kernel(first_ref, top_ref, down_ref, rows_ref, raw_ref):
    number = first_ref[0] + pl.program_id(0)
    chosen = (lane_index((8, LANES)) == number).astype(bf16)
    slot = lax.broadcasted_iota(jnp.int32, (CAP, TOK), 0).astype(f32)
    for n in range(16):
        place = dot_rows(chosen, top_ref[n, :, D:])[0:1]
        rows = dot((slot == place).astype(bf16), top_ref[n, :, :D])
        rows_ref[CAP * n : CAP * n + CAP] = rows.astype(bf16)
    raw_ref[...] = branch_scale * dot_rows(rows_ref[...], down_ref[...])


def raw_grads(first, top, down):
    return call(
        raw_kernel,
        (struct((2, 768, D), bf16), struct((2, 768, F), f32)),
        2 * SLOTS * D * F,
        1.2e7,
        grid=(2,),
        in_specs=[
            pl.BlockSpec(memory_space=pltpu.SMEM),
            pl.BlockSpec((16, TOK, D + LANES), lambda n: (0, 0, 0)),
            owned(F, D),
        ],
        out_specs=(owned(768, D), owned(768, F)),
        name="raw",
    )(first, top, down)


def expert_kernel(
    first_ref, x_ref, raw_ref, gu_ref, wr_ref, back_ref, hidden_ref, mixed_ref, gate_ref, logit_ref, norm_ref
):
    number = first_ref[0] + pl.program_id(0)
    wr = wr_ref[...]
    for part in range(2):
        take = slice(8 * part, 8 * part + 8)
        rows = slice(384 * part, 384 * part + 384)
        x = x_ref[take].reshape(384, D)
        logits = dot(x, wr)
        raised = jnp.exp(logits - jnp.max(logits, axis=-1, keepdims=True))
        probs = raised / jnp.sum(raised, axis=-1, keepdims=True)
        chosen = (lane_index(probs.shape) == number).astype(f32)
        gate_value = jnp.sum(probs * chosen, axis=-1, keepdims=True)
        gate_ref[rows] = gate_value
        pre = dot(x, gu_ref[...])
        raw = raw_ref[rows]
        gate = pre[:, :F]
        up = pre[:, F:]
        sig = 1.0 / (1.0 + jnp.exp(-gate))
        act = gate * sig
        hidden = (act * up).astype(bf16)
        hidden_ref[rows] = hidden
        grad_gate = jnp.sum(hidden.astype(f32) * raw, axis=-1, keepdims=True)
        grad_logits = (gate_value * grad_gate) * (chosen - probs)
        logit_ref[rows] = grad_logits
        raw = raw * gate_value
        mixed_gate = (raw * up * sig * (1.0 + gate * (1.0 - sig))).astype(bf16)
        mixed_up = (raw * act).astype(bf16)
        mixed_ref[rows, :F] = mixed_gate
        mixed_ref[rows, F:] = mixed_up
        hi, lo = split2(grad_logits)
        back = dot_rows(mixed_gate, gu_ref[:, :F]) + dot_rows(mixed_up, gu_ref[:, F:])
        back = back + dot_rows(hi, wr) + dot_rows(lo, wr)
        back_ref[take] = back.astype(bf16).reshape(8, CAP, D)
        product = jnp.sum(back * x.astype(f32), axis=0, keepdims=True)
        if part == 0:
            norm_ref[...] = jnp.broadcast_to(product, (8, D))
        else:
            norm_ref[...] += product


def owned(*shape):
    return pl.BlockSpec((None, *shape), lambda n: (n, *([0] * len(shape))))


def experts(first, x, raw, gate_up, wr):
    per = pl.BlockSpec((16, None, CAP, D), lambda n: (0, n, 0, 0))
    return call(
        expert_kernel,
        (
            struct((16, 2, CAP, D), bf16),
            struct((2, 768, F), bf16),
            struct((2, 768, D), bf16),
            struct((2, 768, 1), f32),
            struct((2, 768, EXPERTS), f32),
            struct((2, 8, D), f32),
        ),
        2 * SLOTS * D * 2560,
        2e7,
        grid=(2,),
        in_specs=[
            pl.BlockSpec(memory_space=pltpu.SMEM),
            per,
            owned(768, F),
            owned(D, D),
            pl.BlockSpec((D, EXPERTS), lambda n: (0, 0)),
        ],
        out_specs=(per, owned(768, F), owned(768, D), owned(768, 1), owned(768, EXPERTS), owned(8, D)),
        name="experts",
    )(first, x, raw, gate_up, wr)


def expert_grads_kernel(
    x_ref, top_ref, gate_ref, logit_ref, hidden_ref, mixed_ref, down_ref, norm_ref, gain_ref,
    out_ref, dgu_ref, ddown_ref, router_ref,
):
    n = pl.program_id(0)
    hidden = hidden_ref[...]
    gate = gate_ref[...]
    x = x_ref[...].reshape(768, D)
    out = (gate * dot(hidden, down_ref[...])).astype(bf16).reshape(16, CAP, D)
    out_ref[:, pl.ds(pl.multiple_of(n * CAP, 16), CAP), :] = out
    top = (branch_scale * gate * top_ref[...].astype(f32)).astype(bf16)
    ddown_ref[...] = dot_down(hidden, top).astype(bf16)
    dgu_ref[...] = dot_down(x, mixed_ref[...]).astype(bf16)
    hi, lo = split2(logit_ref[...])
    router = dot_down(hi, x) + dot_down(lo, x)

    @pl.when(n == 0)
    def _():
        router_ref[...] = router

    @pl.when(n == 1)
    def _():
        total = router_ref[...] + router
        norm = (norm_ref[0, 0:1] + norm_ref[1, 0:1]) / gain_ref[...]
        for e in range(16):
            if e < 8:
                extra = jnp.concatenate([total[4 * e : 4 * e + 4], jnp.zeros((12, D), f32)], axis=0)
            elif e == 8:
                extra = jnp.concatenate([norm, jnp.zeros((15, D), f32)], axis=0)
            else:
                extra = jnp.zeros((16, D), f32)
            out_ref[e, 96:112] = extra.astype(bf16)


def expert_grads(x, top, gate, logits, hidden, mixed, down, norm, gain):
    per = pl.BlockSpec((16, None, CAP, D), lambda n: (0, n, 0, 0))
    return call(
        expert_grads_kernel,
        (struct((16, 176, D), bf16), struct((2, D, D), bf16), struct((2, F, D), bf16)),
        2 * SLOTS * D * 2048,
        2.4e7,
        grid=(2,),
        in_specs=[
            per,
            owned(768, D),
            owned(768, 1),
            owned(768, EXPERTS),
            owned(768, F),
            owned(768, D),
            owned(F, D),
            pl.BlockSpec((2, 8, D), lambda n: (0, 0, 0)),
            pl.BlockSpec((1, D), lambda n: (0, 0)),
        ],
        out_specs=(pl.BlockSpec((16, 176, D), lambda n: (0, 0, 0)), owned(D, D), owned(F, D)),
        scratch_shapes=[pltpu.VMEM((EXPERTS, D), f32)],
        name="expert_grads",
    )(x, top, gate, logits, hidden, mixed, down, norm, gain.reshape(1, D))


def turn_back_kernel(
    back_ref, spot_ref, hidden_ref, gain_ref, top_ref, wo_ref, before_ref,
    state_ref, buffer_ref, send_ref, attn_ref, done_ref,
):
    grad = dot(spot_ref[...], back_ref[...])
    hidden = hidden_ref[...]
    inverse = lax.rsqrt(jnp.mean(hidden * hidden, axis=-1, keepdims=True) + norm_eps)
    normed = hidden * inverse
    scaled = grad * gain_ref[...]
    state = top_ref[...].astype(f32) + inverse * (scaled - normed * jnp.mean(scaled * normed, axis=-1, keepdims=True))
    state_ref[...] = state
    attn = (branch_scale * state).astype(bf16)
    for e in range(16):
        attn_ref[e] = attn[64 * (e % 2) : 64 * (e % 2) + 64]
    copy = pltpu.make_async_copy(attn_ref, buffer_ref.at[:, pl.ds(112, 64), :], done_ref)
    copy.start()
    attended = dot_rows(attn, wo_ref[...]).astype(bf16)
    for j in range(PAIRS):
        for h in range(2):
            send_ref[2 * j + h] = attended[h * 64 : h * 64 + 64, j * LANES : (j + 1) * LANES]
    copy.wait()


def turn_back(back, spot, hidden, gain, top, wo, buffer):
    vmem = pl.BlockSpec(memory_space=pltpu.VMEM)
    outside = pl.BlockSpec(memory_space=pl.ANY)
    return call(
        turn_back_kernel,
        (
            struct((TOK, D), f32),
            struct((16, 176, D), bf16),
            struct((16, TOK // 2, LANES), bf16),
        ),
        2 * 256 * D * (D + SLOTS),
        8e6,
        in_specs=[vmem] * 6 + [outside],
        out_specs=(vmem, outside, vmem),
        scratch_shapes=[pltpu.VMEM((16, 64, D), bf16), pltpu.SemaphoreType.DMA],
        input_output_aliases={6: 1},
        name="turn_back",
    )(back, spot, hidden, gain.reshape(1, D), top, wo, buffer)


def unturn(v, cos, sin, first):
    scaled = v * sin
    return v * cos + jnp.where(first, pltpu.roll(scaled, LANES - 32, 1), pltpu.roll(scaled, 32, 1))


def merge_kernel(
    place_ref, d0_ref, left_a_ref, left_b_ref, right_a_ref, right_b_ref, keep_ref, give_ref, sum_ref
):
    half = place_ref[1]
    for part, left, right in ((0, left_a_ref, right_a_ref), (1, left_b_ref, right_b_ref)):
        rows = slice(part * 1024, part * 1024 + 1024)
        total = d0_ref[rows] + left[...].astype(f32) + right[...].astype(f32)
        sum_ref[8 * part : 8 * part + 8] = total.reshape(8, TOK, LANES)
    keep_ref[...] = sum_ref[:, pl.ds(pl.multiple_of(half * 64, 64), 64), :]
    give_ref[...] = sum_ref[:, pl.ds(pl.multiple_of((1 - half) * 64, 64), 64), :].astype(bf16)


def merge(place, *pieces):
    smem = pl.BlockSpec(memory_space=pltpu.SMEM)
    vmem = pl.BlockSpec(memory_space=pltpu.VMEM)
    return call(
        merge_kernel,
        (struct((16, 64, LANES), f32), struct((16, 64, LANES), bf16)),
        1e6,
        3e6,
        in_specs=[smem] + [vmem] * 5,
        out_specs=(vmem, vmem),
        scratch_shapes=[pltpu.VMEM((16, TOK, LANES), f32)],
        name="merge",
    )(place, *pieces)


def unturn_kernel(dq_ref, dq_far_ref, keep_ref, got_ref, cos_ref, sin_ref, grads_ref):
    lane = lane_index((512, LANES))
    first = lane % HEAD_DIM < HEAD_DIM // 2
    for part, dq in ((0, dq_ref), (1, dq_far_ref)):
        rows = slice(512 * part, 512 * part + 512)
        take = slice(8 * part, 8 * part + 8)
        cos = cos_ref[rows]
        sin = sin_ref[rows]
        grads_ref[rows, :LANES] = unturn(dq[...].reshape(512, LANES).astype(f32), cos, sin, first).astype(bf16)
        both = (keep_ref[take] + got_ref[take].astype(f32)).reshape(512, LANES).astype(bf16).astype(f32)
        grads_ref[rows, LANES:] = jnp.where(lane < HEAD_DIM, unturn(both, cos, sin, first), both).astype(bf16)


def unturn_rows(dq, dq_far, keep, got, cos, sin):
    return call(unturn_kernel, struct((1024, 256), bf16), 1e6, 3e6, name="unturn")(dq, dq_far, keep, got, cos, sin)


def head_kernel(
    place_ref, act_ref, o_ref, grads_ref, extra_ref, a0_ref, a1_ref, a2_ref, a3_ref, mine_ref, other_ref, all_ref, attn_ref
):
    grads = dot_down(act_ref[...], grads_ref[...]).astype(bf16)
    for part, ref in enumerate((a0_ref, a1_ref, a2_ref, a3_ref)):
        attn_ref[:, 16 * part : 16 * part + 16, :] = ref[...]
    out = dot_down(o_ref[...], attn_ref[...].reshape(1024, D)).astype(bf16)
    for quarter in range(4):
        start = 384 * quarter
        all_ref[start : start + 256] = grads[256 * quarter : 256 * quarter + 256]
        all_ref[start + 256 : start + 384] = out[:, 256 * quarter : 256 * quarter + 256]
    extra = extra_ref[0].astype(f32)
    for e in range(1, 16):
        extra = extra + extra_ref[e].astype(f32)
    packed = extra[:, :256]
    for b in range(1, 4):
        packed = packed + pltpu.roll(extra[:, 256 * b : 256 * (b + 1)], 4 * b, 0)
    packed = packed.astype(bf16)
    core = place_ref[2]
    for which, out_ref in ((1 - core, other_ref), (core, mine_ref)):
        out_ref[:768] = all_ref[pl.ds(pl.multiple_of(which * 768, 768), 768), :]
        out_ref[768:] = packed


def head_grads(place, act, o, grads, returned):
    whole = lambda *shape: pl.BlockSpec(shape, lambda i, place: (0,) * len(shape))
    half = struct((784, 256), bf16)
    return call(
        head_kernel,
        (half, half),
        2 * 1024 * 1024 * 512,
        8e6,
        grid_spec=pltpu.PrefetchScalarGridSpec(
            num_scalar_prefetch=1,
            grid=(1,),
            in_specs=[
                whole(1024, D),
                whole(1024, LANES),
                whole(1024, 256),
                pl.BlockSpec((16, 16, D), lambda i, place: (0, 6, 0)),
                pl.BlockSpec((16, 16, D), lambda i, place: (0, 7, 0)),
                pl.BlockSpec((16, 16, D), lambda i, place: (0, 8, 0)),
                pl.BlockSpec((16, 16, D), lambda i, place: (0, 9, 0)),
                pl.BlockSpec((16, 16, D), lambda i, place: (0, 10, 0)),
            ],
            out_specs=(whole(784, 256), whole(784, 256)),
            scratch_shapes=[pltpu.VMEM((1536, 256), bf16), pltpu.VMEM((16, 64, D), bf16)],
        ),
        name="head_grads",
    )(place, act, o, grads, *([returned] * 5))


def split_kernel(place_ref, mine_ref, other_ref, keep_ref, give_ref):
    half = place_ref[1]
    rows = pl.ds(pl.multiple_of(half * 384, 384), 384)
    keep_ref[:384] = mine_ref[rows, :].astype(f32) + other_ref[rows, :].astype(f32)
    keep_ref[384:] = mine_ref[768:, :].astype(f32) + other_ref[768:, :].astype(f32)
    rows = pl.ds(pl.multiple_of((1 - half) * 384, 384), 384)
    give_ref[...] = (mine_ref[rows, :].astype(f32) + other_ref[rows, :].astype(f32)).astype(bf16)


def split_halves(place, mine, other):
    smem = pl.BlockSpec(memory_space=pltpu.SMEM)
    vmem = pl.BlockSpec(memory_space=pltpu.VMEM)
    return call(
        split_kernel,
        (struct((400, 256), f32), struct((384, 256), bf16)),
        1e6,
        2e6,
        in_specs=[smem, vmem, vmem],
        out_specs=(vmem, vmem),
        name="split",
    )(place, mine, other)


def finish_kernel(grads_ref, x_ref, gain_ref, wq_ref, wk_ref, wv_ref, state_ref, out_ref, flat_ref):
    left = lane_index((TOK // 2, LANES)) < HEAD_DIM
    for h in range(2):
        rows = slice(64 * h, 64 * h + 64)
        for j in range(PAIRS):
            flat_ref[rows, j * LANES : (j + 1) * LANES] = grads_ref[2 * j + h, :, :LANES]
        for b in range(PAIRS // 2):
            even = grads_ref[4 * b + h, :, LANES:].astype(f32)
            odd = grads_ref[4 * b + 2 + h, :, LANES:].astype(f32)
            k = jnp.where(left, even, pltpu.roll(odd, HEAD_DIM, 1))
            v = jnp.where(left, pltpu.roll(even, HEAD_DIM, 1), odd)
            flat_ref[rows, D + b * LANES : D + (b + 1) * LANES] = k.astype(bf16)
            flat_ref[rows, D + 512 + b * LANES : D + 512 + (b + 1) * LANES] = v.astype(bf16)
    grad = dot_rows(flat_ref[:, :D], wq_ref[...])
    grad = grad + dot_rows(flat_ref[:, D : D + 512], wk_ref[...])
    grad = grad + dot_rows(flat_ref[:, D + 512 :], wv_ref[...])
    x = x_ref[...].astype(f32)
    inverse = lax.rsqrt(jnp.mean(x * x, axis=-1, keepdims=True) + norm_eps)
    normed = x * inverse
    scaled = grad * gain_ref[...]
    out_ref[...] = state_ref[...] + inverse * (scaled - normed * jnp.mean(scaled * normed, axis=-1, keepdims=True))


def finish(grads, x, gain, wq, wk, wv, state):
    return call(
        finish_kernel,
        struct((TOK, D), f32),
        2 * 256 * D * 2048,
        8e6,
        scratch_shapes=[pltpu.VMEM((TOK, 2048), bf16)],
        name="finish",
    )(grads, x, gain.reshape(1, D), wq, wk, wv, state)


def assemble_kernel(place_ref, piece, wq_ref, wk_ref, wv_ref, gain_ref, *refs):
    q_ref, k_ref, v_ref, o_ref, norm_ref = refs[-5:]
    left = lane_index((256, LANES)) < HEAD_DIM
    total = jnp.zeros((256, LANES), f32)
    for j in range(PAIRS):
        lanes = slice(j * LANES, (j + 1) * LANES)
        value = piece[j, :256, :LANES].astype(f32)
        q_ref[:, lanes] = value
        total = total + value * wq_ref[:, lanes].astype(f32)
        o_ref[lanes, :] = piece[j, 256:384, :].astype(f32)
    for b in range(PAIRS // 2):
        lanes = slice(b * LANES, (b + 1) * LANES)
        even = piece[2 * b, :256, LANES:].astype(f32)
        odd = piece[2 * b + 1, :256, LANES:].astype(f32)
        k = jnp.where(left, even, pltpu.roll(odd, HEAD_DIM, 1))
        v = jnp.where(left, pltpu.roll(even, HEAD_DIM, 1), odd)
        k_ref[:, lanes] = k
        v_ref[:, lanes] = v
        total = total + k * wk_ref[:, lanes].astype(f32) + v * wv_ref[:, lanes].astype(f32)
    norm_ref[...] = jnp.sum(jnp.transpose(total), axis=0, keepdims=True) / gain_ref[...]


def assemble(place, core, pieces, wq, wk, wv, gain, before=()):
    def quarter(i, place):
        return 2 * (place[2] if core == 0 else 1 - place[2]) + i

    rows = lambda width: pl.BlockSpec((256, width), lambda i, place: (quarter(i, place), 0))
    columns = lambda height: pl.BlockSpec((height, 256), lambda i, place: (0, quarter(i, place)))
    return call(
        assemble_kernel,
        (
            struct((D, D), f32),
            struct((D, 512), f32),
            struct((D, 512), f32),
            struct((D, D), f32),
            struct((1, D), f32),
        ),
        1e6,
        1.1e7,
        grid_spec=pltpu.PrefetchScalarGridSpec(
            num_scalar_prefetch=1,
            grid=(2,),
            in_specs=[
                pl.BlockSpec((PAIRS, None, 400, 256), lambda i, place: (0, i, 0, 0)),
                rows(D),
                rows(512),
                rows(512),
                columns(1),
            ]
            + [pl.BlockSpec(memory_space=pl.ANY)] * len(before),
            out_specs=(rows(D), rows(512), rows(512), columns(D), columns(1)),
        ),
        input_output_aliases={6 + i: i for i in range(len(before))},
        name="assemble",
    )(place, pieces.reshape(PAIRS, 2, 400, 256), wq, wk, wv, gain.reshape(1, D), *before)


def spread_kernel(a_ref, b_ref, out_ref):
    total = (a_ref[...].astype(f32) + b_ref[...].astype(f32)).astype(bf16)
    for e in range(16):
        out_ref[e] = total


def add_and_spread(a, b):
    return call(spread_kernel, struct((16, 400, 256), bf16), 1e6, 4e6, name="spread")(a, b)


def after(x, *earlier):
    return lax.optimization_barrier((x, *earlier))[0]


def to_owners(x):
    return lax.all_to_all(x, "expert", split_axis=0, concat_axis=0, tiled=True)


def mirror(x):
    return lax.ppermute(x, "context", [(0, 3), (1, 2), (2, 1), (3, 0)])


def swap_cores(x):
    return lax.ppermute(x, "dp", [(0, 1), (1, 0)])


def shift(x, by):
    return lax.ppermute(x, "context", [(i, (i + by) % 4) for i in range(4)])


def neighbour(x):
    return lax.ppermute(x, "context", [(0, 1), (1, 0), (2, 3), (3, 2)])


def swap_halves(x):
    return lax.ppermute(x, "expert", [(i, i ^ 1) for i in range(16)])


def pick(x, index, axis=0):
    return lax.dynamic_index_in_dim(x, index, axis, False)


def rope_tables(positions):
    frequency = rope_base ** (-jnp.arange(0, HEAD_DIM, 2, dtype=f32) / HEAD_DIM)
    angles = positions.astype(f32)[:, None] * frequency[None, :]
    cos, sin = jnp.cos(angles), jnp.sin(angles)
    return jnp.concatenate([cos] * 4, -1), jnp.concatenate([-sin, sin] * 2, -1)


def local(
    layer_input, grad_output, norm1_gain, norm2_gain, w_query, w_key, w_value, w_out, w_router, w_gate_up, w_down, routes
):
    context = lax.axis_index("context")
    expert = lax.axis_index("expert")
    x = layer_input[0, 0]
    top = grad_output[0, 0]

    half = expert % 2

    cos, sin = rope_tables(context * BLOCK + expert * TOK + jnp.arange(TOK, dtype=jnp.int32))
    order = jnp.arange(1024, dtype=jnp.int32)
    half_cos, half_sin = rope_tables(context * BLOCK + order + (order // 64) * 64 + half * 64)

    hits = jnp.sum((routes[0, 0][:, :, None] == jnp.arange(EXPERTS, dtype=jnp.int32)).astype(f32), 1)
    lower = np.tril(np.ones((TOK, TOK), np.float32), -1)
    place = dot(jnp.asarray(lower, bf16), hits.astype(bf16))
    owner = np.repeat(np.eye(EXPERTS, dtype=np.float32), CAP, 0)
    owner16 = jnp.asarray(owner, bf16)
    slot_number = jnp.arange(SLOTS, dtype=jnp.int32) % CAP
    marked = jnp.where(hits > 0.5, place, 255.0).astype(bf16)
    spot = (dot_rows(marked, owner16) == slot_number[None, :].astype(f32)).astype(bf16)
    selector = (dot_rows(owner16, marked) == slot_number[:, None].astype(f32)).astype(bf16)

    act_send, q_send, kv_send = project(x, norm1_gain, w_query, w_key, w_value, cos, sin)
    kv_own = to_owners(kv_send).reshape(BLOCK, LANES)
    kv_left, kv_right = shift(kv_own, 1), shift(kv_own, 3)
    q_own = to_owners(after(q_send, kv_own))
    q_far = mirror(q_own[8:])
    far_a, far_b = shift(kv_left[: BLOCK // 2], 1), shift(kv_right[BLOCK // 2 :], 3)

    down = lax.all_gather(w_down, ("context", "dp"), axis=1, tiled=True)
    wide = jnp.concatenate([top, jnp.pad(marked, ((0, 0), (0, LANES - EXPERTS)))], 1)
    top_all = lax.all_gather(after(wide, q_far), "expert", axis=0, tiled=True)
    gate_up = lax.all_gather(w_gate_up, ("context", "dp"), axis=1, tiled=True)
    act_rows = to_owners(after(act_send, q_far, far_a, far_b)).reshape(1024, D)

    seat = jnp.stack([context, half, lax.axis_index("dp")]).astype(jnp.int32)
    o, o_low, o_far, lse, kv = attend_forward(
        seat, q_own, q_far, (kv_own, kv_left, far_a, far_b, kv_right)
    )
    o_far = after(o_far, act_rows)
    o_own = jnp.concatenate([o_low, mirror(o_far)], 0)
    att = to_owners(o_own)
    first = (2 * expert).astype(jnp.int32).reshape(1)
    top_rows, raw = raw_grads(first, top_all.reshape(16, TOK, D + LANES), down)

    hidden, send = middle(att, x, w_out, norm2_gain, selector)
    rows = after(to_owners(send.reshape(16, 2, CAP, D)), raw)
    grad_rows, expert_hidden, mixed, gates, logits, norm2_sum = experts(first, rows, raw, gate_up, w_router)
    back = to_owners(grad_rows)
    buffer, dgu, ddown = expert_grads(
        rows, top_rows, gates, logits, expert_hidden, mixed, down, norm2_sum, norm2_gain
    )
    state, buffer, do_send = turn_back(back.reshape(SLOTS, D), spot, hidden, norm2_gain, top, w_out, buffer)
    do_own = to_owners(do_send)
    do_far = mirror(do_own[8:])
    returned = to_owners(after(buffer, do_own))
    grad_gate_up = lax.psum_scatter(
        after(dgu, do_own), ("context", "dp"), scatter_dimension=1, tiled=True
    ).astype(f32)

    dq, dq_far, d0, d1a, d1b, d2a, d2b, d3a, d3b = attend_backward(seat, q_own, q_far, do_own, do_far, o, lse, kv)

    far_a, far_b = shift(d2a, 1), shift(d2b, 3)
    from_left_b, from_right_a = shift(d3b, 1), shift(d1a, 3)
    dq_far = mirror(after(dq_far, far_a, far_b))
    from_left_a = shift((d3a.astype(f32) + far_a.astype(f32)).astype(bf16), 1)
    from_right_b = shift((d1b.astype(f32) + far_b.astype(f32)).astype(bf16), 3)
    keep, give = merge(seat, d0, from_left_a, from_left_b, from_right_a, from_right_b)
    got = after(swap_halves(give), returned)
    grads = unturn_rows(dq, dq_far, keep, got, half_cos, half_sin)
    mine, other = head_grads(
        seat,
        act_rows,
        o_own.reshape(1024, LANES),
        grads,
        returned,
    )
    keep, give = split_halves(seat, mine, swap_cores(other))
    total = keep + jnp.pad(swap_halves(give), ((0, 16), (0, 0))).astype(f32)
    total = total.astype(bf16)
    total = (total.astype(f32) + neighbour(total).astype(f32)).astype(bf16)
    whole = to_owners(add_and_spread(total, mirror(total)))

    block_out = hidden + branch_scale * dot(spot, returned[:, :96].reshape(SLOTS, D))
    grad_down = lax.psum_scatter(after(ddown, got), ("context", "dp"), scatter_dimension=1, tiled=True).astype(f32)
    whole, block_out, grad_gate_up, grad_down = lax.optimization_barrier((whole, block_out, grad_gate_up, grad_down))
    grads_back = to_owners(after(grads, whole).reshape(16, 64, 256))
    grad_input = finish(grads_back, x, norm1_gain, w_query, w_key, w_value, state)
    weights = (w_query, w_key, w_value, norm1_gain)
    own_part = assemble(seat, 0, whole, *weights)
    dwq, dwk, dwv, dwo, norm1_grad = assemble(seat, 1, swap_cores(whole), *weights, before=own_part)
    small = whole[:, 384:].reshape(16, 4, 4, 256).transpose(0, 2, 1, 3).reshape(64, D).astype(f32)
    return (
        block_out.reshape(1, 1, TOK, D),
        grad_input.reshape(1, 1, TOK, D),
        norm1_grad[0],
        small[EXPERTS],
        dwq,
        dwk,
        dwv,
        dwo,
        small[:EXPERTS].T,
        grad_gate_up,
        grad_down,
    )


def solution(mesh):
    tokens = P("dp", "context", "expert", None)
    weights = P("expert", ("context", "dp"), None)
    return jax.shard_map(
        local,
        mesh=mesh,
        in_specs=(tokens, tokens, P(), P(), P(), P(), P(), P(), P(), weights, weights, tokens),
        out_specs=(tokens, tokens, P(), P(), P(), P(), P(), P(), P(), weights, weights),
        check_vma=False,
    )
```

```python
import jax
import jax.numpy as jnp
import numpy as np
from jax import lax
from jax.experimental import pallas as pl
from jax.experimental.pallas import tpu as pltpu
from jax.sharding import PartitionSpec as P

D = 1024
HEAD_DIM = 64
F = 512
EXPERTS = 32
CAP = 48
TOK = 128
BLOCK = 2048
LANES = 128
SLOTS = EXPERTS * CAP
PAIRS = 8
CHUNK = 512

norm_eps = 1e-06
score_scale = 0.015625
branch_scale = 0.22
rope_base = 10000.0
huge_negative = -1e30
bf16 = jnp.bfloat16
f32 = jnp.float32
VMEM_LIMIT = 56 * 1024 * 1024


def call(kernel, out_shape, flops, moved, **kw):
    return pl.pallas_call(
        kernel,
        out_shape=out_shape,
        compiler_params=pltpu.CompilerParams(vmem_limit_bytes=VMEM_LIMIT),
        cost_estimate=pl.CostEstimate(flops=int(flops), bytes_accessed=int(moved), transcendentals=0),
        **kw,
    )


def struct(shape, dtype):
    return jax.ShapeDtypeStruct(shape, dtype)


def dot(a, b):
    return jnp.dot(a, b, preferred_element_type=f32)


def dot_rows(a, b):
    return lax.dot_general(a, b, (((1,), (1,)), ((), ())), preferred_element_type=f32)


def dot_down(a, b):
    return lax.dot_general(a, b, (((0,), (0,)), ((), ())), preferred_element_type=f32)


def split2(x):
    hi = x.astype(bf16)
    return hi, (x - hi.astype(f32)).astype(bf16)


def lane_index(shape):
    return lax.broadcasted_iota(jnp.int32, shape, len(shape) - 1)


def project_kernel(x_ref, gain_ref, wq_ref, wk_ref, wv_ref, cos_ref, sin_ref, act_ref, q_ref, kv_ref):
    x = x_ref[...].astype(f32)
    inverse = lax.rsqrt(jnp.mean(x * x, axis=-1, keepdims=True) + norm_eps)
    act = (x * inverse * gain_ref[...]).astype(bf16)
    for e in range(16):
        act_ref[e] = act[64 * (e % 2) : 64 * (e % 2) + 64]
    cos = cos_ref[...]
    sin = sin_ref[...]
    lane = lane_index((TOK, LANES))
    first = lane % HEAD_DIM < HEAD_DIM // 2
    left = lane < HEAD_DIM

    def turn(v):
        moved = jnp.where(first, pltpu.roll(v, LANES - 32, 1), pltpu.roll(v, 32, 1))
        return v * cos + moved * sin

    q = dot(act, wq_ref[...])
    for j in range(PAIRS):
        rows = turn(q[:, j * LANES : (j + 1) * LANES]).astype(bf16)
        q_ref[2 * j] = rows[: TOK // 2]
        q_ref[2 * j + 1] = rows[TOK // 2 :]
    k = dot(act, wk_ref[...])
    v = dot(act, wv_ref[...])
    for b in range(PAIRS // 2):
        kb = turn(k[:, b * LANES : (b + 1) * LANES])
        vb = v[:, b * LANES : (b + 1) * LANES]
        even = jnp.where(left, kb, pltpu.roll(vb, HEAD_DIM, 1)).astype(bf16)
        odd = jnp.where(left, pltpu.roll(kb, HEAD_DIM, 1), vb).astype(bf16)
        kv_ref[4 * b] = even
        kv_ref[4 * b + 1] = even
        kv_ref[4 * b + 2] = odd
        kv_ref[4 * b + 3] = odd


def project(x, gain, wq, wk, wv, cos, sin):
    return call(
        project_kernel,
        (struct((16, 64, D), bf16), struct((16, 64, LANES), bf16), struct((16, TOK, LANES), bf16)),
        2 * TOK * D * 2048,
        6e6,
        name="project",
    )(x, gain.reshape(1, D), wq, wk, wv, cos, sin)


def query_of_head(q, head, left):
    q = q.astype(f32) * score_scale
    if head:
        q = pltpu.roll(q, HEAD_DIM, 1)
    return jnp.where(left, q, 0.0).astype(bf16)


def forward_kernel(
    place_ref, q_ref, q_far_ref, own_ref, left_ref, far_a_ref, far_b_ref, right_ref,
    o_ref, low_ref, low_far_ref, lse_ref, kv_ref, qm_ref, top_ref, acc_ref,
):
    tile = 1024
    context = place_ref[0]
    half = place_ref[1]

    def put(back, part, ref):
        start = lax.rem(context + 4 - back, 4) * BLOCK + part * (BLOCK // 2)
        rows = ref.shape[0]
        kv_ref[pl.ds(pl.multiple_of(start, BLOCK // 2), rows), :] = ref[...]

    put(0, 0, own_ref)
    put(1, 0, left_ref)
    put(2, 0, far_a_ref)
    put(2, 1, far_b_ref)
    put(3, 0, right_ref)
    left = lane_index((CHUNK, LANES)) < HEAD_DIM
    left_keys = lane_index((tile, LANES)) < HEAD_DIM
    for chunk in range(2):
        whole = 2 * (context if chunk == 0 else 3 - context) + chunk
        queries = (q_far_ref[...] if chunk else q_ref[:8]).reshape(CHUNK, LANES)
        for head in range(2):
            qm_ref[head] = query_of_head(queries, head, left)
            top_ref[head] = jnp.full((CHUNK, LANES), huge_negative, f32)
            acc_ref[head] = jnp.zeros((CHUNK, LANES), f32)

        def step(index, masked):
            keys = kv_ref[pl.ds(pl.multiple_of(index * tile, tile), tile), :]
            values = jnp.where(left_keys, jnp.ones_like(keys), keys)
            for head in range(2):
                for part in range(2):
                    rows = slice(part * 256, part * 256 + 256)
                    s = dot_rows(qm_ref[head, rows], keys)
                    if masked:
                        r = lax.broadcasted_iota(jnp.int32, s.shape, 0) + part * 256
                        place = r + (r // 64) * 64 + half * 64
                        s = jnp.where(lane_index(s.shape) <= place, s, huge_negative)
                    old = top_ref[head, rows]
                    new = jnp.maximum(old, jnp.max(s, axis=1, keepdims=True))
                    p = jnp.exp(s - new[:, :1]).astype(bf16)
                    acc_ref[head, rows] = acc_ref[head, rows] * jnp.exp(old - new) + dot(p, values)
                    top_ref[head, rows] = new

        def visit(index, carry):
            step(index, False)
            return carry

        lax.fori_loop(0, whole, visit, 0)
        step(whole, True)
        outs = []
        for head in range(2):
            acc = acc_ref[head]
            outs.append(pltpu.roll(acc, HEAD_DIM, 1) / acc)
            total = top_ref[head] + jnp.log(jnp.where(left, acc, 1.0))
            lse_ref[2 * chunk + head] = jnp.transpose(total)[0:8]
        o = jnp.where(left, outs[0], pltpu.roll(outs[1], HEAD_DIM, 1))
        o_ref[chunk] = o
        (low_far_ref if chunk else low_ref)[...] = o.astype(bf16).reshape(8, 64, LANES)


def attend_forward(place, q, q_far, kv_parts):
    smem = pl.BlockSpec(memory_space=pltpu.SMEM)
    vmem = pl.BlockSpec(memory_space=pltpu.VMEM)
    return call(
        forward_kernel,
        (
            struct((2, CHUNK, LANES), f32),
            struct((8, 64, LANES), bf16),
            struct((8, 64, LANES), bf16),
            struct((4, 8, CHUNK), f32),
            struct((4 * BLOCK, LANES), bf16),
        ),
        2e10,
        4e6,
        in_specs=[smem] + [vmem] * 7,
        out_specs=(vmem,) * 5,
        scratch_shapes=[
            pltpu.VMEM((2, CHUNK, LANES), bf16),
            pltpu.VMEM((2, CHUNK, LANES), f32),
            pltpu.VMEM((2, CHUNK, LANES), f32),
        ],
        name="attend",
    )(place, q, q_far, *kv_parts)


def backward_kernel(
    place_ref, q_ref, q_far_ref, do_ref, do_far_ref, o_ref, lse_ref, kv_ref,
    dq_ref, dq_far_ref, d0_ref, d1a_ref, d1b_ref, d2a_ref, d2b_ref, d3a_ref, d3b_ref,
    qm_ref, dom_ref, row_ref, dqt_ref, acc_ref,
):
    tile = 512
    context = place_ref[0]
    half = place_ref[1]
    left = lane_index((CHUNK, LANES)) < HEAD_DIM
    acc_ref[...] = jnp.zeros_like(acc_ref)
    for chunk in range(2):
        whole = 2 * (2 * (context if chunk == 0 else 3 - context) + chunk)
        queries = (q_far_ref[...] if chunk else q_ref[:8]).reshape(CHUNK, LANES)
        do = (do_far_ref[...] if chunk else do_ref[:8]).reshape(CHUNK, LANES).astype(f32)
        product = jnp.transpose(do * o_ref[chunk])
        for head in range(2):
            qm_ref[head] = query_of_head(queries, head, left)
            moved = do if head else pltpu.roll(do, HEAD_DIM, 1)
            dom_ref[head] = jnp.where(left, 0.0, moved).astype(bf16)
            dqt_ref[head] = jnp.zeros((LANES, CHUNK), f32)
            rows = product[head * HEAD_DIM : (head + 1) * HEAD_DIM]
            row_ref[head] = jnp.broadcast_to(jnp.sum(rows, axis=0, keepdims=True), (8, CHUNK))

        def step(index, offset):
            span = pl.ds(pl.multiple_of(index * tile, tile), tile)
            keys = kv_ref[span, :]
            for head in range(2):
                qm = qm_ref[head]
                dom = dom_ref[head]
                s = dot_rows(keys, qm)
                dp = dot_rows(keys, dom)
                p = jnp.exp(s - lse_ref[2 * chunk + head, 0:1])
                if offset is not None:
                    r = lane_index(s.shape)
                    place = r + (r // 64) * 64 + half * 64
                    key = lax.broadcasted_iota(jnp.int32, s.shape, 0) + offset
                    p = jnp.where(key <= place, p, 0.0)
                ds = (p * (dp - row_ref[head, 0:1])).astype(bf16)
                acc_ref[span, :] += dot(ds, qm) + dot(p.astype(bf16), dom)
                dqt_ref[head] += dot_down(keys, ds)

        def visit(index, carry):
            step(index, None)
            return carry

        lax.fori_loop(0, whole, visit, 0)
        step(whole, 0)
        step(whole + 1, tile)
        parts = [jnp.transpose(dqt_ref[head]) * score_scale for head in range(2)]
        dq = jnp.where(left, parts[0], pltpu.roll(parts[1], HEAD_DIM, 1)).astype(bf16)
        (dq_far_ref if chunk else dq_ref)[...] = dq.reshape(8, 64, LANES)
    d0_ref[...] = acc_ref[pl.ds(pl.multiple_of(context * BLOCK, BLOCK), BLOCK), :]
    for back, first, second in ((1, d1a_ref, d1b_ref), (2, d2a_ref, d2b_ref), (3, d3a_ref, d3b_ref)):
        start = pl.multiple_of(lax.rem(context + 4 - back, 4) * BLOCK, BLOCK)
        first[...] = acc_ref[pl.ds(start, BLOCK // 2), :].astype(bf16)
        second[...] = acc_ref[pl.ds(pl.multiple_of(start + BLOCK // 2, BLOCK // 2), BLOCK // 2), :].astype(bf16)


def attend_backward(place, q, q_far, do, do_far, o, lse, kv):
    smem = pl.BlockSpec(memory_space=pltpu.SMEM)
    vmem = pl.BlockSpec(memory_space=pltpu.VMEM)
    rows = kv.shape[0]
    return call(
        backward_kernel,
        (struct((8, 64, LANES), bf16), struct((8, 64, LANES), bf16), struct((BLOCK, LANES), f32))
        + (struct((BLOCK // 2, LANES), bf16),) * 6,
        5e10,
        8e6,
        in_specs=[smem] + [vmem] * 7,
        out_specs=(vmem,) * 9,
        scratch_shapes=[
            pltpu.VMEM((2, CHUNK, LANES), bf16),
            pltpu.VMEM((2, CHUNK, LANES), bf16),
            pltpu.VMEM((2, 8, CHUNK), f32),
            pltpu.VMEM((2, LANES, CHUNK), f32),
            pltpu.VMEM((rows, LANES), f32),
        ],
        name="attend_back",
    )(place, q, q_far, do, do_far, o, lse, kv)


def middle_kernel(att_ref, x_ref, wo_ref, gain_ref, pick_ref, hidden_ref, send_ref, attended_ref):
    for j in range(PAIRS):
        for h in range(2):
            attended_ref[h * 64 : h * 64 + 64, j * LANES : (j + 1) * LANES] = att_ref[2 * j + h]
    hidden = x_ref[...].astype(f32) + branch_scale * dot(attended_ref[...], wo_ref[...])
    hidden_ref[...] = hidden
    inverse = lax.rsqrt(jnp.mean(hidden * hidden, axis=-1, keepdims=True) + norm_eps)
    act = (hidden * inverse * gain_ref[...]).astype(bf16)
    send_ref[...] = dot(pick_ref[...], act).astype(bf16)


def middle(att, x, wo, gain, pick):
    return call(
        middle_kernel,
        (struct((TOK, D), f32), struct((SLOTS, D), bf16)),
        2 * TOK * D * (D + SLOTS),
        8e6,
        scratch_shapes=[pltpu.VMEM((TOK, D), bf16)],
        name="middle",
    )(att, x, wo, gain.reshape(1, D), pick)


def raw_kernel(first_ref, top_ref, down_ref, rows_ref, raw_ref):
    number = first_ref[0] + pl.program_id(0)
    chosen = (lane_index((8, LANES)) == number).astype(bf16)
    slot = lax.broadcasted_iota(jnp.int32, (CAP, TOK), 0).astype(f32)
    for n in range(16):
        place = dot_rows(chosen, top_ref[n, :, D:])[0:1]
        rows = dot((slot == place).astype(bf16), top_ref[n, :, :D])
        rows_ref[CAP * n : CAP * n + CAP] = rows.astype(bf16)
    raw_ref[...] = branch_scale * dot_rows(rows_ref[...], down_ref[...])


def raw_grads(first, top, down):
    return call(
        raw_kernel,
        (struct((2, 768, D), bf16), struct((2, 768, F), f32)),
        2 * SLOTS * D * F,
        1.2e7,
        grid=(2,),
        in_specs=[
            pl.BlockSpec(memory_space=pltpu.SMEM),
            pl.BlockSpec((16, TOK, D + LANES), lambda n: (0, 0, 0)),
            owned(F, D),
        ],
        out_specs=(owned(768, D), owned(768, F)),
        name="raw",
    )(first, top, down)


def expert_kernel(
    first_ref, x_ref, raw_ref, gu_ref, wr_ref, back_ref, hidden_ref, mixed_ref, gate_ref, logit_ref, norm_ref
):
    number = first_ref[0] + pl.program_id(0)
    wr = wr_ref[...]
    for part in range(2):
        take = slice(8 * part, 8 * part + 8)
        rows = slice(384 * part, 384 * part + 384)
        x = x_ref[take].reshape(384, D)
        logits = dot(x, wr)
        raised = jnp.exp(logits - jnp.max(logits, axis=-1, keepdims=True))
        probs = raised / jnp.sum(raised, axis=-1, keepdims=True)
        chosen = (lane_index(probs.shape) == number).astype(f32)
        gate_value = jnp.sum(probs * chosen, axis=-1, keepdims=True)
        gate_ref[rows] = gate_value
        pre = dot(x, gu_ref[...])
        raw = raw_ref[rows]
        gate = pre[:, :F]
        up = pre[:, F:]
        sig = 1.0 / (1.0 + jnp.exp(-gate))
        act = gate * sig
        hidden = (act * up).astype(bf16)
        hidden_ref[rows] = hidden
        grad_gate = jnp.sum(hidden.astype(f32) * raw, axis=-1, keepdims=True)
        grad_logits = (gate_value * grad_gate) * (chosen - probs)
        logit_ref[rows] = grad_logits
        raw = raw * gate_value
        mixed_gate = (raw * up * sig * (1.0 + gate * (1.0 - sig))).astype(bf16)
        mixed_up = (raw * act).astype(bf16)
        mixed_ref[rows, :F] = mixed_gate
        mixed_ref[rows, F:] = mixed_up
        hi, lo = split2(grad_logits)
        back = dot_rows(mixed_gate, gu_ref[:, :F]) + dot_rows(mixed_up, gu_ref[:, F:])
        back = back + dot_rows(hi, wr) + dot_rows(lo, wr)
        back_ref[take] = back.astype(bf16).reshape(8, CAP, D)
        product = jnp.sum(back * x.astype(f32), axis=0, keepdims=True)
        if part == 0:
            norm_ref[...] = jnp.broadcast_to(product, (8, D))
        else:
            norm_ref[...] += product


def owned(*shape):
    return pl.BlockSpec((None, *shape), lambda n: (n, *([0] * len(shape))))


def experts(first, x, raw, gate_up, wr):
    per = pl.BlockSpec((16, None, CAP, D), lambda n: (0, n, 0, 0))
    return call(
        expert_kernel,
        (
            struct((16, 2, CAP, D), bf16),
            struct((2, 768, F), bf16),
            struct((2, 768, D), bf16),
            struct((2, 768, 1), f32),
            struct((2, 768, EXPERTS), f32),
            struct((2, 8, D), f32),
        ),
        2 * SLOTS * D * 2560,
        2e7,
        grid=(2,),
        in_specs=[
            pl.BlockSpec(memory_space=pltpu.SMEM),
            per,
            owned(768, F),
            owned(D, D),
            pl.BlockSpec((D, EXPERTS), lambda n: (0, 0)),
        ],
        out_specs=(per, owned(768, F), owned(768, D), owned(768, 1), owned(768, EXPERTS), owned(8, D)),
        name="experts",
    )(first, x, raw, gate_up, wr)


def expert_grads_kernel(
    x_ref, top_ref, gate_ref, logit_ref, hidden_ref, mixed_ref, down_ref, norm_ref, gain_ref,
    out_ref, dgu_ref, ddown_ref, router_ref,
):
    n = pl.program_id(0)
    hidden = hidden_ref[...]
    gate = gate_ref[...]
    x = x_ref[...].reshape(768, D)
    out = (gate * dot(hidden, down_ref[...])).astype(bf16).reshape(16, CAP, D)
    out_ref[:, pl.ds(pl.multiple_of(n * CAP, 16), CAP), :] = out
    top = (branch_scale * gate * top_ref[...].astype(f32)).astype(bf16)
    ddown_ref[...] = dot_down(hidden, top).astype(bf16)
    dgu_ref[...] = dot_down(x, mixed_ref[...]).astype(bf16)
    hi, lo = split2(logit_ref[...])
    router = dot_down(hi, x) + dot_down(lo, x)

    @pl.when(n == 0)
    def _():
        router_ref[...] = router

    @pl.when(n == 1)
    def _():
        total = router_ref[...] + router
        norm = (norm_ref[0, 0:1] + norm_ref[1, 0:1]) / gain_ref[...]
        for e in range(16):
            if e < 8:
                extra = jnp.concatenate([total[4 * e : 4 * e + 4], jnp.zeros((12, D), f32)], axis=0)
            elif e == 8:
                extra = jnp.concatenate([norm, jnp.zeros((15, D), f32)], axis=0)
            else:
                extra = jnp.zeros((16, D), f32)
            out_ref[e, 96:112] = extra.astype(bf16)


def expert_grads(x, top, gate, logits, hidden, mixed, down, norm, gain):
    per = pl.BlockSpec((16, None, CAP, D), lambda n: (0, n, 0, 0))
    return call(
        expert_grads_kernel,
        (struct((16, 176, D), bf16), struct((2, D, D), bf16), struct((2, F, D), bf16)),
        2 * SLOTS * D * 2048,
        2.4e7,
        grid=(2,),
        in_specs=[
            per,
            owned(768, D),
            owned(768, 1),
            owned(768, EXPERTS),
            owned(768, F),
            owned(768, D),
            owned(F, D),
            pl.BlockSpec((2, 8, D), lambda n: (0, 0, 0)),
            pl.BlockSpec((1, D), lambda n: (0, 0)),
        ],
        out_specs=(pl.BlockSpec((16, 176, D), lambda n: (0, 0, 0)), owned(D, D), owned(F, D)),
        scratch_shapes=[pltpu.VMEM((EXPERTS, D), f32)],
        name="expert_grads",
    )(x, top, gate, logits, hidden, mixed, down, norm, gain.reshape(1, D))


def turn_back_kernel(
    back_ref, spot_ref, hidden_ref, gain_ref, top_ref, wo_ref, before_ref,
    state_ref, buffer_ref, send_ref, attn_ref, done_ref,
):
    grad = dot(spot_ref[...], back_ref[...])
    hidden = hidden_ref[...]
    inverse = lax.rsqrt(jnp.mean(hidden * hidden, axis=-1, keepdims=True) + norm_eps)
    normed = hidden * inverse
    scaled = grad * gain_ref[...]
    state = top_ref[...].astype(f32) + inverse * (scaled - normed * jnp.mean(scaled * normed, axis=-1, keepdims=True))
    state_ref[...] = state
    attn = (branch_scale * state).astype(bf16)
    for e in range(16):
        attn_ref[e] = attn[64 * (e % 2) : 64 * (e % 2) + 64]
    copy = pltpu.make_async_copy(attn_ref, buffer_ref.at[:, pl.ds(112, 64), :], done_ref)
    copy.start()
    attended = dot_rows(attn, wo_ref[...]).astype(bf16)
    for j in range(PAIRS):
        for h in range(2):
            send_ref[2 * j + h] = attended[h * 64 : h * 64 + 64, j * LANES : (j + 1) * LANES]
    copy.wait()


def turn_back(back, spot, hidden, gain, top, wo, buffer):
    vmem = pl.BlockSpec(memory_space=pltpu.VMEM)
    outside = pl.BlockSpec(memory_space=pl.ANY)
    return call(
        turn_back_kernel,
        (
            struct((TOK, D), f32),
            struct((16, 176, D), bf16),
            struct((16, TOK // 2, LANES), bf16),
        ),
        2 * 256 * D * (D + SLOTS),
        8e6,
        in_specs=[vmem] * 6 + [outside],
        out_specs=(vmem, outside, vmem),
        scratch_shapes=[pltpu.VMEM((16, 64, D), bf16), pltpu.SemaphoreType.DMA],
        input_output_aliases={6: 1},
        name="turn_back",
    )(back, spot, hidden, gain.reshape(1, D), top, wo, buffer)


def unturn(v, cos, sin, first):
    scaled = v * sin
    return v * cos + jnp.where(first, pltpu.roll(scaled, LANES - 32, 1), pltpu.roll(scaled, 32, 1))


def merge_kernel(
    place_ref, d0_ref, left_a_ref, left_b_ref, right_a_ref, right_b_ref, keep_ref, give_ref, sum_ref
):
    half = place_ref[1]
    for part, left, right in ((0, left_a_ref, right_a_ref), (1, left_b_ref, right_b_ref)):
        rows = slice(part * 1024, part * 1024 + 1024)
        total = d0_ref[rows] + left[...].astype(f32) + right[...].astype(f32)
        sum_ref[8 * part : 8 * part + 8] = total.reshape(8, TOK, LANES)
    keep_ref[...] = sum_ref[:, pl.ds(pl.multiple_of(half * 64, 64), 64), :]
    give_ref[...] = sum_ref[:, pl.ds(pl.multiple_of((1 - half) * 64, 64), 64), :].astype(bf16)


def merge(place, *pieces):
    smem = pl.BlockSpec(memory_space=pltpu.SMEM)
    vmem = pl.BlockSpec(memory_space=pltpu.VMEM)
    return call(
        merge_kernel,
        (struct((16, 64, LANES), f32), struct((16, 64, LANES), bf16)),
        1e6,
        3e6,
        in_specs=[smem] + [vmem] * 5,
        out_specs=(vmem, vmem),
        scratch_shapes=[pltpu.VMEM((16, TOK, LANES), f32)],
        name="merge",
    )(place, *pieces)


def unturn_kernel(dq_ref, dq_far_ref, keep_ref, got_ref, cos_ref, sin_ref, grads_ref):
    lane = lane_index((512, LANES))
    first = lane % HEAD_DIM < HEAD_DIM // 2
    for part, dq in ((0, dq_ref), (1, dq_far_ref)):
        rows = slice(512 * part, 512 * part + 512)
        take = slice(8 * part, 8 * part + 8)
        cos = cos_ref[rows]
        sin = sin_ref[rows]
        grads_ref[rows, :LANES] = unturn(dq[...].reshape(512, LANES).astype(f32), cos, sin, first).astype(bf16)
        both = (keep_ref[take] + got_ref[take].astype(f32)).reshape(512, LANES).astype(bf16).astype(f32)
        grads_ref[rows, LANES:] = jnp.where(lane < HEAD_DIM, unturn(both, cos, sin, first), both).astype(bf16)


def unturn_rows(dq, dq_far, keep, got, cos, sin):
    return call(unturn_kernel, struct((1024, 256), bf16), 1e6, 3e6, name="unturn")(dq, dq_far, keep, got, cos, sin)


def head_kernel(
    place_ref, act_ref, o_ref, grads_ref, extra_ref, a0_ref, a1_ref, a2_ref, a3_ref, mine_ref, other_ref, all_ref, attn_ref
):
    grads = dot_down(act_ref[...], grads_ref[...]).astype(bf16)
    for part, ref in enumerate((a0_ref, a1_ref, a2_ref, a3_ref)):
        attn_ref[:, 16 * part : 16 * part + 16, :] = ref[...]
    out = dot_down(o_ref[...], attn_ref[...].reshape(1024, D)).astype(bf16)
    for quarter in range(4):
        start = 384 * quarter
        all_ref[start : start + 256] = grads[256 * quarter : 256 * quarter + 256]
        all_ref[start + 256 : start + 384] = out[:, 256 * quarter : 256 * quarter + 256]
    extra = extra_ref[0].astype(f32)
    for e in range(1, 16):
        extra = extra + extra_ref[e].astype(f32)
    packed = extra[:, :256]
    for b in range(1, 4):
        packed = packed + pltpu.roll(extra[:, 256 * b : 256 * (b + 1)], 4 * b, 0)
    packed = packed.astype(bf16)
    core = place_ref[2]
    for which, out_ref in ((1 - core, other_ref), (core, mine_ref)):
        out_ref[:768] = all_ref[pl.ds(pl.multiple_of(which * 768, 768), 768), :]
        out_ref[768:] = packed


def head_grads(place, act, o, grads, returned):
    whole = lambda *shape: pl.BlockSpec(shape, lambda i, place: (0,) * len(shape))
    half = struct((784, 256), bf16)
    return call(
        head_kernel,
        (half, half),
        2 * 1024 * 1024 * 512,
        8e6,
        grid_spec=pltpu.PrefetchScalarGridSpec(
            num_scalar_prefetch=1,
            grid=(1,),
            in_specs=[
                whole(1024, D),
                whole(1024, LANES),
                whole(1024, 256),
                pl.BlockSpec((16, 16, D), lambda i, place: (0, 6, 0)),
                pl.BlockSpec((16, 16, D), lambda i, place: (0, 7, 0)),
                pl.BlockSpec((16, 16, D), lambda i, place: (0, 8, 0)),
                pl.BlockSpec((16, 16, D), lambda i, place: (0, 9, 0)),
                pl.BlockSpec((16, 16, D), lambda i, place: (0, 10, 0)),
            ],
            out_specs=(whole(784, 256), whole(784, 256)),
            scratch_shapes=[pltpu.VMEM((1536, 256), bf16), pltpu.VMEM((16, 64, D), bf16)],
        ),
        name="head_grads",
    )(place, act, o, grads, *([returned] * 5))


def split_kernel(place_ref, mine_ref, other_ref, keep_ref, give_ref):
    half = place_ref[1]
    rows = pl.ds(pl.multiple_of(half * 384, 384), 384)
    keep_ref[:384] = mine_ref[rows, :].astype(f32) + other_ref[rows, :].astype(f32)
    keep_ref[384:] = mine_ref[768:, :].astype(f32) + other_ref[768:, :].astype(f32)
    rows = pl.ds(pl.multiple_of((1 - half) * 384, 384), 384)
    give_ref[...] = (mine_ref[rows, :].astype(f32) + other_ref[rows, :].astype(f32)).astype(bf16)


def split_halves(place, mine, other):
    smem = pl.BlockSpec(memory_space=pltpu.SMEM)
    vmem = pl.BlockSpec(memory_space=pltpu.VMEM)
    return call(
        split_kernel,
        (struct((400, 256), f32), struct((384, 256), bf16)),
        1e6,
        2e6,
        in_specs=[smem, vmem, vmem],
        out_specs=(vmem, vmem),
        name="split",
    )(place, mine, other)


def finish_kernel(grads_ref, x_ref, gain_ref, wq_ref, wk_ref, wv_ref, state_ref, out_ref, flat_ref):
    left = lane_index((TOK // 2, LANES)) < HEAD_DIM
    for h in range(2):
        rows = slice(64 * h, 64 * h + 64)
        for j in range(PAIRS):
            flat_ref[rows, j * LANES : (j + 1) * LANES] = grads_ref[2 * j + h, :, :LANES]
        for b in range(PAIRS // 2):
            even = grads_ref[4 * b + h, :, LANES:].astype(f32)
            odd = grads_ref[4 * b + 2 + h, :, LANES:].astype(f32)
            k = jnp.where(left, even, pltpu.roll(odd, HEAD_DIM, 1))
            v = jnp.where(left, pltpu.roll(even, HEAD_DIM, 1), odd)
            flat_ref[rows, D + b * LANES : D + (b + 1) * LANES] = k.astype(bf16)
            flat_ref[rows, D + 512 + b * LANES : D + 512 + (b + 1) * LANES] = v.astype(bf16)
    grad = dot_rows(flat_ref[:, :D], wq_ref[...])
    grad = grad + dot_rows(flat_ref[:, D : D + 512], wk_ref[...])
    grad = grad + dot_rows(flat_ref[:, D + 512 :], wv_ref[...])
    x = x_ref[...].astype(f32)
    inverse = lax.rsqrt(jnp.mean(x * x, axis=-1, keepdims=True) + norm_eps)
    normed = x * inverse
    scaled = grad * gain_ref[...]
    out_ref[...] = state_ref[...] + inverse * (scaled - normed * jnp.mean(scaled * normed, axis=-1, keepdims=True))


def finish(grads, x, gain, wq, wk, wv, state):
    return call(
        finish_kernel,
        struct((TOK, D), f32),
        2 * 256 * D * 2048,
        8e6,
        scratch_shapes=[pltpu.VMEM((TOK, 2048), bf16)],
        name="finish",
    )(grads, x, gain.reshape(1, D), wq, wk, wv, state)


def assemble_kernel(place_ref, piece, wq_ref, wk_ref, wv_ref, gain_ref, *refs):
    q_ref, k_ref, v_ref, o_ref, norm_ref = refs[-5:]
    left = lane_index((256, LANES)) < HEAD_DIM
    total = jnp.zeros((256, LANES), f32)
    for j in range(PAIRS):
        lanes = slice(j * LANES, (j + 1) * LANES)
        value = piece[j, :256, :LANES].astype(f32)
        q_ref[:, lanes] = value
        total = total + value * wq_ref[:, lanes].astype(f32)
        o_ref[lanes, :] = piece[j, 256:384, :].astype(f32)
    for b in range(PAIRS // 2):
        lanes = slice(b * LANES, (b + 1) * LANES)
        even = piece[2 * b, :256, LANES:].astype(f32)
        odd = piece[2 * b + 1, :256, LANES:].astype(f32)
        k = jnp.where(left, even, pltpu.roll(odd, HEAD_DIM, 1))
        v = jnp.where(left, pltpu.roll(even, HEAD_DIM, 1), odd)
        k_ref[:, lanes] = k
        v_ref[:, lanes] = v
        total = total + k * wk_ref[:, lanes].astype(f32) + v * wv_ref[:, lanes].astype(f32)
    norm_ref[...] = jnp.sum(jnp.transpose(total), axis=0, keepdims=True) / gain_ref[...]


def assemble(place, core, pieces, wq, wk, wv, gain, before=()):
    def quarter(i, place):
        return 2 * (place[2] if core == 0 else 1 - place[2]) + i

    rows = lambda width: pl.BlockSpec((256, width), lambda i, place: (quarter(i, place), 0))
    columns = lambda height: pl.BlockSpec((height, 256), lambda i, place: (0, quarter(i, place)))
    return call(
        assemble_kernel,
        (
            struct((D, D), f32),
            struct((D, 512), f32),
            struct((D, 512), f32),
            struct((D, D), f32),
            struct((1, D), f32),
        ),
        1e6,
        1.1e7,
        grid_spec=pltpu.PrefetchScalarGridSpec(
            num_scalar_prefetch=1,
            grid=(2,),
            in_specs=[
                pl.BlockSpec((PAIRS, None, 400, 256), lambda i, place: (0, i, 0, 0)),
                rows(D),
                rows(512),
                rows(512),
                columns(1),
            ]
            + [pl.BlockSpec(memory_space=pl.ANY)] * len(before),
            out_specs=(rows(D), rows(512), rows(512), columns(D), columns(1)),
        ),
        input_output_aliases={6 + i: i for i in range(len(before))},
        name="assemble",
    )(place, pieces.reshape(PAIRS, 2, 400, 256), wq, wk, wv, gain.reshape(1, D), *before)


def spread_kernel(a_ref, b_ref, out_ref):
    total = (a_ref[...].astype(f32) + b_ref[...].astype(f32)).astype(bf16)
    for e in range(16):
        out_ref[e] = total


def add_and_spread(a, b):
    return call(spread_kernel, struct((16, 400, 256), bf16), 1e6, 4e6, name="spread")(a, b)


def after(x, *earlier):
    return lax.optimization_barrier((x, *earlier))[0]


def to_owners(x):
    return lax.all_to_all(x, "expert", split_axis=0, concat_axis=0, tiled=True)


def mirror(x):
    return lax.ppermute(x, "context", [(0, 3), (1, 2), (2, 1), (3, 0)])


def swap_cores(x):
    return lax.ppermute(x, "dp", [(0, 1), (1, 0)])


def shift(x, by):
    return lax.ppermute(x, "context", [(i, (i + by) % 4) for i in range(4)])


def neighbour(x):
    return lax.ppermute(x, "context", [(0, 1), (1, 0), (2, 3), (3, 2)])


def swap_halves(x):
    return lax.ppermute(x, "expert", [(i, i ^ 1) for i in range(16)])


def pick(x, index, axis=0):
    return lax.dynamic_index_in_dim(x, index, axis, False)


def rope_tables(positions):
    frequency = rope_base ** (-jnp.arange(0, HEAD_DIM, 2, dtype=f32) / HEAD_DIM)
    angles = positions.astype(f32)[:, None] * frequency[None, :]
    cos, sin = jnp.cos(angles), jnp.sin(angles)
    return jnp.concatenate([cos] * 4, -1), jnp.concatenate([-sin, sin] * 2, -1)


def local(
    layer_input, grad_output, norm1_gain, norm2_gain, w_query, w_key, w_value, w_out, w_router, w_gate_up, w_down, routes
):
    context = lax.axis_index("context")
    expert = lax.axis_index("expert")
    x = layer_input[0, 0]
    top = grad_output[0, 0]

    half = expert % 2

    cos, sin = rope_tables(context * BLOCK + expert * TOK + jnp.arange(TOK, dtype=jnp.int32))
    order = jnp.arange(1024, dtype=jnp.int32)
    half_cos, half_sin = rope_tables(context * BLOCK + order + (order // 64) * 64 + half * 64)

    hits = jnp.sum((routes[0, 0][:, :, None] == jnp.arange(EXPERTS, dtype=jnp.int32)).astype(f32), 1)
    lower = np.tril(np.ones((TOK, TOK), np.float32), -1)
    place = dot(jnp.asarray(lower, bf16), hits.astype(bf16))
    owner = np.repeat(np.eye(EXPERTS, dtype=np.float32), CAP, 0)
    owner16 = jnp.asarray(owner, bf16)
    slot_number = jnp.arange(SLOTS, dtype=jnp.int32) % CAP
    marked = jnp.where(hits > 0.5, place, 255.0).astype(bf16)
    spot = (dot_rows(marked, owner16) == slot_number[None, :].astype(f32)).astype(bf16)
    selector = (dot_rows(owner16, marked) == slot_number[:, None].astype(f32)).astype(bf16)

    act_send, q_send, kv_send = project(x, norm1_gain, w_query, w_key, w_value, cos, sin)
    kv_own = to_owners(kv_send).reshape(BLOCK, LANES)
    kv_left, kv_right = shift(kv_own, 1), shift(kv_own, 3)
    q_own = to_owners(after(q_send, kv_own))
    q_far = mirror(q_own[8:])
    far_a, far_b = shift(kv_left[: BLOCK // 2], 1), shift(kv_right[BLOCK // 2 :], 3)

    down = lax.all_gather(w_down, ("context", "dp"), axis=1, tiled=True)
    wide = jnp.concatenate([top, jnp.pad(marked, ((0, 0), (0, LANES - EXPERTS)))], 1)
    top_all = lax.all_gather(wide, "expert", axis=0, tiled=True)
    gate_up = lax.all_gather(w_gate_up, ("context", "dp"), axis=1, tiled=True)

    seat = jnp.stack([context, half, lax.axis_index("dp")]).astype(jnp.int32)
    o, o_low, o_far, lse, kv = attend_forward(
        seat, q_own, q_far, (kv_own, kv_left, far_a, far_b, kv_right)
    )
    o_own = jnp.concatenate([o_low, mirror(o_far)], 0)
    att = to_owners(o_own)
    first = (2 * expert).astype(jnp.int32).reshape(1)
    top_rows, raw = raw_grads(first, top_all.reshape(16, TOK, D + LANES), down)

    hidden, send = middle(att, x, w_out, norm2_gain, selector)
    rows = after(to_owners(send.reshape(16, 2, CAP, D)), raw)
    act_rows = to_owners(after(act_send, rows)).reshape(1024, D)
    grad_rows, expert_hidden, mixed, gates, logits, norm2_sum = experts(first, rows, raw, gate_up, w_router)
    back = to_owners(after(grad_rows, act_rows))
    buffer, dgu, ddown = expert_grads(
        rows, top_rows, gates, logits, expert_hidden, mixed, down, norm2_sum, norm2_gain
    )
    state, buffer, do_send = turn_back(back.reshape(SLOTS, D), spot, hidden, norm2_gain, top, w_out, buffer)
    do_own = to_owners(do_send)
    do_far = mirror(do_own[8:])
    returned = to_owners(after(buffer, do_own))
    grad_gate_up = lax.psum_scatter(
        after(dgu, do_own), ("context", "dp"), scatter_dimension=1, tiled=True
    ).astype(f32)

    dq, dq_far, d0, d1a, d1b, d2a, d2b, d3a, d3b = attend_backward(seat, q_own, q_far, do_own, do_far, o, lse, kv)

    far_a, far_b = shift(d2a, 1), shift(d2b, 3)
    from_left_b, from_right_a = shift(d3b, 1), shift(d1a, 3)
    dq_far = mirror(after(dq_far, far_a, far_b))
    from_left_a = shift((d3a.astype(f32) + far_a.astype(f32)).astype(bf16), 1)
    from_right_b = shift((d1b.astype(f32) + far_b.astype(f32)).astype(bf16), 3)
    keep, give = merge(seat, d0, from_left_a, from_left_b, from_right_a, from_right_b)
    got = after(swap_halves(give), returned)
    grads = unturn_rows(dq, dq_far, keep, got, half_cos, half_sin)
    mine, other = head_grads(
        seat,
        act_rows,
        o_own.reshape(1024, LANES),
        grads,
        returned,
    )
    keep, give = split_halves(seat, mine, swap_cores(other))
    total = keep + jnp.pad(swap_halves(give), ((0, 16), (0, 0))).astype(f32)
    total = total.astype(bf16)
    total = (total.astype(f32) + neighbour(total).astype(f32)).astype(bf16)
    grads_back = to_owners(grads.reshape(16, 64, 256))
    block = after(add_and_spread(total, mirror(total)), grads_back)
    whole = to_owners(block)
    grad_input = finish(grads_back, x, norm1_gain, w_query, w_key, w_value, state)

    block_out = hidden + branch_scale * dot(spot, returned[:, :96].reshape(SLOTS, D))
    grad_down = lax.psum_scatter(after(ddown, block), ("context", "dp"), scatter_dimension=1, tiled=True).astype(f32)
    whole, grad_input, block_out, grad_gate_up, grad_down = lax.optimization_barrier(
        (whole, grad_input, block_out, grad_gate_up, grad_down)
    )
    weights = (w_query, w_key, w_value, norm1_gain)
    own_part = assemble(seat, 0, whole, *weights)
    dwq, dwk, dwv, dwo, norm1_grad = assemble(seat, 1, swap_cores(whole), *weights, before=own_part)
    small = after(whole, own_part[4])[:, 384:].reshape(16, 4, 4, 256).transpose(0, 2, 1, 3).reshape(64, D).astype(f32)
    return (
        block_out.reshape(1, 1, TOK, D),
        grad_input.reshape(1, 1, TOK, D),
        norm1_grad[0],
        small[EXPERTS],
        dwq,
        dwk,
        dwv,
        dwo,
        small[:EXPERTS].T,
        grad_gate_up,
        grad_down,
    )


def solution(mesh):
    tokens = P("dp", "context", "expert", None)
    weights = P("expert", ("context", "dp"), None)
    return jax.shard_map(
        local,
        mesh=mesh,
        in_specs=(tokens, tokens, P(), P(), P(), P(), P(), P(), P(), weights, weights, tokens),
        out_specs=(tokens, tokens, P(), P(), P(), P(), P(), P(), P(), weights, weights),
        check_vma=False,
    )
```

```python
import jax
import jax.numpy as jnp
import numpy as np
from jax import lax
from jax.experimental import pallas as pl
from jax.experimental.pallas import tpu as pltpu
from jax.sharding import PartitionSpec as P

D = 1024
HEAD_DIM = 64
F = 512
EXPERTS = 32
CAP = 48
TOK = 128
BLOCK = 2048
LANES = 128
SLOTS = EXPERTS * CAP
PAIRS = 8
CHUNK = 512

norm_eps = 1e-06
score_scale = 0.015625
branch_scale = 0.22
rope_base = 10000.0
huge_negative = -1e30
bf16 = jnp.bfloat16
f32 = jnp.float32
VMEM_LIMIT = 56 * 1024 * 1024


def call(kernel, out_shape, flops, moved, **kw):
    return pl.pallas_call(
        kernel,
        out_shape=out_shape,
        compiler_params=pltpu.CompilerParams(vmem_limit_bytes=VMEM_LIMIT),
        cost_estimate=pl.CostEstimate(flops=int(flops), bytes_accessed=int(moved), transcendentals=0),
        **kw,
    )


def struct(shape, dtype):
    return jax.ShapeDtypeStruct(shape, dtype)


def dot(a, b):
    return jnp.dot(a, b, preferred_element_type=f32)


def dot_rows(a, b):
    return lax.dot_general(a, b, (((1,), (1,)), ((), ())), preferred_element_type=f32)


def dot_down(a, b):
    return lax.dot_general(a, b, (((0,), (0,)), ((), ())), preferred_element_type=f32)


def split2(x):
    hi = x.astype(bf16)
    return hi, (x - hi.astype(f32)).astype(bf16)


def lane_index(shape):
    return lax.broadcasted_iota(jnp.int32, shape, len(shape) - 1)


def project_kernel(x_ref, gain_ref, wq_ref, wk_ref, wv_ref, cos_ref, sin_ref, act_ref, q_ref, kv_ref):
    x = x_ref[...].astype(f32)
    inverse = lax.rsqrt(jnp.mean(x * x, axis=-1, keepdims=True) + norm_eps)
    act = (x * inverse * gain_ref[...]).astype(bf16)
    for e in range(16):
        act_ref[e] = act[64 * (e % 2) : 64 * (e % 2) + 64]
    cos = cos_ref[...]
    sin = sin_ref[...]
    lane = lane_index((TOK, LANES))
    first = lane % HEAD_DIM < HEAD_DIM // 2
    left = lane < HEAD_DIM

    def turn(v):
        moved = jnp.where(first, pltpu.roll(v, LANES - 32, 1), pltpu.roll(v, 32, 1))
        return v * cos + moved * sin

    q = dot(act, wq_ref[...])
    for j in range(PAIRS):
        rows = turn(q[:, j * LANES : (j + 1) * LANES]).astype(bf16)
        q_ref[2 * j] = rows[: TOK // 2]
        q_ref[2 * j + 1] = rows[TOK // 2 :]
    k = dot(act, wk_ref[...])
    v = dot(act, wv_ref[...])
    for b in range(PAIRS // 2):
        kb = turn(k[:, b * LANES : (b + 1) * LANES])
        vb = v[:, b * LANES : (b + 1) * LANES]
        even = jnp.where(left, kb, pltpu.roll(vb, HEAD_DIM, 1)).astype(bf16)
        odd = jnp.where(left, pltpu.roll(kb, HEAD_DIM, 1), vb).astype(bf16)
        kv_ref[4 * b] = even
        kv_ref[4 * b + 1] = even
        kv_ref[4 * b + 2] = odd
        kv_ref[4 * b + 3] = odd


def project(x, gain, wq, wk, wv, cos, sin):
    return call(
        project_kernel,
        (struct((16, 64, D), bf16), struct((16, 64, LANES), bf16), struct((16, TOK, LANES), bf16)),
        2 * TOK * D * 2048,
        6e6,
        name="project",
    )(x, gain.reshape(1, D), wq, wk, wv, cos, sin)


def query_of_head(q, head, left):
    q = q.astype(f32) * score_scale
    if head:
        q = pltpu.roll(q, HEAD_DIM, 1)
    return jnp.where(left, q, 0.0).astype(bf16)


def forward_kernel(
    place_ref, q_ref, q_far_ref, own_ref, left_ref, far_a_ref, far_b_ref, right_ref,
    o_ref, low_ref, low_far_ref, lse_ref, kv_ref, qm_ref, top_ref, acc_ref,
):
    tile = 1024
    context = place_ref[0]
    half = place_ref[1]

    def put(back, part, ref):
        start = lax.rem(context + 4 - back, 4) * BLOCK + part * (BLOCK // 2)
        rows = ref.shape[0]
        kv_ref[pl.ds(pl.multiple_of(start, BLOCK // 2), rows), :] = ref[...]

    put(0, 0, own_ref)
    put(1, 0, left_ref)
    put(2, 0, far_a_ref)
    put(2, 1, far_b_ref)
    put(3, 0, right_ref)
    left = lane_index((CHUNK, LANES)) < HEAD_DIM
    left_keys = lane_index((tile, LANES)) < HEAD_DIM
    for chunk in range(2):
        whole = 2 * (context if chunk == 0 else 3 - context) + chunk
        queries = (q_far_ref[...] if chunk else q_ref[:8]).reshape(CHUNK, LANES)
        for head in range(2):
            qm_ref[head] = query_of_head(queries, head, left)
            top_ref[head] = jnp.full((CHUNK, LANES), huge_negative, f32)
            acc_ref[head] = jnp.zeros((CHUNK, LANES), f32)

        def step(index, masked):
            keys = kv_ref[pl.ds(pl.multiple_of(index * tile, tile), tile), :]
            values = jnp.where(left_keys, jnp.ones_like(keys), keys)
            for head in range(2):
                for part in range(2):
                    rows = slice(part * 256, part * 256 + 256)
                    s = dot_rows(qm_ref[head, rows], keys)
                    if masked:
                        r = lax.broadcasted_iota(jnp.int32, s.shape, 0) + part * 256
                        place = r + (r // 64) * 64 + half * 64
                        s = jnp.where(lane_index(s.shape) <= place, s, huge_negative)
                    old = top_ref[head, rows]
                    new = jnp.maximum(old, jnp.max(s, axis=1, keepdims=True))
                    p = jnp.exp(s - new[:, :1]).astype(bf16)
                    acc_ref[head, rows] = acc_ref[head, rows] * jnp.exp(old - new) + dot(p, values)
                    top_ref[head, rows] = new

        def visit(index, carry):
            step(index, False)
            return carry

        lax.fori_loop(0, whole, visit, 0)
        step(whole, True)
        outs = []
        for head in range(2):
            acc = acc_ref[head]
            outs.append(pltpu.roll(acc, HEAD_DIM, 1) / acc)
            total = top_ref[head] + jnp.log(jnp.where(left, acc, 1.0))
            lse_ref[2 * chunk + head] = jnp.transpose(total)[0:8]
        o = jnp.where(left, outs[0], pltpu.roll(outs[1], HEAD_DIM, 1))
        o_ref[chunk] = o
        (low_far_ref if chunk else low_ref)[...] = o.astype(bf16).reshape(8, 64, LANES)


def attend_forward(place, q, q_far, kv_parts):
    smem = pl.BlockSpec(memory_space=pltpu.SMEM)
    vmem = pl.BlockSpec(memory_space=pltpu.VMEM)
    return call(
        forward_kernel,
        (
            struct((2, CHUNK, LANES), f32),
            struct((8, 64, LANES), bf16),
            struct((8, 64, LANES), bf16),
            struct((4, 8, CHUNK), f32),
            struct((4 * BLOCK, LANES), bf16),
        ),
        2e10,
        4e6,
        in_specs=[smem] + [vmem] * 7,
        out_specs=(vmem,) * 5,
        scratch_shapes=[
            pltpu.VMEM((2, CHUNK, LANES), bf16),
            pltpu.VMEM((2, CHUNK, LANES), f32),
            pltpu.VMEM((2, CHUNK, LANES), f32),
        ],
        name="attend",
    )(place, q, q_far, *kv_parts)


def backward_kernel(
    place_ref, q_ref, q_far_ref, do_ref, do_far_ref, o_ref, lse_ref, kv_ref,
    dq_ref, dq_far_ref, d0_ref, d1a_ref, d1b_ref, d2a_ref, d2b_ref, d3a_ref, d3b_ref,
    qm_ref, dom_ref, row_ref, dqt_ref, acc_ref,
):
    tile = 512
    context = place_ref[0]
    half = place_ref[1]
    left = lane_index((CHUNK, LANES)) < HEAD_DIM
    acc_ref[...] = jnp.zeros_like(acc_ref)
    for chunk in range(2):
        whole = 2 * (2 * (context if chunk == 0 else 3 - context) + chunk)
        queries = (q_far_ref[...] if chunk else q_ref[:8]).reshape(CHUNK, LANES)
        do = (do_far_ref[...] if chunk else do_ref[:8]).reshape(CHUNK, LANES).astype(f32)
        product = jnp.transpose(do * o_ref[chunk])
        for head in range(2):
            qm_ref[head] = query_of_head(queries, head, left)
            moved = do if head else pltpu.roll(do, HEAD_DIM, 1)
            dom_ref[head] = jnp.where(left, 0.0, moved).astype(bf16)
            dqt_ref[head] = jnp.zeros((LANES, CHUNK), f32)
            rows = product[head * HEAD_DIM : (head + 1) * HEAD_DIM]
            row_ref[head] = jnp.broadcast_to(jnp.sum(rows, axis=0, keepdims=True), (8, CHUNK))

        def step(index, offset):
            span = pl.ds(pl.multiple_of(index * tile, tile), tile)
            keys = kv_ref[span, :]
            for head in range(2):
                qm = qm_ref[head]
                dom = dom_ref[head]
                s = dot_rows(keys, qm)
                dp = dot_rows(keys, dom)
                p = jnp.exp(s - lse_ref[2 * chunk + head, 0:1])
                if offset is not None:
                    r = lane_index(s.shape)
                    place = r + (r // 64) * 64 + half * 64
                    key = lax.broadcasted_iota(jnp.int32, s.shape, 0) + offset
                    p = jnp.where(key <= place, p, 0.0)
                ds = (p * (dp - row_ref[head, 0:1])).astype(bf16)
                acc_ref[span, :] += dot(ds, qm) + dot(p.astype(bf16), dom)
                dqt_ref[head] += dot_down(keys, ds)

        def visit(index, carry):
            step(index, None)
            return carry

        lax.fori_loop(0, whole, visit, 0)
        step(whole, 0)
        step(whole + 1, tile)
        parts = [jnp.transpose(dqt_ref[head]) * score_scale for head in range(2)]
        dq = jnp.where(left, parts[0], pltpu.roll(parts[1], HEAD_DIM, 1)).astype(bf16)
        (dq_far_ref if chunk else dq_ref)[...] = dq.reshape(8, 64, LANES)
    d0_ref[...] = acc_ref[pl.ds(pl.multiple_of(context * BLOCK, BLOCK), BLOCK), :]
    for back, first, second in ((1, d1a_ref, d1b_ref), (2, d2a_ref, d2b_ref), (3, d3a_ref, d3b_ref)):
        start = pl.multiple_of(lax.rem(context + 4 - back, 4) * BLOCK, BLOCK)
        first[...] = acc_ref[pl.ds(start, BLOCK // 2), :].astype(bf16)
        second[...] = acc_ref[pl.ds(pl.multiple_of(start + BLOCK // 2, BLOCK // 2), BLOCK // 2), :].astype(bf16)


def attend_backward(place, q, q_far, do, do_far, o, lse, kv):
    smem = pl.BlockSpec(memory_space=pltpu.SMEM)
    vmem = pl.BlockSpec(memory_space=pltpu.VMEM)
    rows = kv.shape[0]
    return call(
        backward_kernel,
        (struct((8, 64, LANES), bf16), struct((8, 64, LANES), bf16), struct((BLOCK, LANES), f32))
        + (struct((BLOCK // 2, LANES), bf16),) * 6,
        5e10,
        8e6,
        in_specs=[smem] + [vmem] * 7,
        out_specs=(vmem,) * 9,
        scratch_shapes=[
            pltpu.VMEM((2, CHUNK, LANES), bf16),
            pltpu.VMEM((2, CHUNK, LANES), bf16),
            pltpu.VMEM((2, 8, CHUNK), f32),
            pltpu.VMEM((2, LANES, CHUNK), f32),
            pltpu.VMEM((rows, LANES), f32),
        ],
        name="attend_back",
    )(place, q, q_far, do, do_far, o, lse, kv)


def middle_kernel(att_ref, x_ref, wo_ref, gain_ref, pick_ref, hidden_ref, send_ref, attended_ref):
    for j in range(PAIRS):
        for h in range(2):
            attended_ref[h * 64 : h * 64 + 64, j * LANES : (j + 1) * LANES] = att_ref[2 * j + h]
    hidden = x_ref[...].astype(f32) + branch_scale * dot(attended_ref[...], wo_ref[...])
    hidden_ref[...] = hidden
    inverse = lax.rsqrt(jnp.mean(hidden * hidden, axis=-1, keepdims=True) + norm_eps)
    act = (hidden * inverse * gain_ref[...]).astype(bf16)
    send_ref[...] = dot(pick_ref[...], act).astype(bf16)


def middle(att, x, wo, gain, pick):
    return call(
        middle_kernel,
        (struct((TOK, D), f32), struct((SLOTS, D), bf16)),
        2 * TOK * D * (D + SLOTS),
        8e6,
        scratch_shapes=[pltpu.VMEM((TOK, D), bf16)],
        name="middle",
    )(att, x, wo, gain.reshape(1, D), pick)


def raw_kernel(first_ref, top_ref, down_ref, rows_ref, raw_ref):
    number = first_ref[0] + pl.program_id(0)
    chosen = (lane_index((8, LANES)) == number).astype(bf16)
    slot = lax.broadcasted_iota(jnp.int32, (CAP, TOK), 0).astype(f32)
    for n in range(16):
        place = dot_rows(chosen, top_ref[n, :, D:])[0:1]
        rows = dot((slot == place).astype(bf16), top_ref[n, :, :D])
        rows_ref[CAP * n : CAP * n + CAP] = rows.astype(bf16)
    raw_ref[...] = branch_scale * dot_rows(rows_ref[...], down_ref[...])


def raw_grads(first, top, down):
    return call(
        raw_kernel,
        (struct((2, 768, D), bf16), struct((2, 768, F), f32)),
        2 * SLOTS * D * F,
        1.2e7,
        grid=(2,),
        in_specs=[
            pl.BlockSpec(memory_space=pltpu.SMEM),
            pl.BlockSpec((16, TOK, D + LANES), lambda n: (0, 0, 0)),
            owned(F, D),
        ],
        out_specs=(owned(768, D), owned(768, F)),
        name="raw",
    )(first, top, down)


def expert_kernel(
    first_ref, x_ref, raw_ref, gu_ref, wr_ref, back_ref, hidden_ref, mixed_ref, gate_ref, logit_ref, norm_ref
):
    number = first_ref[0] + pl.program_id(0)
    wr = wr_ref[...]
    for part in range(2):
        take = slice(8 * part, 8 * part + 8)
        rows = slice(384 * part, 384 * part + 384)
        x = x_ref[take].reshape(384, D)
        logits = dot(x, wr)
        raised = jnp.exp(logits - jnp.max(logits, axis=-1, keepdims=True))
        probs = raised / jnp.sum(raised, axis=-1, keepdims=True)
        chosen = (lane_index(probs.shape) == number).astype(f32)
        gate_value = jnp.sum(probs * chosen, axis=-1, keepdims=True)
        gate_ref[rows] = gate_value
        pre = dot(x, gu_ref[...])
        raw = raw_ref[rows]
        gate = pre[:, :F]
        up = pre[:, F:]
        sig = 1.0 / (1.0 + jnp.exp(-gate))
        act = gate * sig
        hidden = (act * up).astype(bf16)
        hidden_ref[rows] = hidden
        grad_gate = jnp.sum(hidden.astype(f32) * raw, axis=-1, keepdims=True)
        grad_logits = (gate_value * grad_gate) * (chosen - probs)
        logit_ref[rows] = grad_logits
        raw = raw * gate_value
        mixed_gate = (raw * up * sig * (1.0 + gate * (1.0 - sig))).astype(bf16)
        mixed_up = (raw * act).astype(bf16)
        mixed_ref[rows, :F] = mixed_gate
        mixed_ref[rows, F:] = mixed_up
        hi, lo = split2(grad_logits)
        back = dot_rows(mixed_gate, gu_ref[:, :F]) + dot_rows(mixed_up, gu_ref[:, F:])
        back = back + dot_rows(hi, wr) + dot_rows(lo, wr)
        back_ref[take] = back.astype(bf16).reshape(8, CAP, D)
        product = jnp.sum(back * x.astype(f32), axis=0, keepdims=True)
        if part == 0:
            norm_ref[...] = jnp.broadcast_to(product, (8, D))
        else:
            norm_ref[...] += product


def owned(*shape):
    return pl.BlockSpec((None, *shape), lambda n: (n, *([0] * len(shape))))


def experts(first, x, raw, gate_up, wr):
    per = pl.BlockSpec((16, None, CAP, D), lambda n: (0, n, 0, 0))
    return call(
        expert_kernel,
        (
            struct((16, 2, CAP, D), bf16),
            struct((2, 768, F), bf16),
            struct((2, 768, D), bf16),
            struct((2, 768, 1), f32),
            struct((2, 768, EXPERTS), f32),
            struct((2, 8, D), f32),
        ),
        2 * SLOTS * D * 2560,
        2e7,
        grid=(2,),
        in_specs=[
            pl.BlockSpec(memory_space=pltpu.SMEM),
            per,
            owned(768, F),
            owned(D, D),
            pl.BlockSpec((D, EXPERTS), lambda n: (0, 0)),
        ],
        out_specs=(per, owned(768, F), owned(768, D), owned(768, 1), owned(768, EXPERTS), owned(8, D)),
        name="experts",
    )(first, x, raw, gate_up, wr)


def expert_grads_kernel(
    x_ref, top_ref, gate_ref, logit_ref, hidden_ref, mixed_ref, down_ref, norm_ref, gain_ref,
    out_ref, dgu_ref, ddown_ref, router_ref,
):
    n = pl.program_id(0)
    hidden = hidden_ref[...]
    gate = gate_ref[...]
    x = x_ref[...].reshape(768, D)
    out = (gate * dot(hidden, down_ref[...])).astype(bf16).reshape(16, CAP, D)
    out_ref[:, pl.ds(pl.multiple_of(n * CAP, 16), CAP), :] = out
    top = (branch_scale * gate * top_ref[...].astype(f32)).astype(bf16)
    ddown_ref[...] = dot_down(hidden, top).astype(bf16)
    dgu_ref[...] = dot_down(x, mixed_ref[...]).astype(bf16)
    hi, lo = split2(logit_ref[...])
    router = dot_down(hi, x) + dot_down(lo, x)

    @pl.when(n == 0)
    def _():
        router_ref[...] = router

    @pl.when(n == 1)
    def _():
        total = router_ref[...] + router
        norm = (norm_ref[0, 0:1] + norm_ref[1, 0:1]) / gain_ref[...]
        for e in range(16):
            if e < 8:
                extra = jnp.concatenate([total[4 * e : 4 * e + 4], jnp.zeros((12, D), f32)], axis=0)
            elif e == 8:
                extra = jnp.concatenate([norm, jnp.zeros((15, D), f32)], axis=0)
            else:
                extra = jnp.zeros((16, D), f32)
            out_ref[e, 96:112] = extra.astype(bf16)


def expert_grads(x, top, gate, logits, hidden, mixed, down, norm, gain):
    per = pl.BlockSpec((16, None, CAP, D), lambda n: (0, n, 0, 0))
    return call(
        expert_grads_kernel,
        (struct((16, 176, D), bf16), struct((2, D, D), bf16), struct((2, F, D), bf16)),
        2 * SLOTS * D * 2048,
        2.4e7,
        grid=(2,),
        in_specs=[
            per,
            owned(768, D),
            owned(768, 1),
            owned(768, EXPERTS),
            owned(768, F),
            owned(768, D),
            owned(F, D),
            pl.BlockSpec((2, 8, D), lambda n: (0, 0, 0)),
            pl.BlockSpec((1, D), lambda n: (0, 0)),
        ],
        out_specs=(pl.BlockSpec((16, 176, D), lambda n: (0, 0, 0)), owned(D, D), owned(F, D)),
        scratch_shapes=[pltpu.VMEM((EXPERTS, D), f32)],
        name="expert_grads",
    )(x, top, gate, logits, hidden, mixed, down, norm, gain.reshape(1, D))


def turn_back_kernel(
    back_ref, spot_ref, hidden_ref, gain_ref, top_ref, wo_ref, before_ref,
    state_ref, buffer_ref, send_ref, attn_ref, done_ref,
):
    grad = dot(spot_ref[...], back_ref[...])
    hidden = hidden_ref[...]
    inverse = lax.rsqrt(jnp.mean(hidden * hidden, axis=-1, keepdims=True) + norm_eps)
    normed = hidden * inverse
    scaled = grad * gain_ref[...]
    state = top_ref[...].astype(f32) + inverse * (scaled - normed * jnp.mean(scaled * normed, axis=-1, keepdims=True))
    state_ref[...] = state
    attn = (branch_scale * state).astype(bf16)
    for e in range(16):
        attn_ref[e] = attn[64 * (e % 2) : 64 * (e % 2) + 64]
    copy = pltpu.make_async_copy(attn_ref, buffer_ref.at[:, pl.ds(112, 64), :], done_ref)
    copy.start()
    attended = dot_rows(attn, wo_ref[...]).astype(bf16)
    for j in range(PAIRS):
        for h in range(2):
            send_ref[2 * j + h] = attended[h * 64 : h * 64 + 64, j * LANES : (j + 1) * LANES]
    copy.wait()


def turn_back(back, spot, hidden, gain, top, wo, buffer):
    vmem = pl.BlockSpec(memory_space=pltpu.VMEM)
    outside = pl.BlockSpec(memory_space=pl.ANY)
    return call(
        turn_back_kernel,
        (
            struct((TOK, D), f32),
            struct((16, 176, D), bf16),
            struct((16, TOK // 2, LANES), bf16),
        ),
        2 * 256 * D * (D + SLOTS),
        8e6,
        in_specs=[vmem] * 6 + [outside],
        out_specs=(vmem, outside, vmem),
        scratch_shapes=[pltpu.VMEM((16, 64, D), bf16), pltpu.SemaphoreType.DMA],
        input_output_aliases={6: 1},
        name="turn_back",
    )(back, spot, hidden, gain.reshape(1, D), top, wo, buffer)


def unturn(v, cos, sin, first):
    scaled = v * sin
    return v * cos + jnp.where(first, pltpu.roll(scaled, LANES - 32, 1), pltpu.roll(scaled, 32, 1))


def merge_kernel(
    place_ref, d0_ref, left_a_ref, left_b_ref, right_a_ref, right_b_ref, keep_ref, give_ref, sum_ref
):
    half = place_ref[1]
    for part, left, right in ((0, left_a_ref, right_a_ref), (1, left_b_ref, right_b_ref)):
        rows = slice(part * 1024, part * 1024 + 1024)
        total = d0_ref[rows] + left[...].astype(f32) + right[...].astype(f32)
        sum_ref[8 * part : 8 * part + 8] = total.reshape(8, TOK, LANES)
    keep_ref[...] = sum_ref[:, pl.ds(pl.multiple_of(half * 64, 64), 64), :]
    give_ref[...] = sum_ref[:, pl.ds(pl.multiple_of((1 - half) * 64, 64), 64), :].astype(bf16)


def merge(place, *pieces):
    smem = pl.BlockSpec(memory_space=pltpu.SMEM)
    vmem = pl.BlockSpec(memory_space=pltpu.VMEM)
    return call(
        merge_kernel,
        (struct((16, 64, LANES), f32), struct((16, 64, LANES), bf16)),
        1e6,
        3e6,
        in_specs=[smem] + [vmem] * 5,
        out_specs=(vmem, vmem),
        scratch_shapes=[pltpu.VMEM((16, TOK, LANES), f32)],
        name="merge",
    )(place, *pieces)


def unturn_kernel(dq_ref, dq_far_ref, keep_ref, got_ref, cos_ref, sin_ref, grads_ref):
    lane = lane_index((512, LANES))
    first = lane % HEAD_DIM < HEAD_DIM // 2
    for part, dq in ((0, dq_ref), (1, dq_far_ref)):
        rows = slice(512 * part, 512 * part + 512)
        take = slice(8 * part, 8 * part + 8)
        cos = cos_ref[rows]
        sin = sin_ref[rows]
        grads_ref[rows, :LANES] = unturn(dq[...].reshape(512, LANES).astype(f32), cos, sin, first).astype(bf16)
        both = (keep_ref[take] + got_ref[take].astype(f32)).reshape(512, LANES).astype(bf16).astype(f32)
        grads_ref[rows, LANES:] = jnp.where(lane < HEAD_DIM, unturn(both, cos, sin, first), both).astype(bf16)


def unturn_rows(dq, dq_far, keep, got, cos, sin):
    return call(unturn_kernel, struct((1024, 256), bf16), 1e6, 3e6, name="unturn")(dq, dq_far, keep, got, cos, sin)


def head_kernel(
    place_ref, act_ref, o_ref, grads_ref, extra_ref, a0_ref, a1_ref, a2_ref, a3_ref, mine_ref, other_ref, all_ref, attn_ref
):
    grads = dot_down(act_ref[...], grads_ref[...]).astype(bf16)
    for part, ref in enumerate((a0_ref, a1_ref, a2_ref, a3_ref)):
        attn_ref[:, 16 * part : 16 * part + 16, :] = ref[...]
    out = dot_down(o_ref[...], attn_ref[...].reshape(1024, D)).astype(bf16)
    for quarter in range(4):
        start = 384 * quarter
        all_ref[start : start + 256] = grads[256 * quarter : 256 * quarter + 256]
        all_ref[start + 256 : start + 384] = out[:, 256 * quarter : 256 * quarter + 256]
    extra = extra_ref[0].astype(f32)
    for e in range(1, 16):
        extra = extra + extra_ref[e].astype(f32)
    packed = extra[:, :256]
    for b in range(1, 4):
        packed = packed + pltpu.roll(extra[:, 256 * b : 256 * (b + 1)], 4 * b, 0)
    packed = packed.astype(bf16)
    core = place_ref[2]
    for which, out_ref in ((1 - core, other_ref), (core, mine_ref)):
        out_ref[:768] = all_ref[pl.ds(pl.multiple_of(which * 768, 768), 768), :]
        out_ref[768:] = packed


def head_grads(place, act, o, grads, returned):
    whole = lambda *shape: pl.BlockSpec(shape, lambda i, place: (0,) * len(shape))
    half = struct((784, 256), bf16)
    return call(
        head_kernel,
        (half, half),
        2 * 1024 * 1024 * 512,
        8e6,
        grid_spec=pltpu.PrefetchScalarGridSpec(
            num_scalar_prefetch=1,
            grid=(1,),
            in_specs=[
                whole(1024, D),
                whole(1024, LANES),
                whole(1024, 256),
                pl.BlockSpec((16, 16, D), lambda i, place: (0, 6, 0)),
                pl.BlockSpec((16, 16, D), lambda i, place: (0, 7, 0)),
                pl.BlockSpec((16, 16, D), lambda i, place: (0, 8, 0)),
                pl.BlockSpec((16, 16, D), lambda i, place: (0, 9, 0)),
                pl.BlockSpec((16, 16, D), lambda i, place: (0, 10, 0)),
            ],
            out_specs=(whole(784, 256), whole(784, 256)),
            scratch_shapes=[pltpu.VMEM((1536, 256), bf16), pltpu.VMEM((16, 64, D), bf16)],
        ),
        name="head_grads",
    )(place, act, o, grads, *([returned] * 5))


def split_kernel(place_ref, mine_ref, other_ref, keep_ref, give_ref):
    half = place_ref[1]
    rows = pl.ds(pl.multiple_of(half * 384, 384), 384)
    keep_ref[:384] = mine_ref[rows, :].astype(f32) + other_ref[rows, :].astype(f32)
    keep_ref[384:] = mine_ref[768:, :].astype(f32) + other_ref[768:, :].astype(f32)
    rows = pl.ds(pl.multiple_of((1 - half) * 384, 384), 384)
    give_ref[...] = (mine_ref[rows, :].astype(f32) + other_ref[rows, :].astype(f32)).astype(bf16)


def split_halves(place, mine, other):
    smem = pl.BlockSpec(memory_space=pltpu.SMEM)
    vmem = pl.BlockSpec(memory_space=pltpu.VMEM)
    return call(
        split_kernel,
        (struct((400, 256), f32), struct((384, 256), bf16)),
        1e6,
        2e6,
        in_specs=[smem, vmem, vmem],
        out_specs=(vmem, vmem),
        name="split",
    )(place, mine, other)


def finish_kernel(grads_ref, x_ref, gain_ref, wq_ref, wk_ref, wv_ref, state_ref, out_ref, flat_ref):
    left = lane_index((TOK // 2, LANES)) < HEAD_DIM
    for h in range(2):
        rows = slice(64 * h, 64 * h + 64)
        for j in range(PAIRS):
            flat_ref[rows, j * LANES : (j + 1) * LANES] = grads_ref[2 * j + h, :, :LANES]
        for b in range(PAIRS // 2):
            even = grads_ref[4 * b + h, :, LANES:].astype(f32)
            odd = grads_ref[4 * b + 2 + h, :, LANES:].astype(f32)
            k = jnp.where(left, even, pltpu.roll(odd, HEAD_DIM, 1))
            v = jnp.where(left, pltpu.roll(even, HEAD_DIM, 1), odd)
            flat_ref[rows, D + b * LANES : D + (b + 1) * LANES] = k.astype(bf16)
            flat_ref[rows, D + 512 + b * LANES : D + 512 + (b + 1) * LANES] = v.astype(bf16)
    grad = dot_rows(flat_ref[:, :D], wq_ref[...])
    grad = grad + dot_rows(flat_ref[:, D : D + 512], wk_ref[...])
    grad = grad + dot_rows(flat_ref[:, D + 512 :], wv_ref[...])
    x = x_ref[...].astype(f32)
    inverse = lax.rsqrt(jnp.mean(x * x, axis=-1, keepdims=True) + norm_eps)
    normed = x * inverse
    scaled = grad * gain_ref[...]
    out_ref[...] = state_ref[...] + inverse * (scaled - normed * jnp.mean(scaled * normed, axis=-1, keepdims=True))


def finish(grads, x, gain, wq, wk, wv, state):
    return call(
        finish_kernel,
        struct((TOK, D), f32),
        2 * 256 * D * 2048,
        8e6,
        scratch_shapes=[pltpu.VMEM((TOK, 2048), bf16)],
        name="finish",
    )(grads, x, gain.reshape(1, D), wq, wk, wv, state)


def assemble_kernel(place_ref, piece, wq_ref, wk_ref, wv_ref, gain_ref, *refs):
    q_ref, k_ref, v_ref, o_ref, norm_ref = refs[-5:]
    left = lane_index((256, LANES)) < HEAD_DIM
    total = jnp.zeros((256, LANES), f32)
    for j in range(PAIRS):
        lanes = slice(j * LANES, (j + 1) * LANES)
        value = piece[j, :256, :LANES].astype(f32)
        q_ref[:, lanes] = value
        total = total + value * wq_ref[:, lanes].astype(f32)
        o_ref[lanes, :] = piece[j, 256:384, :].astype(f32)
    for b in range(PAIRS // 2):
        lanes = slice(b * LANES, (b + 1) * LANES)
        even = piece[2 * b, :256, LANES:].astype(f32)
        odd = piece[2 * b + 1, :256, LANES:].astype(f32)
        k = jnp.where(left, even, pltpu.roll(odd, HEAD_DIM, 1))
        v = jnp.where(left, pltpu.roll(even, HEAD_DIM, 1), odd)
        k_ref[:, lanes] = k
        v_ref[:, lanes] = v
        total = total + k * wk_ref[:, lanes].astype(f32) + v * wv_ref[:, lanes].astype(f32)
    norm_ref[...] = jnp.sum(jnp.transpose(total), axis=0, keepdims=True) / gain_ref[...]


def assemble(place, core, pieces, wq, wk, wv, gain, before=()):
    def quarter(i, place):
        return 2 * (place[2] if core == 0 else 1 - place[2]) + i

    rows = lambda width: pl.BlockSpec((256, width), lambda i, place: (quarter(i, place), 0))
    columns = lambda height: pl.BlockSpec((height, 256), lambda i, place: (0, quarter(i, place)))
    return call(
        assemble_kernel,
        (
            struct((D, D), f32),
            struct((D, 512), f32),
            struct((D, 512), f32),
            struct((D, D), f32),
            struct((1, D), f32),
        ),
        1e6,
        1.1e7,
        grid_spec=pltpu.PrefetchScalarGridSpec(
            num_scalar_prefetch=1,
            grid=(2,),
            in_specs=[
                pl.BlockSpec((PAIRS, None, 400, 256), lambda i, place: (0, i, 0, 0)),
                rows(D),
                rows(512),
                rows(512),
                columns(1),
            ]
            + [pl.BlockSpec(memory_space=pl.ANY)] * len(before),
            out_specs=(rows(D), rows(512), rows(512), columns(D), columns(1)),
        ),
        input_output_aliases={6 + i: i for i in range(len(before))},
        name="assemble",
    )(place, pieces.reshape(PAIRS, 2, 400, 256), wq, wk, wv, gain.reshape(1, D), *before)


def spread_kernel(a_ref, b_ref, out_ref):
    total = (a_ref[...].astype(f32) + b_ref[...].astype(f32)).astype(bf16)
    for e in range(16):
        out_ref[e] = total


def add_and_spread(a, b):
    return call(spread_kernel, struct((16, 400, 256), bf16), 1e6, 4e6, name="spread")(a, b)


def after(x, *earlier):
    return lax.optimization_barrier((x, *earlier))[0]


def to_owners(x):
    return lax.all_to_all(x, "expert", split_axis=0, concat_axis=0, tiled=True)


def mirror(x):
    return lax.ppermute(x, "context", [(0, 3), (1, 2), (2, 1), (3, 0)])


def swap_cores(x):
    return lax.ppermute(x, "dp", [(0, 1), (1, 0)])


def shift(x, by):
    return lax.ppermute(x, "context", [(i, (i + by) % 4) for i in range(4)])


def neighbour(x):
    return lax.ppermute(x, "context", [(0, 1), (1, 0), (2, 3), (3, 2)])


def swap_halves(x):
    return lax.ppermute(x, "expert", [(i, i ^ 1) for i in range(16)])


def pick(x, index, axis=0):
    return lax.dynamic_index_in_dim(x, index, axis, False)


def rope_tables(positions):
    frequency = rope_base ** (-jnp.arange(0, HEAD_DIM, 2, dtype=f32) / HEAD_DIM)
    angles = positions.astype(f32)[:, None] * frequency[None, :]
    cos, sin = jnp.cos(angles), jnp.sin(angles)
    return jnp.concatenate([cos] * 4, -1), jnp.concatenate([-sin, sin] * 2, -1)


def local(
    layer_input, grad_output, norm1_gain, norm2_gain, w_query, w_key, w_value, w_out, w_router, w_gate_up, w_down, routes
):
    context = lax.axis_index("context")
    expert = lax.axis_index("expert")
    x = layer_input[0, 0]
    top = grad_output[0, 0]

    half = expert % 2

    cos, sin = rope_tables(context * BLOCK + expert * TOK + jnp.arange(TOK, dtype=jnp.int32))
    order = jnp.arange(1024, dtype=jnp.int32)
    half_cos, half_sin = rope_tables(context * BLOCK + order + (order // 64) * 64 + half * 64)

    act_send, q_send, kv_send = project(x, norm1_gain, w_query, w_key, w_value, cos, sin)
    kv_own = to_owners(kv_send).reshape(BLOCK, LANES)
    kv_left, kv_right = shift(kv_own, 1), shift(kv_own, 3)
    named = after(routes[0, 0], kv_own)

    hits = jnp.sum((named[:, :, None] == jnp.arange(EXPERTS, dtype=jnp.int32)).astype(f32), 1)
    lower = np.tril(np.ones((TOK, TOK), np.float32), -1)
    place = dot(jnp.asarray(lower, bf16), hits.astype(bf16))
    owner = np.repeat(np.eye(EXPERTS, dtype=np.float32), CAP, 0)
    owner16 = jnp.asarray(owner, bf16)
    slot_number = jnp.arange(SLOTS, dtype=jnp.int32) % CAP
    marked = jnp.where(hits > 0.5, place, 255.0).astype(bf16)
    spot = (dot_rows(marked, owner16) == slot_number[None, :].astype(f32)).astype(bf16)
    selector = (dot_rows(owner16, marked) == slot_number[:, None].astype(f32)).astype(bf16)

    q_own = to_owners(after(q_send, kv_own))
    q_far = mirror(q_own[8:])
    far_a, far_b = shift(kv_left[: BLOCK // 2], 1), shift(kv_right[BLOCK // 2 :], 3)

    down = lax.all_gather(w_down, ("context", "dp"), axis=1, tiled=True)
    wide = jnp.concatenate([top, jnp.pad(marked, ((0, 0), (0, LANES - EXPERTS)))], 1)
    top_all = lax.all_gather(wide, "expert", axis=0, tiled=True)
    gate_up = lax.all_gather(w_gate_up, ("context", "dp"), axis=1, tiled=True)

    seat = jnp.stack([context, half, lax.axis_index("dp")]).astype(jnp.int32)
    o, o_low, o_far, lse, kv = attend_forward(
        seat, q_own, q_far, (kv_own, kv_left, far_a, far_b, kv_right)
    )
    o_own = jnp.concatenate([o_low, mirror(o_far)], 0)
    att = to_owners(o_own)
    first = (2 * expert).astype(jnp.int32).reshape(1)
    top_rows, raw = raw_grads(first, top_all.reshape(16, TOK, D + LANES), down)

    hidden, send = middle(att, x, w_out, norm2_gain, selector)
    rows = after(to_owners(send.reshape(16, 2, CAP, D)), raw)
    act_rows = to_owners(after(act_send, rows)).reshape(1024, D)
    grad_rows, expert_hidden, mixed, gates, logits, norm2_sum = experts(first, rows, raw, gate_up, w_router)
    back = to_owners(after(grad_rows, act_rows))
    buffer, dgu, ddown = expert_grads(
        rows, top_rows, gates, logits, expert_hidden, mixed, down, norm2_sum, norm2_gain
    )
    state, buffer, do_send = turn_back(back.reshape(SLOTS, D), spot, hidden, norm2_gain, top, w_out, buffer)
    do_own = to_owners(do_send)
    do_far = mirror(do_own[8:])
    returned = to_owners(after(buffer, do_own))
    grad_gate_up = lax.psum_scatter(
        after(dgu, do_own), ("context", "dp"), scatter_dimension=1, tiled=True
    ).astype(f32)

    dq, dq_far, d0, d1a, d1b, d2a, d2b, d3a, d3b = attend_backward(seat, q_own, q_far, do_own, do_far, o, lse, kv)

    far_a, far_b = shift(d2a, 1), shift(d2b, 3)
    from_left_b, from_right_a = shift(d3b, 1), shift(d1a, 3)
    dq_far = mirror(after(dq_far, far_a, far_b))
    from_left_a = shift((d3a.astype(f32) + far_a.astype(f32)).astype(bf16), 1)
    from_right_b = shift((d1b.astype(f32) + far_b.astype(f32)).astype(bf16), 3)
    keep, give = merge(seat, d0, from_left_a, from_left_b, from_right_a, from_right_b)
    got = after(swap_halves(give), returned)
    grads = unturn_rows(dq, dq_far, keep, got, half_cos, half_sin)
    mine, other = head_grads(
        seat,
        act_rows,
        o_own.reshape(1024, LANES),
        grads,
        returned,
    )
    keep, give = split_halves(seat, mine, swap_cores(other))
    total = keep + jnp.pad(swap_halves(give), ((0, 16), (0, 0))).astype(f32)
    total = total.astype(bf16)
    total = (total.astype(f32) + neighbour(total).astype(f32)).astype(bf16)
    grads_back = to_owners(grads.reshape(16, 64, 256))
    block = after(add_and_spread(total, mirror(total)), grads_back)
    whole = to_owners(block)
    grad_input = finish(grads_back, x, norm1_gain, w_query, w_key, w_value, state)

    block_out = hidden + branch_scale * dot(spot, returned[:, :96].reshape(SLOTS, D))
    grad_down = lax.psum_scatter(after(ddown, block), ("context", "dp"), scatter_dimension=1, tiled=True).astype(f32)
    whole, grad_input, block_out, grad_gate_up, grad_down = lax.optimization_barrier(
        (whole, grad_input, block_out, grad_gate_up, grad_down)
    )
    weights = (w_query, w_key, w_value, norm1_gain)
    own_part = assemble(seat, 0, whole, *weights)
    dwq, dwk, dwv, dwo, norm1_grad = assemble(seat, 1, swap_cores(whole), *weights, before=own_part)
    small = after(whole, own_part[4])[:, 384:].reshape(16, 4, 4, 256).transpose(0, 2, 1, 3).reshape(64, D).astype(f32)
    return (
        block_out.reshape(1, 1, TOK, D),
        grad_input.reshape(1, 1, TOK, D),
        norm1_grad[0],
        small[EXPERTS],
        dwq,
        dwk,
        dwv,
        dwo,
        small[:EXPERTS].T,
        grad_gate_up,
        grad_down,
    )


def solution(mesh):
    tokens = P("dp", "context", "expert", None)
    weights = P("expert", ("context", "dp"), None)
    return jax.shard_map(
        local,
        mesh=mesh,
        in_specs=(tokens, tokens, P(), P(), P(), P(), P(), P(), P(), weights, weights, tokens),
        out_specs=(tokens, tokens, P(), P(), P(), P(), P(), P(), P(), weights, weights),
        check_vma=False,
    )
```
